512 devices in a mesh: sec: 4 (over x_lo, core), seq: 128 (over z, y, x_hi).
Axes of the slice: x: 4 (x_hi: 2, x_lo: 2; x = x_hi * 2 + x_lo), y: 8, z: 8, core: 2. Of those that a mesh axis runs over, the one named last changes fastest.
Arguments:
- queries: bfloat16 [4, 4096, 3072], P('sec', 'seq'), may hold values from -21 to 21
- keys: bfloat16 [4, 4096, 3072], P('sec', 'seq'), may hold values from -8 to 8
- values: bfloat16 [4, 4096, 3072], P('sec', 'seq'), may hold values from -6 to 6
- residual: bfloat16 [4, 4096, 3072], P('sec', 'seq'), may hold values from -6 to 6
- shift_mod: float32 [4, 3072], P('sec'), may hold values from -4 to 4
- scale_mod: float32 [4, 3072], P('sec'), may hold values from -4 to 4
- gate_mod: float32 [4, 3072], P('sec'), may hold values from 0.5 to 1.5
- final_weight: bfloat16 [3072, 64], replicated, may hold values from -0.109375 to 0.109375
- final_bias: float32 [64], replicated, may hold values from -4 to 4
- conv_weight: bfloat16 [432, 512], replicated, may hold values from -0.3125 to 0.3125
- conv_bias: float32 [512], replicated, may hold values from -4 to 4
- group_gain: float32 [512], replicated, may hold values from 0.1 to 1.9
- group_bias: float32 [512], replicated, may hold values from -4 to 4
Outputs:
- features: bfloat16 [4, 16, 128, 8, 512], P(None, 'sec', 'seq')
The draws below stay inside these ranges and needn't reach their ends.
All inputs are finite; a program needn't handle non-finite values.
Results may differ from the reference program's by a relative error of at most 0.015.
Values may be sent and summed in bfloat16 or wider, within the bound.
A program may use at most 64 MiB of HBM per device.

```python
import jax
import jax.numpy as jnp
from jax import lax

D = 3072
H = 24
HD = 128
LATC = 16
VAE_CH = 512
F = 16
BR = 2
BC = 4
REQ = 4
GC = 16
GR = 8
L = 4096
KIN = 432
POUT = 64


def spread_keys(key):
    key = jax.random.fold_in(key, 3)
    return jnp.clip(1.7 * jax.random.normal(key, (REQ, L, D), jnp.float32), -8.0, 8.0)


def draw_keys(key, part):
    return spread_keys(key).astype(jnp.bfloat16)


def draw_queries(key, part):
    pair_weight = 3.4 / HD ** 0.5
    partner = jnp.roll(spread_keys(key), -(L // 2), axis=1)
    key = jax.random.fold_in(key, 5)
    own_draw = jnp.clip(1.7 * jax.random.normal(key, (REQ, L, D), jnp.float32), -8.0, 8.0)
    return (0.5 * own_draw + pair_weight * partner).astype(jnp.bfloat16)


def shard_levels(rng, extent, cuts, least, high):
    def one(dim, parts):
        heights = jax.random.uniform(jax.random.fold_in(jax.random.fold_in(rng, 6), dim), (parts,), jnp.float32, least / len(cuts), high / len(cuts))
        return jnp.repeat(jnp.exp(heights), extent[dim] // parts).reshape((-1,) + (1,) * (len(extent) - dim - 1))

    loudness = one(*cuts[0])
    for cut in cuts[1:]:
        loudness = loudness * one(*cut)
    return loudness


def noise(key, shape, scale, most, shards=(), held_as=jnp.bfloat16):
    array = jax.random.normal(key, shape, jnp.float32) * scale
    if len(shards) > 0:
        array = shard_levels(key, shape, shards, -0.22, 0.18) * array
    return jnp.clip(array, min=-most, max=most).astype(held_as)


def setup_inputs(seed: int = 0) -> dict:
    splits = jax.random.split(jax.random.key(seed), 14)
    return {
        "queries": draw_queries(jax.random.fold_in(splits[13], 71), 0),
        "keys": draw_keys(jax.random.fold_in(splits[13], 71), 0),
        "values": noise(splits[2], (REQ, L, D), 1.0, 6.0, ((0, 4), (1, 128))),
        "residual": noise(splits[3], (REQ, L, D), 0.5, 6.0, ((0, 4), (1, 128))),
        "shift_mod": noise(splits[4], (REQ, D), 0.5, 4.0, ((0, 4),), jnp.float32),
        "scale_mod": noise(splits[5], (REQ, D), 0.5, 4.0, ((0, 4),), jnp.float32),
        "gate_mod": jnp.clip(0.5 + 1.0 * jax.random.uniform(splits[6], (REQ, D), jnp.float32) ** shard_levels(splits[6], (REQ, D), ((0, 4),), -0.2, 0.2), 0.5, 1.5),
        "final_weight": noise(splits[7], (D, POUT), D ** -0.5, 0.109375),
        "final_bias": noise(splits[8], (POUT,), 0.5, 4.0, (), jnp.float32),
        "conv_weight": noise(splits[9], (KIN, VAE_CH), KIN ** -0.5, 0.3125),
        "conv_bias": noise(splits[10], (VAE_CH,), 0.5, 4.0, (), jnp.float32),
        "group_gain": jnp.clip(1.0 + 0.18 * jax.random.normal(splits[11], (VAE_CH,), jnp.float32), 0.1, 1.9),
        "group_bias": noise(splits[12], (VAE_CH,), 0.5, 4.0, (), jnp.float32),
    }


scaling = 0.476986
norm_eps = 1e-06

def attend_head(head_parts):
    query_rows, key_rows, value_rows = head_parts
    scores = jnp.dot(query_rows, key_rows.T, preferred_element_type=jnp.float32) * HD ** (-0.5)
    row_peak = lax.optimization_barrier(jnp.max(scores, axis=1, keepdims=True))
    weights = jnp.exp(scores - row_peak)
    row_total = lax.optimization_barrier(jnp.sum(weights, axis=1, keepdims=True))
    mixed_rows = jnp.dot(weights.astype(jnp.bfloat16), value_rows, preferred_element_type=jnp.float32)
    return (mixed_rows / row_total).astype(jnp.bfloat16)

def section_latents(query_all, key_all, value_all, residual_s, shift_s, scale_s, gate_s, final_weight, final_bias):
    split_q = query_all.reshape(L, H, HD).transpose(1, 0, 2)
    split_k = key_all.reshape(L, H, HD).transpose(1, 0, 2)
    split_v = value_all.reshape(L, H, HD).transpose(1, 0, 2)
    heads_out = lax.map(attend_head, (split_q, split_k, split_v))
    attended = heads_out.transpose(1, 0, 2).reshape(L, D)
    hidden = residual_s.astype(jnp.float32) + gate_s * attended.astype(jnp.float32)
    center = hidden - lax.optimization_barrier(jnp.mean(hidden, axis=1, keepdims=True))
    normed = center * lax.rsqrt(lax.optimization_barrier(jnp.mean(center * center, axis=1, keepdims=True)) + norm_eps)
    modulated = (normed * (1.0 + scale_s) + shift_s).astype(jnp.bfloat16)
    patches = ((jnp.dot(modulated, final_weight, preferred_element_type=jnp.float32) + final_bias) / scaling).astype(jnp.bfloat16)
    latent_grid = patches.reshape(GR, GC, F, BR // 2, BC // 2, 2, 2, LATC)
    latent_grid = latent_grid.transpose(2, 0, 3, 5, 1, 4, 6, 7).reshape(F, GR * BR, GC * BC, LATC)
    return latent_grid

def decode_request(latent_grid, conv_weight, conv_bias, group_gain, group_bias):
    rows_all = GR * BR
    cols_all = GC * BC
    padded = jnp.concatenate([latent_grid[:1], latent_grid[:1], latent_grid], axis=0)
    padded = jnp.pad(padded, ((0, 0), (1, 1), (1, 1), (0, 0)))
    columns = jnp.concatenate([padded[t_step:t_step + F, y_step:y_step + rows_all, x_step:x_step + cols_all] for t_step in range(3) for y_step in range(3) for x_step in range(3)], axis=-1)
    conv_out = jnp.dot(columns.reshape(-1, KIN), conv_weight, preferred_element_type=jnp.float32) + conv_bias
    normed = conv_out.reshape(F, GR, BR, GC, BC, VAE_CH) * group_gain + group_bias
    activated = jax.nn.silu(normed).astype(jnp.bfloat16)
    return activated.transpose(0, 1, 3, 2, 4, 5).reshape(F, GR * GC, BR * BC, VAE_CH)

def reference(queries, keys, values, residual, shift_mod, scale_mod, gate_mod, final_weight, final_bias, conv_weight, conv_bias, group_gain, group_bias):

    def per_section(section_args):
        return section_latents(*section_args, final_weight, final_bias)
    latents = lax.map(per_section, (queries, keys, values, residual, shift_mod, scale_mod, gate_mod))
    return lax.map(lambda latent_grid: decode_request(latent_grid, conv_weight, conv_bias, group_gain, group_bias), latents)
```

```python
import functools

import jax
import jax.numpy as jnp
from jax import lax
from jax.experimental import pallas as pl
from jax.experimental.pallas import tpu as pltpu
from jax.sharding import PartitionSpec as P

H = 24
HD = 128
LATC = 16
F = 16
BR = 2
BC = 4
NZ = 8
NY = 8
TOK = 32
HG = 3
GW = HG * HD
NBLK = NZ * TOK

scaling = 0.476986
norm_eps = 1e-06
EXP2_SCALE = HD ** (-0.5) * 1.4426950408889634
F32 = jnp.float32
BF16 = jnp.bfloat16


def remote(src, dst, send_sem, recv_sem, sec, seq):
    return pltpu.make_async_remote_copy(
        src_ref=src,
        dst_ref=dst,
        send_sem=send_sem,
        recv_sem=recv_sem,
        device_id={"sec": sec, "seq": seq},
        device_id_type=pl.DeviceIdType.MESH,
    )


def signal(sem, sec, seq):
    pl.semaphore_signal(
        sem, inc=1, device_id={"sec": sec, "seq": seq}, device_id_type=pl.DeviceIdType.MESH
    )


def position():
    s = lax.axis_index("sec")
    g = lax.axis_index("seq")
    return s, g, s % 2, s // 2, g // (2 * NY), (g // 2) % NY, g % 2

NEAREST = (0, 1, 7, 2, 6, 3, 5, 4)
HALVES = 2
HALF = NBLK // HALVES
AROUND = [(dy, dx) for dy in (-1, 0, 1) for dx in (-1, 0, 1)]


def whole_kernel(
    q_ref,
    k_ref,
    v_ref,
    res_hbm,
    shift_hbm,
    scale_hbm,
    gate_hbm,
    fw_hbm,
    fb_hbm,
    cw_hbm,
    cb_hbm,
    gg_hbm,
    gb_hbm,
    out_ref,
    qb,
    kb,
    vb,
    ob,
    att,
    peak,
    total,
    acc,
    pat,
    tiles,
    near_tiles,
    windows,
    res_ref,
    shift_ref,
    scale_ref,
    gate_ref,
    fw_ref,
    fb_ref,
    cw_ref,
    cb_ref,
    gg_ref,
    gb_ref,
    load_sem,
    cw_sem,
    s1_send,
    s1_recv,
    ring_send,
    ring_recv,
    sib_send,
    sib_recv,
    o_send,
    o_recv,
    halo_send,
    halo_recv,
):
    s, g, core, xl, z, y, xh = position()
    stays = core == xh
    moves = jnp.logical_not(stays)
    swap_sec = xl * 2 + xh

    def swap_seq(zp):
        return (zp * NY + y) * 2 + core

    right = (z * NY + (y + 1) % NY) * 2 + xh
    left = (z * NY + (y + NY - 1) % NY) * 2 + xh
    sibling = xl * 2 + 1 - core
    col = y * 2 + xh
    last_col = 2 * NY - 1

    def there(dy, dx):
        row_ok = z + dy >= 0 if dy < 0 else z + dy < NZ
        col_ok = col + dx >= 0 if dx < 0 else col + dx <= last_col
        return jnp.logical_and(row_ok, col_ok)

    def for_sections(dy, dx, one):
        def body(ds, carry):
            one((s + ds) % 4)
            return carry

        if dy == 0 and dx == 0:
            lax.fori_loop(1, 4, body, 0)
        else:

            @pl.when(there(dy, dx))
            def _():
                lax.fori_loop(0, 4, body, 0)

    barrier = pltpu.get_barrier_semaphore()
    for e in NEAREST[1:]:
        signal(barrier, swap_sec, swap_seq((z + e) % NZ))

    @pl.when(moves)
    def _():
        signal(barrier, swap_sec, swap_seq(z))

    signal(barrier, s, right)
    signal(barrier, s, left)
    signal(barrier, sibling, g)
    for dy, dx in AROUND:
        for_sections(dy, dx, lambda sp: signal(barrier, sp, g + dy * 2 * NY + dx))

    loads = [
        pltpu.make_async_copy(src, dst, load_sem.at[i])
        for i, (src, dst) in enumerate(
            (
                (res_hbm, res_ref),
                (shift_hbm, shift_ref),
                (scale_hbm, scale_ref),
                (gate_hbm, gate_ref),
                (fw_hbm, fw_ref),
                (fb_hbm, fb_ref),
                (cb_hbm, cb_ref),
                (gg_hbm, gg_ref),
                (gb_hbm, gb_ref),
            )
        )
    ] + [
        pltpu.make_async_copy(
            cw_hbm.at[pl.ds(tap * 48, 48), :], cw_ref.at[tap, pl.ds(0, 48), :], cw_sem.at[tap]
        )
        for tap in range(9)
    ]
    for load in loads:
        load.start()

    n_rows = 3 - jnp.where(z == 0, 1, 0) - jnp.where(z == NZ - 1, 1, 0)
    n_cols = 3 - jnp.where(col == 0, 1, 0) - jnp.where(col == last_col, 1, 0)
    pl.semaphore_wait(barrier, NZ + 1 + jnp.where(stays, 0, 1) + 4 * n_rows * n_cols)

    def group_cols(zp):
        return pl.ds(pl.multiple_of(zp * GW, HD), GW)

    def block_rows(place):
        return pl.ds(place * TOK, TOK)

    stage_one = ((k_ref, kb.at[0]), (v_ref, vb.at[0]), (q_ref, qb))

    def stage_copy(t, e):
        src, buf = stage_one[t]
        zp = (z + e) % NZ
        place = NEAREST.index((NZ - e) % NZ)
        return remote(
            src.at[:, group_cols(zp)],
            buf.at[block_rows(place), :],
            s1_send.at[t, place],
            s1_recv.at[t, place],
            swap_sec,
            swap_seq(zp),
        )

    for t in range(3):

        @pl.when(stays)
        def _(t=t):
            src, buf = stage_one[t]
            pltpu.make_async_copy(
                src.at[:, group_cols(z)], buf.at[block_rows(0), :], s1_recv.at[t, 0]
            ).start()

        @pl.when(moves)
        def _(t=t):
            stage_copy(t, 0).start()

        for e in NEAREST[1:]:
            stage_copy(t, e).start()

    def await_stage(t, places):
        src, buf = stage_one[t]
        for place in places:
            pltpu.make_async_copy(
                src.at[:, group_cols(0)], buf.at[block_rows(place), :], s1_recv.at[t, place]
            ).wait()

    bufs = (kb, vb)

    def slot_of(way, hops):
        if hops in (0, 4):
            return hops
        return hops if way == 0 else 4 + hops

    def half_of(t, slot, half):
        return bufs[t].at[slot, pl.ds(half * HALF, HALF), :]

    def hop(way, t, half, hops):
        return remote(
            half_of(t, slot_of(way, hops - 1), half),
            half_of(t, slot_of(way, hops), half),
            ring_send.at[way, t, half, hops],
            ring_recv.at[way, t, half, hops],
            s,
            (right, left)[way],
        )

    def across(t, slot, half):
        return remote(
            half_of(t, slot, half),
            half_of(t, 8 + slot, half),
            sib_send.at[t, slot, half],
            sib_recv.at[t, slot, half],
            sibling,
            g,
        )

    hops_used = [
        (way, t, half, n)
        for n in range(1, 5)
        for t in range(2)
        for half in range(HALVES)
        for way in range(2)
        if n < 4 or way == t
    ]

    def attend(slots, first):
        def one_head(h):
            lanes = slice(h * HD, (h + 1) * HD)
            q = qb[:, lanes]
            scores = [
                lax.dot_general(
                    q, kb[slot, :, lanes], (((1,), (1,)), ((), ())), preferred_element_type=F32
                )
                for slot in slots
            ]
            top = functools.reduce(jnp.maximum, scores)
            top = jnp.max(top, axis=1, keepdims=True)
            top = jnp.broadcast_to(top, (NBLK, HD))
            if not first:
                old = peak[h]
                top = jnp.maximum(old, top)
            peak[h] = top
            wide = jnp.concatenate([top, top], axis=1)
            part = None
            mixed = None
            for slot, score in zip(slots, scores):
                weights = jnp.exp2((score - wide) * EXP2_SCALE)
                halves = weights[:, :HD] + weights[:, HD:]
                part = halves if part is None else part + halves
                term = jnp.dot(
                    weights.astype(BF16), vb[slot, :, lanes], preferred_element_type=F32
                )
                mixed = term if mixed is None else mixed + term
            if first:
                total[h] = part
                acc[h] = mixed
            else:
                fade = jnp.exp2((old - top) * EXP2_SCALE)
                total[h] = total[h] * fade + part
                acc[h] = acc[h] * fade + mixed

        for h in range(HG):
            one_head(h)

    per_half = NZ // HALVES
    for t in range(2):
        for half in range(HALVES):
            await_stage(t, range(half * per_half, (half + 1) * per_half))
            hop(0, t, half, 1).start()
            hop(1, t, half, 1).start()
            across(t, 0, half).start()
    cw_ref[:, 48:, :] = jnp.zeros((9, 80, cw_ref.shape[2]), BF16)
    pieces = [(t, half) for t in range(2) for half in range(HALVES)]
    for n in range(1, 4):
        for t, half in pieces:
            for way in range(2):
                hop(way, t, half, n).wait_recv()
                if (way, t, half, n + 1) in hops_used:
                    hop(way, t, half, n + 1).start()
                across(t, slot_of(way, n), half).start()
        if n == 1:
            await_stage(2, range(NZ))
            for t, half in pieces:
                across(t, 0, half).wait_recv()
            attend((0, 8), True)
        for t, half in pieces:
            for way in range(2):
                across(t, slot_of(way, n), half).wait_recv()
        attend((n, 4 + n, 8 + n, 12 + n), False)
    for half in range(HALVES):
        for t in range(2):
            hop(t, t, half, 4).wait_recv()
            across(t, 4, half).start()
    for t, half in pieces:
        across(t, 4, half).wait_recv()
    attend((4, 12), False)

    for h in range(HG):
        lanes = slice(h * HD, (h + 1) * HD)
        ob[:, lanes] = (acc[h] / jnp.sum(total[h], axis=1, keepdims=True)).astype(BF16)

    def back_copy(place):
        zp = (z + NEAREST[place]) % NZ
        return remote(
            ob.at[block_rows(place), :],
            att.at[:, group_cols(z)],
            o_send.at[place],
            o_recv.at[place],
            swap_sec,
            swap_seq(zp),
        )

    for place in range(NZ - 1, 0, -1):
        back_copy(place).start()

    @pl.when(moves)
    def _():
        back_copy(0).start()

    @pl.when(stays)
    def _():
        pltpu.make_async_copy(
            ob.at[block_rows(0), :], att.at[:, group_cols(z)], o_recv.at[0]
        ).start()

    for load in loads:
        load.wait()
    for place in range(NZ):
        zp = (z + NZ - NEAREST[place]) % NZ
        pltpu.make_async_copy(
            ob.at[block_rows(0), :], att.at[:, group_cols(zp)], o_recv.at[place]
        ).wait()

    hidden = res_ref[...].astype(F32) + gate_ref[...] * att[...].astype(F32)
    center = hidden - jnp.mean(hidden, axis=1, keepdims=True)
    normed = center * lax.rsqrt(jnp.mean(center * center, axis=1, keepdims=True) + norm_eps)
    modulated = (normed * (1.0 + scale_ref[...]) + shift_ref[...]).astype(BF16)
    patches = (
        lax.dot_general(
            modulated, fw_ref[...], (((1,), (1,)), ((), ())), preferred_element_type=F32
        )
        + fb_ref[...]
    ) / scaling
    pat[...] = patches.astype(BF16).astype(F32)
    even = pat[pl.ds(0, F, stride=2), :]
    odd = pat[pl.ds(1, F, stride=2), :]
    side = 2 * LATC
    tile = jnp.concatenate([even[:, :side], odd[:, :side], even[:, side:], odd[:, side:]], axis=1)
    tiles[0, 0:1, :] = tile[:1]
    tiles[0, 1:2, :] = tile[:1]
    tiles[0, 2:8, :] = tile[:6]
    for part in (1, 2):
        tiles[part] = tile[4 * part - 2 : 4 * part + 6]
    tiles[3, 0:6, :] = tile[10:16]
    tiles[3, 6:8, :] = tile[14:16]

    def halo_copy(dy, dx, sp):
        place = (1 - dy) * 3 + 1 - dx
        return remote(
            tiles.at[sp],
            near_tiles.at[s, place],
            halo_send.at[place, sp],
            halo_recv.at[place, s],
            sp,
            g + dy * 2 * NY + dx,
        )

    for dy, dx in AROUND:
        for_sections(dy, dx, lambda sp: halo_copy(dy, dx, sp).start())
    near_tiles[s, 4] = tiles[s]
    for dy, dx in AROUND:
        if (dy, dx) != (0, 0):
            place = (1 + dy) * 3 + 1 + dx

            @pl.when(jnp.logical_not(there(dy, dx)))
            def _():
                for sp in range(4):
                    near_tiles[sp, place] = jnp.zeros((8, 128), F32)

    for t in range(3):

        @pl.when(moves)
        def _(t=t):
            stage_copy(t, 0).wait_send()

        for e in NEAREST[1:]:
            stage_copy(t, e).wait_send()
    for used in hops_used:
        hop(*used).wait_send()
    for t, half in pieces:
        for slot in range(8):
            across(t, slot, half).wait_send()
    for place in range(1, NZ):
        back_copy(place).wait_send()

    @pl.when(moves)
    def _():
        back_copy(0).wait_send()

    def halo_wait(dy, dx, sp):
        place = (1 + dy) * 3 + 1 + dx
        pltpu.make_async_copy(
            tiles.at[0], near_tiles.at[sp, place], halo_recv.at[place, sp]
        ).wait()

    for dy, dx in AROUND:
        for_sections(dy, dx, lambda sp: halo_wait(dy, dx, sp))

    for yy in range(4):
        vert, dr = ((0, 1), (1, 0), (1, 1), (2, 0))[yy]
        lo = dr * BC * LATC
        hi = lo + BC * LATC
        sides = [near_tiles[:, vert * 3 + dx].reshape(32, 128) for dx in range(3)]
        strip = jnp.concatenate(
            [
                sides[0][:, hi - LATC : hi],
                sides[1][:, lo:hi],
                sides[2][:, lo : lo + LATC],
                jnp.zeros((32, 2 * LATC), F32),
            ],
            axis=1,
        )
        for x in range(BC):
            moved = strip if x == 0 else pltpu.roll(strip, 128 - x * LATC, axis=1)
            moved = moved.reshape(4, 8, 128)
            for dt in range(3):
                piece = moved[:, dt : dt + 4, :].reshape(16, 128)
                for dy in range(3):
                    row = yy - dy
                    if 0 <= row < BR:
                        windows[dt * 3 + dy, pl.ds(row * BC + x, 16, stride=8), :] = piece
    left_side = jnp.concatenate([windows[tap].astype(BF16) for tap in range(9)], axis=1)
    conv = jnp.dot(
        left_side, cw_ref[...].reshape(9 * 128, cw_ref.shape[2]), preferred_element_type=F32
    )
    conv = (conv + cb_ref[...]) * gg_ref[...] + gb_ref[...]
    out_ref[...] = (conv / (1.0 + jnp.exp(-conv))).astype(BF16)

    for dy, dx in AROUND:
        for_sections(dy, dx, lambda sp: halo_copy(dy, dx, sp).wait_send())


def on_device(
    queries,
    keys,
    values,
    residual,
    shift_mod,
    scale_mod,
    gate_mod,
    final_weight,
    final_bias,
    conv_weight,
    conv_bias,
    group_gain,
    group_bias,
):
    any_spec = pl.BlockSpec(memory_space=pl.ANY)
    dma = pltpu.SemaphoreType.DMA
    vae_width = conv_weight.shape[1]
    features = pl.pallas_call(
        whole_kernel,
        out_shape=jax.ShapeDtypeStruct((4 * 4 * BR * BC, vae_width), BF16),
        in_specs=[any_spec] * 13,
        out_specs=pl.BlockSpec(memory_space=pltpu.VMEM),
        scratch_shapes=[
            pltpu.VMEM((NBLK, GW), BF16),
            pltpu.VMEM((16, NBLK, GW), BF16),
            pltpu.VMEM((16, NBLK, GW), BF16),
            pltpu.VMEM((NBLK, GW), BF16),
            pltpu.VMEM((TOK, H * HD), BF16),
            pltpu.VMEM((HG, NBLK, HD), F32),
            pltpu.VMEM((HG, NBLK, HD), F32),
            pltpu.VMEM((HG, NBLK, HD), F32),
            pltpu.VMEM((TOK, 4 * LATC), F32),
            pltpu.VMEM((4, 8, 128), F32),
            pltpu.VMEM((4, 9, 8, 128), F32),
            pltpu.VMEM((9, 4 * 4 * BR * BC, 128), F32),
            pltpu.VMEM((TOK, H * HD), BF16),
            pltpu.VMEM((1, H * HD), F32),
            pltpu.VMEM((1, H * HD), F32),
            pltpu.VMEM((1, H * HD), F32),
            pltpu.VMEM((4 * LATC, H * HD), BF16),
            pltpu.VMEM((1, 4 * LATC), F32),
            pltpu.VMEM((9, 128, vae_width), BF16),
            pltpu.VMEM((1, vae_width), F32),
            pltpu.VMEM((1, vae_width), F32),
            pltpu.VMEM((1, vae_width), F32),
            dma((9,)),
            dma((9,)),
            dma((3, NZ)),
            dma((3, NZ)),
            dma((2, 2, HALVES, 5)),
            dma((2, 2, HALVES, 5)),
            dma((2, 8, HALVES)),
            dma((2, 8, HALVES)),
            dma((NZ,)),
            dma((NZ,)),
            dma((9, 4)),
            dma((9, 4)),
        ],
        compiler_params=pltpu.CompilerParams(
            collective_id=0, has_side_effects=True, vmem_limit_bytes=60 * 1024 * 1024
        ),
        name="whole",
    )(
        queries[0],
        keys[0],
        values[0],
        residual[0],
        shift_mod,
        scale_mod,
        gate_mod,
        final_weight.T,
        final_bias[None],
        conv_weight,
        conv_bias[None],
        group_gain[None],
        group_bias[None],
    )
    return features.reshape(4, 4, 1, BR * BC, vae_width)


def solution(mesh):
    return jax.shard_map(
        on_device,
        mesh=mesh,
        in_specs=(
            P("sec", "seq", None),
            P("sec", "seq", None),
            P("sec", "seq", None),
            P("sec", "seq", None),
            P("sec", None),
            P("sec", None),
            P("sec", None),
            P(),
            P(),
            P(),
            P(),
            P(),
            P(),
        ),
        out_specs=P(None, "sec", "seq", None, None),
        check_vma=False,
    )
```

```python
import functools

import jax
import jax.numpy as jnp
from jax import lax
from jax.experimental import pallas as pl
from jax.experimental.pallas import tpu as pltpu
from jax.sharding import PartitionSpec as P

H = 24
HD = 128
LATC = 16
F = 16
BR = 2
BC = 4
NZ = 8
NY = 8
TOK = 32
HG = 3
GW = HG * HD
NBLK = NZ * TOK

scaling = 0.476986
norm_eps = 1e-06
EXP2_SCALE = HD ** (-0.5) * 1.4426950408889634
F32 = jnp.float32
BF16 = jnp.bfloat16


def remote(src, dst, send_sem, recv_sem, sec, seq):
    return pltpu.make_async_remote_copy(
        src_ref=src,
        dst_ref=dst,
        send_sem=send_sem,
        recv_sem=recv_sem,
        device_id={"sec": sec, "seq": seq},
        device_id_type=pl.DeviceIdType.MESH,
    )


def signal(sem, sec, seq):
    pl.semaphore_signal(
        sem, inc=1, device_id={"sec": sec, "seq": seq}, device_id_type=pl.DeviceIdType.MESH
    )


def position():
    s = lax.axis_index("sec")
    g = lax.axis_index("seq")
    return s, g, s % 2, s // 2, g // (2 * NY), (g // 2) % NY, g % 2

NEAREST = (0, 1, 7, 2, 6, 3, 5, 4)
AROUND = [(dy, dx) for dy in (-1, 0, 1) for dx in (-1, 0, 1)]

ITEMS = (
    ((0, 0), (0, 7), (0, 6)),
    ((0, 1), (0, 2), (0, 5)),
    ((0, 3), (0, 4), (1, 1)),
    ((1, 2), (1, 3), (1, 0)),
    ((1, 4), (1, 5), (1, 7)),
    ((1, 6), (2, 3), (2, 4)),
    ((2, 5), (2, 6), (2, 2)),
    ((2, 7), (2, 0), (2, 1)),
)
STREAM_START = ((5, 0, 3), (4, 7, 2))
STREAM_HOPS = ((5, 5, 4), (4, 5, 5))
STREAM_ENTRY = ((3, 2, 2), (2, 2, 3))
MOST_HOPS = 5
MOST_STEPS = 4
HALVES = 2
PER_HALF = NZ // HALVES
HALF = NBLK // HALVES
STREAMS = [(way, h) for h in range(HG) for way in range(2)]


def stream_place(way, h, y):
    first = STREAM_START[way][h]
    return (y + NY - first) % NY if way == 0 else (first + NY - y) % NY


def block_order(y, h):
    found = []
    for way in range(2):
        place = stream_place(way, h, y)
        past = place - STREAM_ENTRY[way][h]
        if past >= 0 and place <= STREAM_HOPS[way][h]:
            found += [(min(n, past + 1), n, way) for n in range(1, place + 1)]
    return [(h * 2 + way) * MOST_HOPS + n - 1 for _, n, way in sorted(found)]


ORDER = [
    [[block_order(y, ITEMS[y][i][0])[k] for y in range(NY)] for k in range(NY - 1)]
    for i in range(HG)
]


def pick(table, index):
    out = table[0]
    for k in range(1, len(table)):
        out = jnp.where(index == k, table[k], out)
    return out


def whole_kernel(
    q_ref,
    k_ref,
    v_ref,
    res_hbm,
    shift_hbm,
    scale_hbm,
    gate_hbm,
    fw_hbm,
    fb_hbm,
    cw_hbm,
    cb_hbm,
    gg_hbm,
    gb_hbm,
    out_ref,
    q_own,
    own,
    beside,
    ring,
    cross,
    qb,
    ob,
    att,
    peak,
    total,
    acc,
    pat,
    tiles,
    near_tiles,
    windows,
    res_ref,
    shift_ref,
    scale_ref,
    gate_ref,
    fw_ref,
    fb_ref,
    cw_ref,
    cb_ref,
    gg_ref,
    gb_ref,
    load_sem,
    cw_sem,
    s1_send,
    s1_recv,
    q_send,
    q_recv,
    ring_send,
    ring_recv,
    own_send,
    beside_send,
    beside_recv,
    cross_send,
    cross_recv,
    o_send,
    o_recv,
    sec_send,
    sec_recv,
    halo_send,
    halo_recv,
):
    s, g, core, xl, z, y, xh = position()
    stays = core == xh
    moves = jnp.logical_not(stays)
    swap_sec = xl * 2 + xh

    def swap_seq(zp, yp):
        return (zp * NY + yp) * 2 + core

    def ring_seq(yp):
        return (z * NY + yp) * 2 + xh

    steps = (1, NY - 1)
    sibling = xl * 2 + 1 - core
    col = y * 2 + xh
    last_col = 2 * NY - 1

    item_head = [pick([ITEMS[k][i][0] for k in range(NY)], y) for i in range(HG)]
    item_y = [pick([ITEMS[k][i][1] for k in range(NY)], y) for i in range(HG)]
    homes = {item: (k, i) for k in range(NY) for i, item in enumerate(ITEMS[k])}
    query_chip = [pick([homes[j, k][0] for k in range(NY)], y) for j in range(HG)]
    query_slot = [pick([homes[j, k][1] for k in range(NY)], y) for j in range(HG)]
    places = {(way, h): stream_place(way, h, y) for way, h in STREAMS}

    def sends_own(way, h):
        return places[way, h] < STREAM_HOPS[way][h]

    def takes(way, h, n):
        place = places[way, h]
        working = jnp.logical_and(place >= STREAM_ENTRY[way][h], place <= STREAM_HOPS[way][h])
        return jnp.logical_and(working, place >= n)

    def passes(way, h):
        place = places[way, h]
        return jnp.logical_and(place >= STREAM_ENTRY[way][h], place < STREAM_HOPS[way][h])

    def step_of(way, h, n):
        return jnp.minimum(n, places[way, h] - STREAM_ENTRY[way][h] + 1)

    def there(dy, dx):
        row_ok = z + dy >= 0 if dy < 0 else z + dy < NZ
        col_ok = col + dx >= 0 if dx < 0 else col + dx <= last_col
        return jnp.logical_and(row_ok, col_ok)

    neighbours = [(dy, dx) for dy, dx in AROUND if (dy, dx) != (0, 0)]

    barrier = pltpu.get_barrier_semaphore()
    for e in NEAREST[1:]:
        signal(barrier, swap_sec, swap_seq((z + e) % NZ, y))

    @pl.when(moves)
    def _():
        signal(barrier, swap_sec, swap_seq(z, y))

    for e in range(1, NY):
        signal(barrier, s, ring_seq((y + e) % NY))
    for ds in range(1, 4):
        signal(barrier, (s + ds) % 4, g)
    for dy, dx in neighbours:

        @pl.when(there(dy, dx))
        def _(dy=dy, dx=dx):
            signal(barrier, s, g + dy * 2 * NY + dx)

    loads = [
        pltpu.make_async_copy(src, dst, load_sem.at[i])
        for i, (src, dst) in enumerate(
            (
                (res_hbm, res_ref),
                (shift_hbm, shift_ref),
                (scale_hbm, scale_ref),
                (gate_hbm, gate_ref),
                (fw_hbm, fw_ref),
                (fb_hbm, fb_ref),
                (cb_hbm, cb_ref),
                (gg_hbm, gg_ref),
                (gb_hbm, gb_ref),
            )
        )
    ] + [
        pltpu.make_async_copy(
            cw_hbm.at[pl.ds(tap * 48, 48), :], cw_ref.at[tap, pl.ds(0, 48), :], cw_sem.at[tap]
        )
        for tap in range(9)
    ]
    for load in loads:
        load.start()

    n_rows = 3 - jnp.where(z == 0, 1, 0) - jnp.where(z == NZ - 1, 1, 0)
    n_cols = 3 - jnp.where(col == 0, 1, 0) - jnp.where(col == last_col, 1, 0)
    pl.semaphore_wait(barrier, 2 * NZ + 1 - jnp.where(stays, 1, 0) + n_rows * n_cols)

    def group_cols(zp):
        return pl.ds(pl.multiple_of(zp * GW, HD), GW)

    def head_cols(h):
        return pl.ds(pl.multiple_of(h * HD, HD), HD)

    def block_rows(place):
        return pl.ds(place * TOK, TOK)

    sources = (k_ref, v_ref, q_ref)

    def landing(t, place):
        if t == 2:
            return q_own.at[block_rows(place), :]
        return own.at[place // PER_HALF, t, block_rows(place % PER_HALF), :]

    def stage_copy(t, place):
        zp = (z + NZ - NEAREST[place]) % NZ
        return remote(
            sources[t].at[:, group_cols(zp)],
            landing(t, place),
            s1_send.at[t, place],
            s1_recv.at[t, place],
            swap_sec,
            swap_seq(zp, y),
        )

    def start_stage(t, first, last):
        for place in range(first, last):
            if place > 0:
                stage_copy(t, place).start()
                continue

            @pl.when(stays)
            def _():
                pltpu.make_async_copy(
                    sources[t].at[:, group_cols(z)], landing(t, 0), s1_recv.at[t, 0]
                ).start()

            @pl.when(moves)
            def _():
                stage_copy(t, 0).start()

    def await_stage(t, first, last):
        for place in range(first, last):
            pltpu.make_async_copy(
                sources[t].at[:, group_cols(0)], landing(t, place), s1_recv.at[t, place]
            ).wait()

    for half in range(HALVES):
        for t in range(2):
            start_stage(t, half * PER_HALF, (half + 1) * PER_HALF)
    start_stage(2, 0, NZ)

    def slot_of(way, h, n):
        return (h * 2 + way) * MOST_HOPS + n - 1

    def own_hop(way, h, half):
        place = places[way, h]
        target = jnp.maximum(STREAM_ENTRY[way][h], place + 1)
        slot = slot_of(way, h, target - place)
        first = STREAM_START[way][h]
        chip = (first + target) % NY if way == 0 else (first + NY - target) % NY
        return remote(
            own.at[half, :, :, pl.ds(h * HD, HD)],
            ring.at[slot, half],
            own_send.at[half, slot_of(way, h, 1)],
            ring_recv.at[half, slot],
            s,
            ring_seq(chip),
        )

    def hop(way, h, half, n):
        slot = slot_of(way, h, n)
        return remote(
            ring.at[slot, half],
            ring.at[slot + 1, half],
            ring_send.at[half, slot],
            ring_recv.at[half, slot + 1],
            s,
            ring_seq((y + steps[way]) % NY),
        )

    def arrived(way, h, half, n):
        slot = slot_of(way, h, n)
        return pltpu.make_async_copy(
            ring.at[slot, half], ring.at[slot, half], ring_recv.at[half, slot]
        )

    def own_across(half):
        return remote(
            own.at[half], beside.at[half], beside_send.at[half], beside_recv.at[half], sibling, g
        )

    def across(way, h, half, n):
        slot = slot_of(way, h, n)
        return remote(
            ring.at[slot, half],
            cross.at[slot, half],
            cross_send.at[half, slot],
            cross_recv.at[half, slot],
            sibling,
            g,
        )

    def start_streams(half):
        for t in range(2):
            await_stage(t, half * PER_HALF, (half + 1) * PER_HALF)
        for way, h in STREAMS:

            @pl.when(sends_own(way, h))
            def _(way=way, h=h):
                own_hop(way, h, half).start()

        own_across(half).start()

    def pass_on(half, step):
        for way, h in STREAMS:
            hops = STREAM_HOPS[way][h]
            for n in range(step, hops + 1):

                @pl.when(jnp.logical_and(takes(way, h, n), step_of(way, h, n) == step))
                def _(way=way, h=h, n=n):
                    arrived(way, h, half, n).wait()

                    if n < hops:

                        @pl.when(passes(way, h))
                        def _():
                            hop(way, h, half, n).start()

                    across(way, h, half, n).start()

    def for_crossed(half, one):
        for way, h in STREAMS:
            for n in range(1, STREAM_HOPS[way][h] + 1):

                @pl.when(takes(way, h, n))
                def _(way=way, h=h, n=n):
                    one(across(way, h, half, n))

    def attend(blocks_of, first):
        for i in range(HG):
            q = qb[i]
            blocks = blocks_of(i)
            scores = [
                lax.dot_general(
                    q, k_block(), (((1,), (1,)), ((), ())), preferred_element_type=F32
                )
                for k_block, _ in blocks
            ]
            top = functools.reduce(jnp.maximum, scores)
            top = jnp.max(top, axis=1, keepdims=True)
            top = jnp.broadcast_to(top, (NBLK, HD))
            if not first:
                old = peak[i]
                top = jnp.maximum(old, top)
            peak[i] = top
            wide = jnp.concatenate([top, top], axis=1)
            part = None
            mixed = None
            for (_, v_block), score in zip(blocks, scores):
                weights = jnp.exp2((score - wide) * EXP2_SCALE)
                halves = weights[:, :HD] + weights[:, HD:]
                part = halves if part is None else part + halves
                term = jnp.dot(weights.astype(BF16), v_block(), preferred_element_type=F32)
                mixed = term if mixed is None else mixed + term
            if first:
                total[i] = part
                acc[i] = mixed
            else:
                fade = jnp.exp2((old - top) * EXP2_SCALE)
                total[i] = total[i] * fade + part
                acc[i] = acc[i] * fade + mixed

    def joined(one, other):
        return lambda: jnp.concatenate([one(), other()], axis=0)

    def blocks_of(half, with_own, arrivals):
        def of(i):
            out = []
            if with_own:
                lanes = head_cols(item_head[i])
                out.append(
                    tuple(
                        joined(
                            lambda t=t: own[half, t, :, lanes], lambda t=t: beside[half, t, :, lanes]
                        )
                        for t in range(2)
                    )
                )
            for k in arrivals:
                slot = pick(ORDER[i][k], y)
                out.append(
                    tuple(
                        joined(
                            lambda t=t, slot=slot: ring[slot, half, t],
                            lambda t=t, slot=slot: cross[slot, half, t],
                        )
                        for t in range(2)
                    )
                )
            return out

        return of

    start_streams(0)
    cw_ref[:, 48:, :] = jnp.zeros((9, 80, cw_ref.shape[2]), BF16)
    pass_on(0, 1)
    pass_on(0, 2)
    start_streams(1)
    pass_on(0, 3)
    pass_on(0, 4)
    pass_on(1, 1)
    await_stage(2, 0, NZ)

    def query_copy(j):
        return remote(
            q_own.at[:, pl.ds(j * HD, HD)],
            qb.at[query_slot[j]],
            q_send.at[j],
            q_recv.at[query_slot[j]],
            s,
            ring_seq(query_chip[j]),
        )

    for j in range(HG):

        @pl.when(query_chip[j] != y)
        def _(j=j):
            query_copy(j).start()

        @pl.when(query_chip[j] == y)
        def _(j=j):
            pltpu.make_async_copy(
                q_own.at[:, pl.ds(j * HD, HD)], qb.at[query_slot[j]], q_recv.at[query_slot[j]]
            ).start()

    pass_on(1, 2)
    for i in range(HG):
        pltpu.make_async_copy(q_own.at[:, pl.ds(0, HD)], qb.at[i], q_recv.at[i]).wait()
    own_across(0).wait_recv()
    for_crossed(0, lambda copy: copy.wait_recv())
    attend(blocks_of(0, True, (0, 1, 2)), True)
    pass_on(1, 3)
    attend(blocks_of(0, False, (3, 4, 5, 6)), False)
    pass_on(1, 4)
    own_across(1).wait_recv()
    for_crossed(1, lambda copy: copy.wait_recv())
    attend(blocks_of(1, True, (0, 1, 2)), False)
    attend(blocks_of(1, False, (3, 4, 5, 6)), False)

    def back_copy(i, place):
        zp = (z + NEAREST[place]) % NZ
        return remote(
            ob.at[i, block_rows(place), :],
            att.at[:, head_cols(z * HG + item_head[i])],
            o_send.at[i, place],
            o_recv.at[item_head[i], place],
            swap_sec,
            swap_seq(zp, item_y[i]),
        )

    for i in range(HG):
        ob[i] = (acc[i] / jnp.sum(total[i], axis=1, keepdims=True)).astype(BF16)
        for place in range(NZ - 1, 0, -1):
            back_copy(i, place).start()
        here = jnp.logical_and(stays, item_y[i] == y)

        @pl.when(jnp.logical_not(here))
        def _(i=i):
            back_copy(i, 0).start()

        @pl.when(here)
        def _(i=i):
            pltpu.make_async_copy(
                ob.at[i, block_rows(0), :],
                att.at[:, head_cols(z * HG + item_head[i])],
                o_recv.at[item_head[i], 0],
            ).start()

    for load in loads:
        load.wait()
    for place in range(NZ):
        zp = (z + NZ - NEAREST[place]) % NZ
        for h in range(HG):
            pltpu.make_async_copy(
                ob.at[0, block_rows(0), :], att.at[:, head_cols(zp * HG + h)], o_recv.at[h, place]
            ).wait()

    hidden = res_ref[...].astype(F32) + gate_ref[...] * att[...].astype(F32)
    center = hidden - jnp.mean(hidden, axis=1, keepdims=True)
    normed = center * lax.rsqrt(jnp.mean(center * center, axis=1, keepdims=True) + norm_eps)
    modulated = (normed * (1.0 + scale_ref[...]) + shift_ref[...]).astype(BF16)
    patches = (
        lax.dot_general(
            modulated, fw_ref[...], (((1,), (1,)), ((), ())), preferred_element_type=F32
        )
        + fb_ref[...]
    ) / scaling
    pat[...] = patches.astype(BF16).astype(F32)
    even = pat[pl.ds(0, F, stride=2), :]
    odd = pat[pl.ds(1, F, stride=2), :]
    side = 2 * LATC
    tile = jnp.concatenate([even[:, :side], odd[:, :side], even[:, side:], odd[:, side:]], axis=1)
    tiles[0, 0:1, :] = tile[:1]
    tiles[0, 1:2, :] = tile[:1]
    tiles[0, 2:8, :] = tile[:6]
    for part in (1, 2):
        tiles[part] = tile[4 * part - 2 : 4 * part + 6]
    tiles[3, 0:6, :] = tile[10:16]
    tiles[3, 6:8, :] = tile[14:16]

    def frames_copy(ds):
        sp = (s + ds) % 4
        return remote(
            tiles.at[sp], near_tiles.at[4, s], sec_send.at[ds], sec_recv.at[4 - ds], sp, g
        )

    for ds in range(1, 4):
        frames_copy(ds).start()
    near_tiles[4, s] = tiles[s]

    def halo_copy(dy, dx):
        place = (1 - dy) * 3 + 1 - dx
        return remote(
            near_tiles.at[4],
            near_tiles.at[place],
            halo_send.at[place],
            halo_recv.at[place],
            s,
            g + dy * 2 * NY + dx,
        )

    for dy, dx in neighbours:

        @pl.when(jnp.logical_not(there(dy, dx)))
        def _(dy=dy, dx=dx):
            near_tiles[(1 + dy) * 3 + 1 + dx] = jnp.zeros((4, 8, 128), F32)

    for ds in range(1, 4):
        pltpu.make_async_copy(
            tiles.at[0], near_tiles.at[4, (s + ds) % 4], sec_recv.at[ds]
        ).wait()
    for dy, dx in neighbours:

        @pl.when(there(dy, dx))
        def _(dy=dy, dx=dx):
            halo_copy(dy, dx).start()

    for t in range(3):

        @pl.when(moves)
        def _(t=t):
            stage_copy(t, 0).wait_send()

        for place in range(1, NZ):
            stage_copy(t, place).wait_send()
    for j in range(HG):

        @pl.when(query_chip[j] != y)
        def _(j=j):
            query_copy(j).wait_send()

    for half in range(HALVES):
        own_across(half).wait_send()
        for way, h in STREAMS:

            @pl.when(sends_own(way, h))
            def _(way=way, h=h, half=half):
                own_hop(way, h, half).wait_send()

            for n in range(1, STREAM_HOPS[way][h]):

                @pl.when(jnp.logical_and(takes(way, h, n), passes(way, h)))
                def _(way=way, h=h, half=half, n=n):
                    hop(way, h, half, n).wait_send()

        for_crossed(half, lambda copy: copy.wait_send())
    for i in range(HG):
        for place in range(1, NZ):
            back_copy(i, place).wait_send()

        @pl.when(jnp.logical_not(jnp.logical_and(stays, item_y[i] == y)))
        def _(i=i):
            back_copy(i, 0).wait_send()

    for ds in range(1, 4):
        frames_copy(ds).wait_send()

    for dy, dx in neighbours:

        @pl.when(there(dy, dx))
        def _(dy=dy, dx=dx):
            place = (1 + dy) * 3 + 1 + dx
            pltpu.make_async_copy(
                near_tiles.at[4], near_tiles.at[place], halo_recv.at[place]
            ).wait()

    for yy in range(4):
        vert, dr = ((0, 1), (1, 0), (1, 1), (2, 0))[yy]
        lo = dr * BC * LATC
        hi = lo + BC * LATC
        sides = [near_tiles[vert * 3 + dx].reshape(32, 128) for dx in range(3)]
        strip = jnp.concatenate(
            [
                sides[0][:, hi - LATC : hi],
                sides[1][:, lo:hi],
                sides[2][:, lo : lo + LATC],
                jnp.zeros((32, 2 * LATC), F32),
            ],
            axis=1,
        )
        for x in range(BC):
            moved = strip if x == 0 else pltpu.roll(strip, 128 - x * LATC, axis=1)
            moved = moved.reshape(4, 8, 128)
            for dt in range(3):
                piece = moved[:, dt : dt + 4, :].reshape(16, 128)
                for dy in range(3):
                    row = yy - dy
                    if 0 <= row < BR:
                        windows[dt * 3 + dy, pl.ds(row * BC + x, 16, stride=8), :] = piece
    left_side = jnp.concatenate([windows[tap].astype(BF16) for tap in range(9)], axis=1)
    conv = jnp.dot(
        left_side, cw_ref[...].reshape(9 * 128, cw_ref.shape[2]), preferred_element_type=F32
    )
    conv = (conv + cb_ref[...]) * gg_ref[...] + gb_ref[...]
    out_ref[...] = (conv / (1.0 + jnp.exp(-conv))).astype(BF16)

    for dy, dx in neighbours:

        @pl.when(there(dy, dx))
        def _(dy=dy, dx=dx):
            halo_copy(dy, dx).wait_send()


def on_device(
    queries,
    keys,
    values,
    residual,
    shift_mod,
    scale_mod,
    gate_mod,
    final_weight,
    final_bias,
    conv_weight,
    conv_bias,
    group_gain,
    group_bias,
):
    any_spec = pl.BlockSpec(memory_space=pl.ANY)
    dma = pltpu.SemaphoreType.DMA
    vae_width = conv_weight.shape[1]
    slots = 2 * HG * MOST_HOPS
    features = pl.pallas_call(
        whole_kernel,
        out_shape=jax.ShapeDtypeStruct((4 * 4 * BR * BC, vae_width), BF16),
        in_specs=[any_spec] * 13,
        out_specs=pl.BlockSpec(memory_space=pltpu.VMEM),
        scratch_shapes=[
            pltpu.VMEM((NBLK, GW), BF16),
            pltpu.VMEM((HALVES, 2, HALF, GW), BF16),
            pltpu.VMEM((HALVES, 2, HALF, GW), BF16),
            pltpu.VMEM((slots, HALVES, 2, HALF, HD), BF16),
            pltpu.VMEM((slots, HALVES, 2, HALF, HD), BF16),
            pltpu.VMEM((HG, NBLK, HD), BF16),
            pltpu.VMEM((HG, NBLK, HD), BF16),
            pltpu.VMEM((TOK, H * HD), BF16),
            pltpu.VMEM((HG, NBLK, HD), F32),
            pltpu.VMEM((HG, NBLK, HD), F32),
            pltpu.VMEM((HG, NBLK, HD), F32),
            pltpu.VMEM((TOK, 4 * LATC), F32),
            pltpu.VMEM((4, 8, 128), F32),
            pltpu.VMEM((9, 4, 8, 128), F32),
            pltpu.VMEM((9, 4 * 4 * BR * BC, 128), F32),
            pltpu.VMEM((TOK, H * HD), BF16),
            pltpu.VMEM((1, H * HD), F32),
            pltpu.VMEM((1, H * HD), F32),
            pltpu.VMEM((1, H * HD), F32),
            pltpu.VMEM((4 * LATC, H * HD), BF16),
            pltpu.VMEM((1, 4 * LATC), F32),
            pltpu.VMEM((9, 128, vae_width), BF16),
            pltpu.VMEM((1, vae_width), F32),
            pltpu.VMEM((1, vae_width), F32),
            pltpu.VMEM((1, vae_width), F32),
            dma((9,)),
            dma((9,)),
            dma((3, NZ)),
            dma((3, NZ)),
            dma((HG,)),
            dma((HG,)),
            dma((HALVES, slots)),
            dma((HALVES, slots)),
            dma((HALVES, slots)),
            dma((HALVES,)),
            dma((HALVES,)),
            dma((HALVES, slots)),
            dma((HALVES, slots)),
            dma((HG, NZ)),
            dma((HG, NZ)),
            dma((4,)),
            dma((4,)),
            dma((9,)),
            dma((9,)),
        ],
        compiler_params=pltpu.CompilerParams(
            collective_id=0, has_side_effects=True, vmem_limit_bytes=60 * 1024 * 1024
        ),
        name="whole",
    )(
        queries[0],
        keys[0],
        values[0],
        residual[0],
        shift_mod,
        scale_mod,
        gate_mod,
        final_weight.T,
        final_bias[None],
        conv_weight,
        conv_bias[None],
        group_gain[None],
        group_bias[None],
    )
    return features.reshape(4, 4, 1, BR * BC, vae_width)


def solution(mesh):
    return jax.shard_map(
        on_device,
        mesh=mesh,
        in_specs=(
            P("sec", "seq", None),
            P("sec", "seq", None),
            P("sec", "seq", None),
            P("sec", "seq", None),
            P("sec", None),
            P("sec", None),
            P("sec", None),
            P(),
            P(),
            P(),
            P(),
            P(),
            P(),
        ),
        out_specs=P(None, "sec", "seq", None, None),
        check_vma=False,
    )
```

```python
import functools

import jax
import jax.numpy as jnp
from jax import lax
from jax.experimental import pallas as pl
from jax.experimental.pallas import tpu as pltpu
from jax.sharding import PartitionSpec as P

H = 24
HD = 128
LATC = 16
F = 16
BR = 2
BC = 4
NZ = 8
NY = 8
TOK = 32
HG = 3
GW = HG * HD
NBLK = NZ * TOK

scaling = 0.476986
norm_eps = 1e-06
EXP2_SCALE = HD ** (-0.5) * 1.4426950408889634
F32 = jnp.float32
BF16 = jnp.bfloat16


def remote(src, dst, send_sem, recv_sem, sec, seq):
    return pltpu.make_async_remote_copy(
        src_ref=src,
        dst_ref=dst,
        send_sem=send_sem,
        recv_sem=recv_sem,
        device_id={"sec": sec, "seq": seq},
        device_id_type=pl.DeviceIdType.MESH,
    )


def signal(sem, sec, seq):
    pl.semaphore_signal(
        sem, inc=1, device_id={"sec": sec, "seq": seq}, device_id_type=pl.DeviceIdType.MESH
    )


def position():
    s = lax.axis_index("sec")
    g = lax.axis_index("seq")
    return s, g, s % 2, s // 2, g // (2 * NY), (g // 2) % NY, g % 2

NEAREST = (0, 1, 7, 2, 6, 3, 5, 4)
AROUND = [(dy, dx) for dy in (-1, 0, 1) for dx in (-1, 0, 1)]

ITEMS = (
    ((0, 0), (0, 7), (0, 6)),
    ((0, 1), (0, 2), (0, 5)),
    ((0, 3), (0, 4), (1, 1)),
    ((1, 2), (1, 3), (1, 0)),
    ((1, 4), (1, 5), (1, 7)),
    ((1, 6), (2, 3), (2, 4)),
    ((2, 5), (2, 6), (2, 2)),
    ((2, 7), (2, 0), (2, 1)),
)
STREAM_START = ((5, 0, 3), (4, 7, 2))
STREAM_HOPS = ((5, 5, 4), (4, 5, 5))
STREAM_ENTRY = ((3, 2, 2), (2, 2, 3))
MOST_HOPS = 5
MOST_STEPS = 4
HALVES = 2
PER_HALF = NZ // HALVES
HALF = NBLK // HALVES
STREAMS = [(way, h) for h in range(HG) for way in range(2)]


def stream_place(way, h, y):
    first = STREAM_START[way][h]
    return (y + NY - first) % NY if way == 0 else (first + NY - y) % NY


def block_order(y, h):
    found = []
    for way in range(2):
        place = stream_place(way, h, y)
        past = place - STREAM_ENTRY[way][h]
        if past >= 0 and place <= STREAM_HOPS[way][h]:
            found += [(min(n, past + 1), n, way) for n in range(1, place + 1)]
    return [(h * 2 + way) * MOST_HOPS + n - 1 for _, n, way in sorted(found)]


ORDER = [
    [[block_order(y, ITEMS[y][i][0])[k] for y in range(NY)] for k in range(NY - 1)]
    for i in range(HG)
]


def pick(table, index):
    out = table[0]
    for k in range(1, len(table)):
        out = jnp.where(index == k, table[k], out)
    return out


def gather_kernel(
    q_ref,
    k_ref,
    v_ref,
    qb,
    own,
    beside,
    ring,
    cross,
    q_own,
    s1_send,
    s1_recv,
    q_send,
    q_recv,
    ring_send,
    ring_recv,
    own_send,
    beside_send,
    beside_recv,
    cross_send,
    cross_recv,
):
    s, g, core, xl, z, y, xh = position()
    stays = core == xh
    moves = jnp.logical_not(stays)
    swap_sec = xl * 2 + xh

    def swap_seq(zp, yp):
        return (zp * NY + yp) * 2 + core

    def ring_seq(yp):
        return (z * NY + yp) * 2 + xh

    steps = (1, NY - 1)
    sibling = xl * 2 + 1 - core

    item_head = [pick([ITEMS[k][i][0] for k in range(NY)], y) for i in range(HG)]
    item_y = [pick([ITEMS[k][i][1] for k in range(NY)], y) for i in range(HG)]
    homes = {item: (k, i) for k in range(NY) for i, item in enumerate(ITEMS[k])}
    query_chip = [pick([homes[j, k][0] for k in range(NY)], y) for j in range(HG)]
    query_slot = [pick([homes[j, k][1] for k in range(NY)], y) for j in range(HG)]
    places = {(way, h): stream_place(way, h, y) for way, h in STREAMS}

    def sends_own(way, h):
        return places[way, h] < STREAM_HOPS[way][h]

    def takes(way, h, n):
        place = places[way, h]
        working = jnp.logical_and(place >= STREAM_ENTRY[way][h], place <= STREAM_HOPS[way][h])
        return jnp.logical_and(working, place >= n)

    def passes(way, h):
        place = places[way, h]
        return jnp.logical_and(place >= STREAM_ENTRY[way][h], place < STREAM_HOPS[way][h])

    def step_of(way, h, n):
        return jnp.minimum(n, places[way, h] - STREAM_ENTRY[way][h] + 1)

    barrier = pltpu.get_barrier_semaphore()
    for e in NEAREST[1:]:
        signal(barrier, swap_sec, swap_seq((z + e) % NZ, y))

    @pl.when(moves)
    def _():
        signal(barrier, swap_sec, swap_seq(z, y))

    for e in range(1, NY):
        signal(barrier, s, ring_seq((y + e) % NY))
    signal(barrier, sibling, g)
    pl.semaphore_wait(barrier, 2 * NZ - jnp.where(stays, 1, 0))

    def group_cols(zp):
        return pl.ds(pl.multiple_of(zp * GW, HD), GW)

    def head_cols(h):
        return pl.ds(pl.multiple_of(h * HD, HD), HD)

    def block_rows(place):
        return pl.ds(place * TOK, TOK)

    sources = (k_ref, v_ref, q_ref)

    def landing(t, place):
        if t == 2:
            return q_own.at[block_rows(place), :]
        return own.at[place // PER_HALF, t, block_rows(place % PER_HALF), :]

    def stage_copy(t, place):
        zp = (z + NZ - NEAREST[place]) % NZ
        return remote(
            sources[t].at[:, group_cols(zp)],
            landing(t, place),
            s1_send.at[t, place],
            s1_recv.at[t, place],
            swap_sec,
            swap_seq(zp, y),
        )

    def start_stage(t, first, last):
        for place in range(first, last):
            if place > 0:
                stage_copy(t, place).start()
                continue

            @pl.when(stays)
            def _():
                pltpu.make_async_copy(
                    sources[t].at[:, group_cols(z)], landing(t, 0), s1_recv.at[t, 0]
                ).start()

            @pl.when(moves)
            def _():
                stage_copy(t, 0).start()

    def await_stage(t, first, last):
        for place in range(first, last):
            pltpu.make_async_copy(
                sources[t].at[:, group_cols(0)], landing(t, place), s1_recv.at[t, place]
            ).wait()

    for half in range(HALVES):
        for t in range(2):
            start_stage(t, half * PER_HALF, (half + 1) * PER_HALF)
    start_stage(2, 0, NZ)

    def slot_of(way, h, n):
        return (h * 2 + way) * MOST_HOPS + n - 1

    def own_hop(way, h, half):
        place = places[way, h]
        target = jnp.maximum(STREAM_ENTRY[way][h], place + 1)
        slot = slot_of(way, h, target - place)
        first = STREAM_START[way][h]
        chip = (first + target) % NY if way == 0 else (first + NY - target) % NY
        return remote(
            own.at[half, :, :, pl.ds(h * HD, HD)],
            ring.at[slot, half],
            own_send.at[half, slot_of(way, h, 1)],
            ring_recv.at[half, slot],
            s,
            ring_seq(chip),
        )

    def hop(way, h, half, n):
        slot = slot_of(way, h, n)
        return remote(
            ring.at[slot, half],
            ring.at[slot + 1, half],
            ring_send.at[half, slot],
            ring_recv.at[half, slot + 1],
            s,
            ring_seq((y + steps[way]) % NY),
        )

    def arrived(way, h, half, n):
        slot = slot_of(way, h, n)
        return pltpu.make_async_copy(
            ring.at[slot, half], ring.at[slot, half], ring_recv.at[half, slot]
        )

    def own_across(half):
        return remote(
            own.at[half], beside.at[half], beside_send.at[half], beside_recv.at[half], sibling, g
        )

    def across(way, h, half, n):
        slot = slot_of(way, h, n)
        return remote(
            ring.at[slot, half],
            cross.at[slot, half],
            cross_send.at[half, slot],
            cross_recv.at[half, slot],
            sibling,
            g,
        )

    def start_streams(half):
        for t in range(2):
            await_stage(t, half * PER_HALF, (half + 1) * PER_HALF)
        for way, h in STREAMS:

            @pl.when(sends_own(way, h))
            def _(way=way, h=h):
                own_hop(way, h, half).start()

        own_across(half).start()

    def pass_on(half, step):
        for way, h in STREAMS:
            hops = STREAM_HOPS[way][h]
            for n in range(step, hops + 1):

                @pl.when(jnp.logical_and(takes(way, h, n), step_of(way, h, n) == step))
                def _(way=way, h=h, n=n):
                    arrived(way, h, half, n).wait()

                    if n < hops:

                        @pl.when(passes(way, h))
                        def _():
                            hop(way, h, half, n).start()

                    across(way, h, half, n).start()

    def for_crossed(half, one):
        for way, h in STREAMS:
            for n in range(1, STREAM_HOPS[way][h] + 1):

                @pl.when(takes(way, h, n))
                def _(way=way, h=h, n=n):
                    one(across(way, h, half, n))

    start_streams(0)
    for step in range(1, MOST_STEPS + 1):
        pass_on(0, step)
        if step == 2:
            start_streams(1)
    pass_on(1, 1)
    await_stage(2, 0, NZ)

    def query_copy(j):
        return remote(
            q_own.at[:, pl.ds(j * HD, HD)],
            qb.at[query_slot[j]],
            q_send.at[j],
            q_recv.at[query_slot[j]],
            s,
            ring_seq(query_chip[j]),
        )

    for j in range(HG):

        @pl.when(query_chip[j] != y)
        def _(j=j):
            query_copy(j).start()

        @pl.when(query_chip[j] == y)
        def _(j=j):
            pltpu.make_async_copy(
                q_own.at[:, pl.ds(j * HD, HD)], qb.at[query_slot[j]], q_recv.at[query_slot[j]]
            ).start()

    for step in range(2, MOST_STEPS + 1):
        pass_on(1, step)
    for i in range(HG):
        pltpu.make_async_copy(q_own.at[:, pl.ds(0, HD)], qb.at[i], q_recv.at[i]).wait()
    for half in range(HALVES):
        own_across(half).wait_recv()
        for_crossed(half, lambda copy: copy.wait_recv())
    for t in range(3):

        @pl.when(moves)
        def _(t=t):
            stage_copy(t, 0).wait_send()

        for place in range(1, NZ):
            stage_copy(t, place).wait_send()
    for j in range(HG):

        @pl.when(query_chip[j] != y)
        def _(j=j):
            query_copy(j).wait_send()

    for half in range(HALVES):
        own_across(half).wait_send()
        for way, h in STREAMS:

            @pl.when(sends_own(way, h))
            def _(way=way, h=h, half=half):
                own_hop(way, h, half).wait_send()

            for n in range(1, STREAM_HOPS[way][h]):

                @pl.when(jnp.logical_and(takes(way, h, n), passes(way, h)))
                def _(way=way, h=h, half=half, n=n):
                    hop(way, h, half, n).wait_send()

        for_crossed(half, lambda copy: copy.wait_send())


def attention_kernel(qb, own, beside, ring, cross, ob, peak, total, acc):
    y = (lax.axis_index("seq") // 2) % NY
    item_head = [pick([ITEMS[k][i][0] for k in range(NY)], y) for i in range(HG)]

    def head_cols(h):
        return pl.ds(pl.multiple_of(h * HD, HD), HD)

    def attend(blocks_of, first):
        for i in range(HG):
            q = qb[i]
            blocks = blocks_of(i)
            scores = [
                lax.dot_general(
                    q, k_block(), (((1,), (1,)), ((), ())), preferred_element_type=F32
                )
                for k_block, _ in blocks
            ]
            top = functools.reduce(jnp.maximum, scores)
            top = jnp.max(top, axis=1, keepdims=True)
            top = jnp.broadcast_to(top, (NBLK, HD))
            if not first:
                old = peak[i]
                top = jnp.maximum(old, top)
            peak[i] = top
            wide = jnp.concatenate([top, top], axis=1)
            part = None
            mixed = None
            for (_, v_block), score in zip(blocks, scores):
                weights = jnp.exp2((score - wide) * EXP2_SCALE)
                halves = weights[:, :HD] + weights[:, HD:]
                part = halves if part is None else part + halves
                term = jnp.dot(weights.astype(BF16), v_block(), preferred_element_type=F32)
                mixed = term if mixed is None else mixed + term
            if first:
                total[i] = part
                acc[i] = mixed
            else:
                fade = jnp.exp2((old - top) * EXP2_SCALE)
                total[i] = total[i] * fade + part
                acc[i] = acc[i] * fade + mixed

    def joined(one, other):
        return lambda: jnp.concatenate([one(), other()], axis=0)

    def blocks_of(half, with_own, arrivals):
        def of(i):
            out = []
            if with_own:
                lanes = head_cols(item_head[i])
                out.append(
                    tuple(
                        joined(
                            lambda t=t: own[half, t, :, lanes], lambda t=t: beside[half, t, :, lanes]
                        )
                        for t in range(2)
                    )
                )
            for k in arrivals:
                slot = pick(ORDER[i][k], y)
                out.append(
                    tuple(
                        joined(
                            lambda t=t, slot=slot: ring[slot, half, t],
                            lambda t=t, slot=slot: cross[slot, half, t],
                        )
                        for t in range(2)
                    )
                )
            return out

        return of

    attend(blocks_of(0, True, (0, 1, 2)), True)
    attend(blocks_of(0, False, (3, 4, 5, 6)), False)
    attend(blocks_of(1, True, (0, 1, 2)), False)
    attend(blocks_of(1, False, (3, 4, 5, 6)), False)
    for i in range(HG):
        ob[i] = (acc[i] / jnp.sum(total[i], axis=1, keepdims=True)).astype(BF16)


def return_kernel(
    ob,
    res_hbm,
    shift_ref,
    scale_ref,
    gate_ref,
    fw_ref,
    fb_ref,
    near_tiles,
    att,
    pat,
    tiles,
    res_ref,
    load_sem,
    o_send,
    o_recv,
    sec_send,
    sec_recv,
    halo_send,
    halo_recv,
):
    s, g, core, xl, z, y, xh = position()
    stays = core == xh
    moves = jnp.logical_not(stays)
    swap_sec = xl * 2 + xh

    def swap_seq(zp, yp):
        return (zp * NY + yp) * 2 + core

    def ring_seq(yp):
        return (z * NY + yp) * 2 + xh

    col = y * 2 + xh
    last_col = 2 * NY - 1

    item_head = [pick([ITEMS[k][i][0] for k in range(NY)], y) for i in range(HG)]
    item_y = [pick([ITEMS[k][i][1] for k in range(NY)], y) for i in range(HG)]
    homes = {item: (k, i) for k in range(NY) for i, item in enumerate(ITEMS[k])}
    query_chip = [pick([homes[j, k][0] for k in range(NY)], y) for j in range(HG)]
    query_slot = [pick([homes[j, k][1] for k in range(NY)], y) for j in range(HG)]
    def there(dy, dx):
        row_ok = z + dy >= 0 if dy < 0 else z + dy < NZ
        col_ok = col + dx >= 0 if dx < 0 else col + dx <= last_col
        return jnp.logical_and(row_ok, col_ok)

    neighbours = [(dy, dx) for dy, dx in AROUND if (dy, dx) != (0, 0)]

    load = pltpu.make_async_copy(res_hbm, res_ref, load_sem)
    load.start()

    barrier = pltpu.get_barrier_semaphore()
    for j in range(HG):
        here = jnp.logical_and(stays, query_chip[j] == y)
        for e in NEAREST[1:]:
            signal(barrier, swap_sec, swap_seq((z + e) % NZ, query_chip[j]))

        @pl.when(jnp.logical_not(here))
        def _(j=j):
            signal(barrier, swap_sec, swap_seq(z, query_chip[j]))

    for ds in range(1, 4):
        signal(barrier, (s + ds) % 4, g)
    for dy, dx in neighbours:

        @pl.when(there(dy, dx))
        def _(dy=dy, dx=dx):
            signal(barrier, s, g + dy * 2 * NY + dx)

    n_rows = 3 - jnp.where(z == 0, 1, 0) - jnp.where(z == NZ - 1, 1, 0)
    n_cols = 3 - jnp.where(col == 0, 1, 0) - jnp.where(col == last_col, 1, 0)
    at_home = pick([sum(item[1] == k for item in ITEMS[k]) for k in range(NY)], y)
    pl.semaphore_wait(
        barrier, HG * NZ + 2 - jnp.where(stays, at_home, 0) + n_rows * n_cols
    )

    def group_cols(zp):
        return pl.ds(pl.multiple_of(zp * GW, HD), GW)

    def head_cols(h):
        return pl.ds(pl.multiple_of(h * HD, HD), HD)

    def block_rows(place):
        return pl.ds(place * TOK, TOK)

    def back_copy(i, place):
        zp = (z + NEAREST[place]) % NZ
        return remote(
            ob.at[i, block_rows(place), :],
            att.at[:, head_cols(z * HG + item_head[i])],
            o_send.at[i, place],
            o_recv.at[item_head[i], place],
            swap_sec,
            swap_seq(zp, item_y[i]),
        )

    for i in range(HG):
        for place in range(NZ - 1, 0, -1):
            back_copy(i, place).start()
        here = jnp.logical_and(stays, item_y[i] == y)

        @pl.when(jnp.logical_not(here))
        def _(i=i):
            back_copy(i, 0).start()

        @pl.when(here)
        def _(i=i):
            pltpu.make_async_copy(
                ob.at[i, block_rows(0), :],
                att.at[:, head_cols(z * HG + item_head[i])],
                o_recv.at[item_head[i], 0],
            ).start()

    load.wait()
    for place in range(NZ):
        zp = (z + NZ - NEAREST[place]) % NZ
        for h in range(HG):
            pltpu.make_async_copy(
                ob.at[0, block_rows(0), :], att.at[:, head_cols(zp * HG + h)], o_recv.at[h, place]
            ).wait()

    hidden = res_ref[...].astype(F32) + gate_ref[...] * att[...].astype(F32)
    center = hidden - jnp.mean(hidden, axis=1, keepdims=True)
    normed = center * lax.rsqrt(jnp.mean(center * center, axis=1, keepdims=True) + norm_eps)
    modulated = (normed * (1.0 + scale_ref[...]) + shift_ref[...]).astype(BF16)
    patches = (
        lax.dot_general(
            modulated, fw_ref[...], (((1,), (1,)), ((), ())), preferred_element_type=F32
        )
        + fb_ref[...]
    ) / scaling
    pat[...] = patches.astype(BF16).astype(F32)
    even = pat[pl.ds(0, F, stride=2), :]
    odd = pat[pl.ds(1, F, stride=2), :]
    side = 2 * LATC
    tile = jnp.concatenate([even[:, :side], odd[:, :side], even[:, side:], odd[:, side:]], axis=1)
    tiles[0, 0:1, :] = tile[:1]
    tiles[0, 1:2, :] = tile[:1]
    tiles[0, 2:8, :] = tile[:6]
    for part in (1, 2):
        tiles[part] = tile[4 * part - 2 : 4 * part + 6]
    tiles[3, 0:6, :] = tile[10:16]
    tiles[3, 6:8, :] = tile[14:16]

    def frames_copy(ds):
        sp = (s + ds) % 4
        return remote(
            tiles.at[sp], near_tiles.at[4, s], sec_send.at[ds], sec_recv.at[4 - ds], sp, g
        )

    for ds in range(1, 4):
        frames_copy(ds).start()
    near_tiles[4, s] = tiles[s]

    def halo_copy(dy, dx):
        place = (1 - dy) * 3 + 1 - dx
        return remote(
            near_tiles.at[4],
            near_tiles.at[place],
            halo_send.at[place],
            halo_recv.at[place],
            s,
            g + dy * 2 * NY + dx,
        )

    for dy, dx in neighbours:

        @pl.when(jnp.logical_not(there(dy, dx)))
        def _(dy=dy, dx=dx):
            near_tiles[(1 + dy) * 3 + 1 + dx] = jnp.zeros((4, 8, 128), F32)

    for ds in range(1, 4):
        pltpu.make_async_copy(
            tiles.at[0], near_tiles.at[4, (s + ds) % 4], sec_recv.at[ds]
        ).wait()
    for dy, dx in neighbours:

        @pl.when(there(dy, dx))
        def _(dy=dy, dx=dx):
            halo_copy(dy, dx).start()

    for i in range(HG):
        for place in range(1, NZ):
            back_copy(i, place).wait_send()

        @pl.when(jnp.logical_not(jnp.logical_and(stays, item_y[i] == y)))
        def _(i=i):
            back_copy(i, 0).wait_send()

    for ds in range(1, 4):
        frames_copy(ds).wait_send()

    for dy, dx in neighbours:

        @pl.when(there(dy, dx))
        def _(dy=dy, dx=dx):
            place = (1 + dy) * 3 + 1 + dx
            pltpu.make_async_copy(
                near_tiles.at[4], near_tiles.at[place], halo_recv.at[place]
            ).wait()

    for dy, dx in neighbours:

        @pl.when(there(dy, dx))
        def _(dy=dy, dx=dx):
            halo_copy(dy, dx).wait_send()


def conv_kernel(near_tiles, cw_hbm, cb_ref, gg_ref, gb_ref, out_ref, windows, cw_ref, cw_sem):
    loads = [
        pltpu.make_async_copy(
            cw_hbm.at[pl.ds(tap * 48, 48), :], cw_ref.at[tap, pl.ds(0, 48), :], cw_sem.at[tap]
        )
        for tap in range(9)
    ]
    for load in loads:
        load.start()
    cw_ref[:, 48:, :] = jnp.zeros((9, 80, cw_ref.shape[2]), BF16)
    for yy in range(4):
        vert, dr = ((0, 1), (1, 0), (1, 1), (2, 0))[yy]
        lo = dr * BC * LATC
        hi = lo + BC * LATC
        sides = [near_tiles[vert * 3 + dx].reshape(32, 128) for dx in range(3)]
        strip = jnp.concatenate(
            [
                sides[0][:, hi - LATC : hi],
                sides[1][:, lo:hi],
                sides[2][:, lo : lo + LATC],
                jnp.zeros((32, 2 * LATC), F32),
            ],
            axis=1,
        )
        for x in range(BC):
            moved = strip if x == 0 else pltpu.roll(strip, 128 - x * LATC, axis=1)
            moved = moved.reshape(4, 8, 128)
            for dt in range(3):
                piece = moved[:, dt : dt + 4, :].reshape(16, 128)
                for dy in range(3):
                    row = yy - dy
                    if 0 <= row < BR:
                        windows[dt * 3 + dy, pl.ds(row * BC + x, 16, stride=8), :] = piece
    for load in loads:
        load.wait()
    left_side = jnp.concatenate([windows[tap].astype(BF16) for tap in range(9)], axis=1)
    conv = jnp.dot(
        left_side, cw_ref[...].reshape(9 * 128, cw_ref.shape[2]), preferred_element_type=F32
    )
    conv = (conv + cb_ref[...]) * gg_ref[...] + gb_ref[...]
    out_ref[...] = (conv / (1.0 + jnp.exp(-conv))).astype(BF16)


def on_device(
    queries,
    keys,
    values,
    residual,
    shift_mod,
    scale_mod,
    gate_mod,
    final_weight,
    final_bias,
    conv_weight,
    conv_bias,
    group_gain,
    group_bias,
):
    any_spec = pl.BlockSpec(memory_space=pl.ANY)
    dma = pltpu.SemaphoreType.DMA
    vae_width = conv_weight.shape[1]
    slots = 2 * HG * MOST_HOPS
    vmem = pl.BlockSpec(memory_space=pltpu.VMEM)
    limit = 30 * 1024 * 1024
    q_items, own, beside, ring, cross = pl.pallas_call(
        gather_kernel,
        out_shape=[
            jax.ShapeDtypeStruct((HG, NBLK, HD), BF16),
            jax.ShapeDtypeStruct((HALVES, 2, HALF, GW), BF16),
            jax.ShapeDtypeStruct((HALVES, 2, HALF, GW), BF16),
            jax.ShapeDtypeStruct((slots, HALVES, 2, HALF, HD), BF16),
            jax.ShapeDtypeStruct((slots, HALVES, 2, HALF, HD), BF16),
        ],
        in_specs=[any_spec] * 3,
        out_specs=[vmem] * 5,
        scratch_shapes=[
            pltpu.VMEM((NBLK, GW), BF16),
            dma((3, NZ)),
            dma((3, NZ)),
            dma((HG,)),
            dma((HG,)),
            dma((HALVES, slots)),
            dma((HALVES, slots)),
            dma((HALVES, slots)),
            dma((HALVES,)),
            dma((HALVES,)),
            dma((HALVES, slots)),
            dma((HALVES, slots)),
        ],
        compiler_params=pltpu.CompilerParams(
            collective_id=0, has_side_effects=True, vmem_limit_bytes=limit
        ),
        name="gather",
    )(queries[0], keys[0], values[0])
    mixed = pl.pallas_call(
        attention_kernel,
        out_shape=jax.ShapeDtypeStruct((HG, NBLK, HD), BF16),
        in_specs=[vmem] * 5,
        out_specs=vmem,
        scratch_shapes=[
            pltpu.VMEM((HG, NBLK, HD), F32),
            pltpu.VMEM((HG, NBLK, HD), F32),
            pltpu.VMEM((HG, NBLK, HD), F32),
        ],
        compiler_params=pltpu.CompilerParams(vmem_limit_bytes=limit),
        name="attention",
    )(q_items, own, beside, ring, cross)
    near_tiles = pl.pallas_call(
        return_kernel,
        out_shape=jax.ShapeDtypeStruct((9, 4, 8, 128), F32),
        in_specs=[vmem, any_spec] + [vmem] * 5,
        out_specs=vmem,
        scratch_shapes=[
            pltpu.VMEM((TOK, H * HD), BF16),
            pltpu.VMEM((TOK, 4 * LATC), F32),
            pltpu.VMEM((4, 8, 128), F32),
            pltpu.VMEM((TOK, H * HD), BF16),
            dma(()),
            dma((HG, NZ)),
            dma((HG, NZ)),
            dma((4,)),
            dma((4,)),
            dma((9,)),
            dma((9,)),
        ],
        compiler_params=pltpu.CompilerParams(
            collective_id=1, has_side_effects=True, vmem_limit_bytes=limit
        ),
        name="return",
    )(
        mixed,
        residual[0],
        shift_mod,
        scale_mod,
        gate_mod,
        final_weight.T,
        final_bias[None],
    )
    features = pl.pallas_call(
        conv_kernel,
        out_shape=jax.ShapeDtypeStruct((4 * 4 * BR * BC, vae_width), BF16),
        in_specs=[vmem, any_spec, vmem, vmem, vmem],
        out_specs=vmem,
        scratch_shapes=[
            pltpu.VMEM((9, 4 * 4 * BR * BC, 128), F32),
            pltpu.VMEM((9, 128, vae_width), BF16),
            dma((9,)),
        ],
        compiler_params=pltpu.CompilerParams(vmem_limit_bytes=limit),
        name="convolution",
    )(near_tiles, conv_weight, conv_bias[None], group_gain[None], group_bias[None])
    return features.reshape(4, 4, 1, BR * BC, vae_width)


def solution(mesh):
    return jax.shard_map(
        on_device,
        mesh=mesh,
        in_specs=(
            P("sec", "seq", None),
            P("sec", "seq", None),
            P("sec", "seq", None),
            P("sec", "seq", None),
            P("sec", None),
            P("sec", None),
            P("sec", None),
            P(),
            P(),
            P(),
            P(),
            P(),
            P(),
        ),
        out_specs=P(None, "sec", "seq", None, None),
        check_vma=False,
    )
```

```python
import functools

import jax
import jax.numpy as jnp
from jax import lax
from jax.experimental import pallas as pl
from jax.experimental.pallas import tpu as pltpu
from jax.sharding import PartitionSpec as P

H = 24
HD = 128
LATC = 16
F = 16
BR = 2
BC = 4
NZ = 8
NY = 8
TOK = 32
HG = 3
GW = HG * HD
NBLK = NZ * TOK

scaling = 0.476986
norm_eps = 1e-06
EXP2_SCALE = HD ** (-0.5) * 1.4426950408889634
F32 = jnp.float32
BF16 = jnp.bfloat16


def remote(src, dst, send_sem, recv_sem, sec, seq):
    return pltpu.make_async_remote_copy(
        src_ref=src,
        dst_ref=dst,
        send_sem=send_sem,
        recv_sem=recv_sem,
        device_id={"sec": sec, "seq": seq},
        device_id_type=pl.DeviceIdType.MESH,
    )


def signal(sem, sec, seq):
    pl.semaphore_signal(
        sem, inc=1, device_id={"sec": sec, "seq": seq}, device_id_type=pl.DeviceIdType.MESH
    )


def position():
    s = lax.axis_index("sec")
    g = lax.axis_index("seq")
    return s, g, s % 2, s // 2, g // (2 * NY), (g // 2) % NY, g % 2

NEAREST = (0, 1, 7, 2, 6, 3, 5, 4)
AROUND = [(dy, dx) for dy in (-1, 0, 1) for dx in (-1, 0, 1)]

HALVES = 2
PER_HALF = NZ // HALVES
HALF = NBLK // HALVES


def whole_kernel(
    q_ref,
    k_ref,
    v_ref,
    res_hbm,
    shift_hbm,
    scale_hbm,
    gate_hbm,
    fw_hbm,
    fb_hbm,
    cw_hbm,
    cb_hbm,
    gg_hbm,
    gb_hbm,
    out_ref,
    qb,
    kb,
    vb,
    ob,
    att,
    peak,
    total,
    acc,
    pat,
    tiles,
    near_tiles,
    windows,
    res_ref,
    shift_ref,
    scale_ref,
    gate_ref,
    fw_ref,
    fb_ref,
    cw_ref,
    cb_ref,
    gg_ref,
    gb_ref,
    load_sem,
    cw_sem,
    s1_send,
    s1_recv,
    ring_send,
    ring_recv,
    last_recv,
    cross_send,
    cross_recv,
    o_send,
    o_recv,
    halo_send,
    halo_recv,
):
    s, g, core, xl, z, y, xh = position()
    stays = core == xh
    moves = jnp.logical_not(stays)
    swap_sec = xl * 2 + xh
    sibling = xl * 2 + 1 - core
    col = y * 2 + xh

    def swap_seq(zp, yp):
        return (zp * NY + yp) * 2 + core

    def ring_seq(yp):
        return (z * NY + yp) * 2 + xh

    right = ring_seq((y + 1) % NY)
    left = ring_seq((y + NY - 1) % NY)

    neighbours = [(dy, dx) for dy, dx in AROUND if (dy, dx) != (0, 0)]

    def tile_seq(dy, dx):
        return (z + NZ + dy) % NZ * (2 * NY) + (col + 2 * NY + dx) % (2 * NY)

    barrier = pltpu.get_barrier_semaphore()
    for e in NEAREST[1:]:
        signal(barrier, swap_sec, swap_seq((z + e) % NZ, y))

    @pl.when(moves)
    def _():
        signal(barrier, swap_sec, swap_seq(z, y))

    signal(barrier, s, right)
    signal(barrier, s, left)
    for ds in range(1, 4):
        signal(barrier, (s + ds) % 4, g)
    for dy, dx in neighbours:
        signal(barrier, s, tile_seq(dy, dx))

    def group_cols(zp):
        return pl.ds(pl.multiple_of(zp * GW, HD), GW)

    def head_cols(h):
        return pl.ds(pl.multiple_of(h * HD, HD), HD)

    def block_rows(place):
        return pl.ds(place * TOK, TOK)

    def await_bytes(ref, sem):
        pltpu.make_async_copy(ref, ref, sem).wait()

    stage_one = ((k_ref, kb.at[0]), (v_ref, vb.at[0]), (q_ref, qb))

    def stage_sem(t, place):
        return s1_recv.at[t, 0 if t == 2 else place // PER_HALF]

    def stage_copy(t, place):
        src, buf = stage_one[t]
        zp = (z + NZ - NEAREST[place]) % NZ
        return remote(
            src.at[:, group_cols(zp)],
            buf.at[block_rows(place), :],
            s1_send.at[t],
            stage_sem(t, place),
            swap_sec,
            swap_seq(zp, y),
        )

    def start_stage(t):
        src, buf = stage_one[t]

        @pl.when(stays)
        def _():
            pltpu.make_async_copy(
                src.at[:, group_cols(z)], buf.at[block_rows(0), :], stage_sem(t, 0)
            ).start()

        @pl.when(moves)
        def _():
            stage_copy(t, 0).start()

        for place in range(1, NZ):
            stage_copy(t, place).start()

    pl.semaphore_wait(barrier, 2 * NZ + 5 - jnp.where(stays, 1, 0))
    for t in range(3):
        start_stage(t)

    loads = [
        pltpu.make_async_copy(src, dst, load_sem.at[i])
        for i, (src, dst) in enumerate(
            (
                (res_hbm, res_ref),
                (shift_hbm, shift_ref),
                (scale_hbm, scale_ref),
                (gate_hbm, gate_ref),
                (fw_hbm, fw_ref),
                (fb_hbm, fb_ref),
                (cb_hbm, cb_ref),
                (gg_hbm, gg_ref),
                (gb_hbm, gb_ref),
            )
        )
    ]
    for load in loads:
        load.start()
    for tap in range(9):
        pltpu.make_async_copy(
            cw_hbm.at[pl.ds(tap * 48, 48), :], cw_ref.at[tap, pl.ds(0, 48), :], cw_sem
        ).start()

    bufs = (kb, vb)

    def slot_of(way, hops):
        if hops in (0, 4):
            return hops
        return hops if way == 0 else 4 + hops

    def half_of(t, slot, half):
        return bufs[t].at[slot, pl.ds(half * HALF, HALF), :]

    def head_of(t, slot, h):
        return bufs[t].at[slot, :, pl.ds(h * HD, HD)]

    def hop(way, t, half, hops):
        return remote(
            half_of(t, slot_of(way, hops - 1), half),
            half_of(t, slot_of(way, hops), half),
            ring_send.at[way],
            ring_recv.at[way, t, half, hops],
            s,
            (right, left)[way],
        )

    def last_hop(t, h):
        return remote(
            head_of(t, slot_of(t, 3), h),
            head_of(t, 4, h),
            ring_send.at[t],
            last_recv.at[t, h],
            s,
            (right, left)[t],
        )

    def across(piece, beside, step):
        remote(piece, beside, cross_send, cross_recv.at[step], sibling, g).start()

    def half_across(t, slot, half, step):
        across(half_of(t, slot, half), half_of(t, 8 + slot, half), step)

    def attend(h, slots, first):
        lanes = slice(h * HD, (h + 1) * HD)
        q = qb[:, lanes]
        scores = [
            lax.dot_general(
                q, kb[slot, :, lanes], (((1,), (1,)), ((), ())), preferred_element_type=F32
            )
            for slot in slots
        ]
        top = functools.reduce(jnp.maximum, scores)
        top = jnp.max(top, axis=1, keepdims=True)
        top = jnp.broadcast_to(top, (NBLK, HD))
        if not first:
            old = peak[h]
            top = jnp.maximum(old, top)
        peak[h] = top
        wide = jnp.concatenate([top, top], axis=1)
        part = None
        mixed = None
        for slot, score in zip(slots, scores):
            weights = jnp.exp2((score - wide) * EXP2_SCALE)
            halves = weights[:, :HD] + weights[:, HD:]
            part = halves if part is None else part + halves
            term = jnp.dot(weights.astype(BF16), vb[slot, :, lanes], preferred_element_type=F32)
            mixed = term if mixed is None else mixed + term
        if first:
            total[h] = part
            acc[h] = mixed
        else:
            fade = jnp.exp2((old - top) * EXP2_SCALE)
            total[h] = total[h] * fade + part
            acc[h] = acc[h] * fade + mixed

    pieces = [(t, half) for t in range(2) for half in range(HALVES)]
    for t, half in pieces:
        await_bytes(half_of(t, 0, half), s1_recv.at[t, half])
        hop(0, t, half, 1).start()
        hop(1, t, half, 1).start()
        half_across(t, 0, half, 0)
    cw_ref[:, 48:, :] = jnp.zeros((9, 80, cw_ref.shape[2]), BF16)
    for n in range(1, 4):
        for t, half in pieces:
            for way in range(2):
                hop(way, t, half, n).wait_recv()
                if n < 3:
                    hop(way, t, half, n + 1).start()
                elif way == t and half == HALVES - 1:
                    for h in range(HG):
                        last_hop(t, h).start()
                half_across(t, slot_of(way, n), half, n)
        if n == 1:
            await_bytes(qb, s1_recv.at[2, 0])
            await_bytes(kb.at[pl.ds(8, 2)], cross_recv.at[0])
            for h in range(HG):
                attend(h, (0, 8), True)
        await_bytes(kb.at[pl.ds(8, 4)], cross_recv.at[n])
        for h in range(HG):
            attend(h, (n, 4 + n, 8 + n, 12 + n), False)
    for h in range(HG):
        for t in range(2):
            last_hop(t, h).wait_recv()
            across(head_of(t, 4, h), head_of(t, 12, h), 4 + h)

    def back_copy(h, place):
        zp = (z + NEAREST[place]) % NZ
        return remote(
            ob.at[h, block_rows(place), :],
            att.at[:, head_cols(z * HG + h)],
            o_send.at[h],
            o_recv,
            swap_sec,
            swap_seq(zp, y),
        )

    for h in range(HG):
        await_bytes(kb.at[pl.ds(8, 2), :, pl.ds(0, HD)], cross_recv.at[4 + h])
        attend(h, (4, 12), False)
        ob[h] = (acc[h] / jnp.sum(total[h], axis=1, keepdims=True)).astype(BF16)
        for place in range(NZ - 1, 0, -1):
            back_copy(h, place).start()

        @pl.when(moves)
        def _(h=h):
            back_copy(h, 0).start()

        @pl.when(stays)
        def _(h=h):
            pltpu.make_async_copy(
                ob.at[h, block_rows(0), :], att.at[:, head_cols(z * HG + h)], o_recv
            ).start()

    def sent_blocks(ref, sem):
        @pl.when(moves)
        def _():
            await_bytes(ref, sem)

        @pl.when(stays)
        def _():
            await_bytes(ref.at[pl.ds(0, NBLK - TOK), :], sem)

    for t in range(3):
        sent_blocks(qb, s1_send.at[t])
    for way in range(2):
        await_bytes(kb.at[pl.ds(0, 7)], ring_send.at[way])
    await_bytes(kb, cross_send)
    for load in loads:
        load.wait()
    await_bytes(att, o_recv)

    hidden = res_ref[...].astype(F32) + gate_ref[...] * att[...].astype(F32)
    center = hidden - jnp.mean(hidden, axis=1, keepdims=True)
    normed = center * lax.rsqrt(jnp.mean(center * center, axis=1, keepdims=True) + norm_eps)
    modulated = (normed * (1.0 + scale_ref[...]) + shift_ref[...]).astype(BF16)
    patches = (
        lax.dot_general(
            modulated, fw_ref[...], (((1,), (1,)), ((), ())), preferred_element_type=F32
        )
        + fb_ref[...]
    ) / scaling
    pat[...] = patches.astype(BF16).astype(F32)
    even = pat[pl.ds(0, F, stride=2), :]
    odd = pat[pl.ds(1, F, stride=2), :]
    side = 2 * LATC
    tile = jnp.concatenate([even[:, :side], odd[:, :side], even[:, side:], odd[:, side:]], axis=1)
    tiles[0, 0:1, :] = tile[:1]
    tiles[0, 1:2, :] = tile[:1]
    tiles[0, 2:8, :] = tile[:6]
    for part in (1, 2):
        tiles[part] = tile[4 * part - 2 : 4 * part + 6]
    tiles[3, 0:6, :] = tile[10:16]
    tiles[3, 6:8, :] = tile[14:16]

    for ds in range(1, 4):
        sp = (s + ds) % 4
        remote(
            tiles.at[sp], near_tiles.at[4, s], halo_send.at[0], halo_recv.at[0], sp, g
        ).start()
    near_tiles[4, s] = tiles[s]
    for h in range(HG):
        sent_blocks(ob.at[h], o_send.at[h])
    await_bytes(tiles.at[pl.ds(0, 3)], halo_recv.at[0])
    for dy, dx in neighbours:
        remote(
            near_tiles.at[4],
            near_tiles.at[(1 - dy) * 3 + 1 - dx],
            halo_send.at[1],
            halo_recv.at[1],
            s,
            tile_seq(dy, dx),
        ).start()
    await_bytes(tiles.at[pl.ds(0, 3)], halo_send.at[0])
    await_bytes(near_tiles.at[pl.ds(0, 8)], halo_recv.at[1])

    def clear(at_edge, gone):
        @pl.when(at_edge)
        def _():
            for place in gone:
                near_tiles[place] = jnp.zeros((4, 8, 128), F32)

    clear(z == 0, (0, 1, 2))
    clear(z == NZ - 1, (6, 7, 8))
    clear(col == 0, (0, 3, 6))
    clear(col == 2 * NY - 1, (2, 5, 8))

    for yy in range(4):
        vert, dr = ((0, 1), (1, 0), (1, 1), (2, 0))[yy]
        lo = dr * BC * LATC
        hi = lo + BC * LATC
        sides = [near_tiles[vert * 3 + dx].reshape(32, 128) for dx in range(3)]
        strip = jnp.concatenate(
            [
                sides[0][:, hi - LATC : hi],
                sides[1][:, lo:hi],
                sides[2][:, lo : lo + LATC],
                jnp.zeros((32, 2 * LATC), F32),
            ],
            axis=1,
        )
        for x in range(BC):
            moved = strip if x == 0 else pltpu.roll(strip, 128 - x * LATC, axis=1)
            moved = moved.reshape(4, 8, 128)
            for dt in range(3):
                piece = moved[:, dt : dt + 4, :].reshape(16, 128)
                for dy in range(3):
                    row = yy - dy
                    if 0 <= row < BR:
                        windows[dt * 3 + dy, pl.ds(row * BC + x, 16, stride=8), :] = piece
    await_bytes(cw_ref.at[:, pl.ds(0, 48), :], cw_sem)
    left_side = jnp.concatenate([windows[tap].astype(BF16) for tap in range(9)], axis=1)
    conv = jnp.dot(
        left_side, cw_ref[...].reshape(9 * 128, cw_ref.shape[2]), preferred_element_type=F32
    )
    conv = (conv + cb_ref[...]) * gg_ref[...] + gb_ref[...]
    out_ref[...] = (conv / (1.0 + jnp.exp(-conv))).astype(BF16)

    await_bytes(near_tiles.at[pl.ds(0, 8)], halo_send.at[1])


def on_device(
    queries,
    keys,
    values,
    residual,
    shift_mod,
    scale_mod,
    gate_mod,
    final_weight,
    final_bias,
    conv_weight,
    conv_bias,
    group_gain,
    group_bias,
):
    any_spec = pl.BlockSpec(memory_space=pl.ANY)
    dma = pltpu.SemaphoreType.DMA
    vae_width = conv_weight.shape[1]
    features = pl.pallas_call(
        whole_kernel,
        out_shape=jax.ShapeDtypeStruct((4 * 4 * BR * BC, vae_width), BF16),
        in_specs=[any_spec] * 13,
        out_specs=pl.BlockSpec(memory_space=pltpu.VMEM),
        scratch_shapes=[
            pltpu.VMEM((NBLK, GW), BF16),
            pltpu.VMEM((16, NBLK, GW), BF16),
            pltpu.VMEM((16, NBLK, GW), BF16),
            pltpu.VMEM((HG, NBLK, HD), BF16),
            pltpu.VMEM((TOK, H * HD), BF16),
            pltpu.VMEM((HG, NBLK, HD), F32),
            pltpu.VMEM((HG, NBLK, HD), F32),
            pltpu.VMEM((HG, NBLK, HD), F32),
            pltpu.VMEM((TOK, 4 * LATC), F32),
            pltpu.VMEM((4, 8, 128), F32),
            pltpu.VMEM((9, 4, 8, 128), F32),
            pltpu.VMEM((9, 4 * 4 * BR * BC, 128), F32),
            pltpu.VMEM((TOK, H * HD), BF16),
            pltpu.VMEM((1, H * HD), F32),
            pltpu.VMEM((1, H * HD), F32),
            pltpu.VMEM((1, H * HD), F32),
            pltpu.VMEM((4 * LATC, H * HD), BF16),
            pltpu.VMEM((1, 4 * LATC), F32),
            pltpu.VMEM((9, 128, vae_width), BF16),
            pltpu.VMEM((1, vae_width), F32),
            pltpu.VMEM((1, vae_width), F32),
            pltpu.VMEM((1, vae_width), F32),
            dma((9,)),
            dma(()),
            dma((3,)),
            dma((3, HALVES)),
            dma((2,)),
            dma((2, 2, HALVES, 4)),
            dma((2, HG)),
            dma(()),
            dma((4 + HG,)),
            dma((HG,)),
            dma(()),
            dma((2,)),
            dma((2,)),
        ],
        compiler_params=pltpu.CompilerParams(
            collective_id=0, has_side_effects=True, vmem_limit_bytes=60 * 1024 * 1024
        ),
        name="whole",
    )(
        queries[0],
        keys[0],
        values[0],
        residual[0],
        shift_mod,
        scale_mod,
        gate_mod,
        final_weight.T,
        final_bias[None],
        conv_weight,
        conv_bias[None],
        group_gain[None],
        group_bias[None],
    )
    return features.reshape(4, 4, 1, BR * BC, vae_width)


def solution(mesh):
    return jax.shard_map(
        on_device,
        mesh=mesh,
        in_specs=(
            P("sec", "seq", None),
            P("sec", "seq", None),
            P("sec", "seq", None),
            P("sec", "seq", None),
            P("sec", None),
            P("sec", None),
            P("sec", None),
            P(),
            P(),
            P(),
            P(),
            P(),
            P(),
        ),
        out_specs=P(None, "sec", "seq", None, None),
        check_vma=False,
    )
```

```python
import functools

import jax
import jax.numpy as jnp
from jax import lax
from jax.experimental import pallas as pl
from jax.experimental.pallas import tpu as pltpu
from jax.sharding import PartitionSpec as P

H = 24
HD = 128
LATC = 16
F = 16
BR = 2
BC = 4
NZ = 8
NY = 8
TOK = 32
HG = 3
GW = HG * HD
NBLK = NZ * TOK

scaling = 0.476986
norm_eps = 1e-06
EXP2_SCALE = HD ** (-0.5) * 1.4426950408889634
F32 = jnp.float32
BF16 = jnp.bfloat16


def remote(src, dst, send_sem, recv_sem, sec, seq):
    return pltpu.make_async_remote_copy(
        src_ref=src,
        dst_ref=dst,
        send_sem=send_sem,
        recv_sem=recv_sem,
        device_id={"sec": sec, "seq": seq},
        device_id_type=pl.DeviceIdType.MESH,
    )


def signal(sem, sec, seq):
    pl.semaphore_signal(
        sem, inc=1, device_id={"sec": sec, "seq": seq}, device_id_type=pl.DeviceIdType.MESH
    )


def position():
    s = lax.axis_index("sec")
    g = lax.axis_index("seq")
    return s, g, s % 2, s // 2, g // (2 * NY), (g // 2) % NY, g % 2

NEAREST = (0, 1, 7, 2, 6, 3, 5, 4)
AROUND = [(dy, dx) for dy in (-1, 0, 1) for dx in (-1, 0, 1)]

ITEMS = (
    ((0, 0), (0, 7), (0, 6)),
    ((0, 1), (0, 2), (0, 5)),
    ((0, 3), (0, 4), (1, 1)),
    ((1, 2), (1, 3), (1, 0)),
    ((1, 4), (1, 5), (1, 7)),
    ((1, 6), (2, 3), (2, 4)),
    ((2, 5), (2, 6), (2, 2)),
    ((2, 7), (2, 0), (2, 1)),
)
STREAM_START = ((5, 0, 3), (4, 7, 2))
STREAM_HOPS = ((5, 5, 4), (4, 5, 5))
STREAM_ENTRY = ((3, 2, 2), (2, 2, 3))
MOST_HOPS = 5
MOST_STEPS = 4
HALVES = 2
PER_HALF = NZ // HALVES
HALF = NBLK // HALVES
STREAMS = [(way, h) for h in range(HG) for way in range(2)]


def stream_place(way, h, chip):
    first = STREAM_START[way][h]
    return (chip - first) % NY if way == 0 else (first - chip) % NY


def slot_of(way, h, n):
    return (h * 2 + way) * MOST_HOPS + n - 1


def chip_plan(chip):
    own_sends = []
    arrivals = [[] for _ in range(MOST_STEPS + 1)]
    for way, h in STREAMS:
        place = stream_place(way, h, chip)
        entry = STREAM_ENTRY[way][h]
        hops = STREAM_HOPS[way][h]
        if place < hops:
            target = max(entry, place + 1)
            ahead = target - place
            to = (chip + ahead) % NY if way == 0 else (chip - ahead) % NY
            own_sends.append((ahead, h, slot_of(way, h, ahead), to))
        if entry <= place <= hops:
            for n in range(1, place + 1):
                step = min(n, place - entry + 1)
                arrivals[step].append((n, slot_of(way, h, n), place < hops, way))
    own_sends = [item[1:] for item in sorted(own_sends, reverse=True)]
    return own_sends, [[item[1:] for item in sorted(step)] for step in arrivals]


PLANS = [chip_plan(chip) for chip in range(NY)]


def block_order(chip, h):
    slots = [item[0] for step in PLANS[chip][1] for item in step]
    return [slot for slot in slots if slot // (2 * MOST_HOPS) == h]


ORDER = [
    [[block_order(chip, ITEMS[chip][i][0])[k] for chip in range(NY)] for k in range(NY - 1)]
    for i in range(HG)
]


def pick(table, index):
    out = table[0]
    for k in range(1, len(table)):
        out = jnp.where(index == k, table[k], out)
    return out


def whole_kernel(
    q_ref,
    k_ref,
    v_ref,
    res_hbm,
    shift_hbm,
    scale_hbm,
    gate_hbm,
    fw_hbm,
    fb_hbm,
    cw_hbm,
    cb_hbm,
    gg_hbm,
    gb_hbm,
    out_ref,
    q_all,
    k_all,
    v_all,
    kv_pack,
    q_pack,
    kv_land,
    q_land,
    q_own,
    own,
    beside,
    ring,
    cross,
    qb,
    ob,
    att,
    peak,
    total,
    acc,
    pat,
    tiles,
    near_tiles,
    windows,
    res_ref,
    shift_ref,
    scale_ref,
    gate_ref,
    fw_ref,
    fb_ref,
    cw_ref,
    cb_ref,
    gg_ref,
    gb_ref,
    in_sem,
    load_sem,
    cw_sem,
    s1_send,
    s1_recv,
    q_send,
    q_recv,
    ring_send,
    ring_recv,
    beside_send,
    beside_recv,
    cross_send,
    cross_recv,
    o_send,
    o_recv,
    halo_send,
    halo_recv,
):
    s, g, core, xl, z, y, xh = position()
    stays = core == xh
    moves = jnp.logical_not(stays)
    swap_sec = xl * 2 + xh
    sibling = xl * 2 + 1 - core
    col = y * 2 + xh

    def swap_seq(zp, yp):
        return (zp * NY + yp) * 2 + core

    def ring_seq(yp):
        return (z * NY + yp) * 2 + xh

    neighbours = [(dy, dx) for dy, dx in AROUND if (dy, dx) != (0, 0)]

    def tile_seq(dy, dx):
        return (z + NZ + dy) % NZ * (2 * NY) + (col + 2 * NY + dx) % (2 * NY)

    fetches = [
        pltpu.make_async_copy(src, dst, in_sem.at[t])
        for t, (src, dst) in enumerate(((k_ref, k_all), (v_ref, v_all), (q_ref, q_all)))
    ]
    for fetch in fetches:
        fetch.start()

    barrier = pltpu.get_barrier_semaphore()
    for e in NEAREST[1:]:
        signal(barrier, swap_sec, swap_seq((z + e) % NZ, y))

    @pl.when(moves)
    def _():
        signal(barrier, swap_sec, swap_seq(z, y))

    for e in range(1, NY):
        signal(barrier, s, ring_seq((y + e) % NY))
    for ds in range(1, 4):
        signal(barrier, (s + ds) % 4, g)
    for dy, dx in neighbours:
        signal(barrier, s, tile_seq(dy, dx))

    item_head = [pick([ITEMS[k][i][0] for k in range(NY)], y) for i in range(HG)]
    item_y = [pick([ITEMS[k][i][1] for k in range(NY)], y) for i in range(HG)]

    def group_cols(zp):
        return pl.ds(pl.multiple_of(zp * GW, HD), GW)

    def block_rows(place):
        return pl.ds(place * TOK, TOK)

    def await_bytes(ref, sem):
        pltpu.make_async_copy(ref, ref, sem).wait()

    def group_at(place):
        return (z + NZ - NEAREST[place]) % NZ

    for fetch in fetches:
        fetch.wait()
    for place in range(NZ):
        cols = group_cols(group_at(place))
        kv_pack[place, 0] = k_all[:, cols]
        kv_pack[place, 1] = v_all[:, cols]
        q_pack[place] = q_all[:, cols]

    def start_stage(pack, land, send_sem, recv_sem, first, last):
        for place in range(first, last):

            def copy(place=place):
                return remote(
                    pack.at[place],
                    land.at[place],
                    send_sem,
                    recv_sem,
                    swap_sec,
                    swap_seq(group_at(place), y),
                )

            if place > 0:
                copy().start()
                continue

            @pl.when(stays)
            def _():
                pltpu.make_async_copy(pack.at[0], land.at[0], recv_sem).start()

            @pl.when(moves)
            def _():
                copy().start()

    pl.semaphore_wait(barrier, 3 * NZ + 2 - jnp.where(stays, 1, 0))
    for half in range(HALVES):
        start_stage(
            kv_pack,
            kv_land,
            s1_send.at[0],
            s1_recv.at[half],
            half * PER_HALF,
            (half + 1) * PER_HALF,
        )
    start_stage(q_pack, q_land, s1_send.at[1], s1_recv.at[HALVES], 0, NZ)

    loads = [
        pltpu.make_async_copy(src, dst, load_sem.at[i])
        for i, (src, dst) in enumerate(
            (
                (res_hbm, res_ref),
                (shift_hbm, shift_ref),
                (scale_hbm, scale_ref),
                (gate_hbm, gate_ref),
                (fw_hbm, fw_ref),
                (fb_hbm, fb_ref),
                (cb_hbm, cb_ref),
                (gg_hbm, gg_ref),
                (gb_hbm, gb_ref),
            )
        )
    ]
    for load in loads:
        load.start()
    for tap in range(9):
        pltpu.make_async_copy(
            cw_hbm.at[pl.ds(tap * 48, 48), :], cw_ref.at[tap, pl.ds(0, 48), :], cw_sem
        ).start()

    def own_hop(half, h, slot, to):
        return remote(
            own.at[half, h],
            ring.at[slot, half],
            ring_send.at[half],
            ring_recv.at[half, slot],
            s,
            ring_seq(to),
        )

    def hop(half, slot, to):
        return remote(
            ring.at[slot, half],
            ring.at[slot + 1, half],
            ring_send.at[half],
            ring_recv.at[half, slot + 1],
            s,
            ring_seq(to),
        )

    def across(src, dst, send_sem, recv_sem):
        remote(src, dst, send_sem, recv_sem, sibling, g).start()

    def by_chip(one):
        for chip in range(NY):

            @pl.when(y == chip)
            def _(chip=chip):
                one(chip)

    def start_streams(half):
        landed = range(half * PER_HALF, (half + 1) * PER_HALF)
        await_bytes(kv_land.at[pl.ds(half * PER_HALF, PER_HALF)], s1_recv.at[half])
        for place in landed:
            rows = block_rows(place % PER_HALF)
            for t in range(2):
                for h in range(HG):
                    own[half, h, t, rows, :] = kv_land[place, t, :, h * HD : (h + 1) * HD]

        def one(chip):
            for h, slot, to in PLANS[chip][0]:
                own_hop(half, h, slot, to).start()

        by_chip(one)
        across(own.at[half], beside.at[half], beside_send.at[half], beside_recv.at[half])

    def pass_on(half, *steps):
        def one(chip):
            for step in steps:
                for slot, passed, way in PLANS[chip][1][step]:
                    await_bytes(ring.at[slot, half], ring_recv.at[half, slot])
                    if passed:
                        hop(half, slot, (chip + (1, NY - 1)[way]) % NY).start()
                    across(
                        ring.at[slot, half],
                        cross.at[slot, half],
                        cross_send.at[half],
                        cross_recv.at[half],
                    )

        by_chip(one)

    def count_arrivals(chip):
        return sum(len(step) for step in PLANS[chip][1])

    def await_crossed(half, own_sem, sem):
        await_bytes(own.at[half], own_sem.at[half])
        by_chip(lambda chip: await_bytes(cross.at[pl.ds(0, count_arrivals(chip)), half], sem.at[half]))

    def attend(blocks_of, first):
        for i in range(HG):
            q = qb[i]
            blocks = blocks_of(i)
            scores = [
                lax.dot_general(
                    q, k_block(), (((1,), (1,)), ((), ())), preferred_element_type=F32
                )
                for k_block, _ in blocks
            ]
            top = functools.reduce(jnp.maximum, scores)
            top = jnp.max(top, axis=1, keepdims=True)
            top = jnp.broadcast_to(top, (NBLK, HD))
            if not first:
                old = peak[i]
                top = jnp.maximum(old, top)
            peak[i] = top
            wide = jnp.concatenate([top, top], axis=1)
            part = None
            mixed = None
            for (_, v_block), score in zip(blocks, scores):
                weights = jnp.exp2((score - wide) * EXP2_SCALE)
                halves = weights[:, :HD] + weights[:, HD:]
                part = halves if part is None else part + halves
                term = jnp.dot(weights.astype(BF16), v_block(), preferred_element_type=F32)
                mixed = term if mixed is None else mixed + term
            if first:
                total[i] = part
                acc[i] = mixed
            else:
                fade = jnp.exp2((old - top) * EXP2_SCALE)
                total[i] = total[i] * fade + part
                acc[i] = acc[i] * fade + mixed

    def joined(one, other):
        return lambda: jnp.concatenate([one(), other()], axis=0)

    def blocks_of(half, with_own, arrivals):
        def of(i):
            out = []
            if with_own:
                h = item_head[i]
                out.append(
                    tuple(
                        joined(
                            lambda t=t: own[half, h, t], lambda t=t: beside[half, h, t]
                        )
                        for t in range(2)
                    )
                )
            for k in arrivals:
                slot = pick(ORDER[i][k], y)
                out.append(
                    tuple(
                        joined(
                            lambda t=t, slot=slot: ring[slot, half, t],
                            lambda t=t, slot=slot: cross[slot, half, t],
                        )
                        for t in range(2)
                    )
                )
            return out

        return of

    start_streams(0)
    pass_on(0, 1)
    pass_on(0, 2)
    start_streams(1)
    pass_on(0, 3, 4)
    pass_on(1, 1)
    cw_ref[:, 48:, :] = jnp.zeros((9, 80, cw_ref.shape[2]), BF16)

    await_bytes(q_land, s1_recv.at[HALVES])
    for place in range(NZ):
        for h in range(HG):
            q_own[h, block_rows(place), :] = q_land[place, :, h * HD : (h + 1) * HD]
    homes = {item: (k, i) for k in range(NY) for i, item in enumerate(ITEMS[k])}

    def send_queries(chip):
        for j in range(HG):
            to, slot = homes[j, chip]
            src = q_own.at[j]
            if to == chip:
                pltpu.make_async_copy(src, qb.at[slot], q_recv).start()
            else:
                remote(src, qb.at[slot], q_send, q_recv, s, ring_seq(to)).start()

    by_chip(send_queries)
    pass_on(1, 2)
    await_bytes(qb, q_recv)
    await_crossed(0, beside_recv, cross_recv)
    attend(blocks_of(0, True, (0, 1, 2)), True)
    pass_on(1, 3)
    attend(blocks_of(0, False, (3, 4, 5, 6)), False)
    pass_on(1, 4)
    await_crossed(1, beside_recv, cross_recv)
    attend(blocks_of(1, True, (0, 1, 2)), False)
    attend(blocks_of(1, False, (3, 4, 5, 6)), False)

    def back_copy(i, place):
        zp = (z + NEAREST[place]) % NZ
        return remote(
            ob.at[i, block_rows(place), :],
            att.at[z * HG + item_head[i]],
            o_send.at[i],
            o_recv,
            swap_sec,
            swap_seq(zp, item_y[i]),
        )

    at_home = [jnp.logical_and(stays, item_y[i] == y) for i in range(HG)]
    for i in range(HG):
        ob[i] = (acc[i] / jnp.sum(total[i], axis=1, keepdims=True)).astype(BF16)
        for place in range(NZ - 1, 0, -1):
            back_copy(i, place).start()

        @pl.when(jnp.logical_not(at_home[i]))
        def _(i=i):
            back_copy(i, 0).start()

        @pl.when(at_home[i])
        def _(i=i):
            pltpu.make_async_copy(
                ob.at[i, block_rows(0), :], att.at[z * HG + item_head[i]], o_recv
            ).start()

    for pack, sem in ((kv_pack, s1_send.at[0]), (q_pack, s1_send.at[1])):

        @pl.when(moves)
        def _(pack=pack, sem=sem):
            await_bytes(pack, sem)

        @pl.when(stays)
        def _(pack=pack, sem=sem):
            await_bytes(pack.at[pl.ds(0, NZ - 1)], sem)

    def ring_sent(chip):
        count = len(PLANS[chip][0]) + sum(
            passed for step in PLANS[chip][1] for _, passed, _ in step
        )
        for half in range(HALVES):
            await_bytes(ring.at[pl.ds(0, count), half], ring_send.at[half])
        away = sum(homes[j, chip][0] != chip for j in range(HG))
        await_bytes(qb.at[pl.ds(0, away)], q_send)

    by_chip(ring_sent)
    for half in range(HALVES):
        await_crossed(half, beside_send, cross_send)
    for load in loads:
        load.wait()
    await_bytes(att, o_recv)

    attended = jnp.concatenate([att[h] for h in range(H)], axis=1)
    hidden = res_ref[...].astype(F32) + gate_ref[...] * attended.astype(F32)
    center = hidden - jnp.mean(hidden, axis=1, keepdims=True)
    normed = center * lax.rsqrt(jnp.mean(center * center, axis=1, keepdims=True) + norm_eps)
    modulated = (normed * (1.0 + scale_ref[...]) + shift_ref[...]).astype(BF16)
    patches = (
        lax.dot_general(
            modulated, fw_ref[...], (((1,), (1,)), ((), ())), preferred_element_type=F32
        )
        + fb_ref[...]
    ) / scaling
    pat[...] = patches.astype(BF16).astype(F32)
    even = pat[pl.ds(0, F, stride=2), :]
    odd = pat[pl.ds(1, F, stride=2), :]
    side = 2 * LATC
    tile = jnp.concatenate([even[:, :side], odd[:, :side], even[:, side:], odd[:, side:]], axis=1)
    tiles[0, 0:1, :] = tile[:1]
    tiles[0, 1:2, :] = tile[:1]
    tiles[0, 2:8, :] = tile[:6]
    for part in (1, 2):
        tiles[part] = tile[4 * part - 2 : 4 * part + 6]
    tiles[3, 0:6, :] = tile[10:16]
    tiles[3, 6:8, :] = tile[14:16]

    for ds in range(1, 4):
        sp = (s + ds) % 4
        remote(
            tiles.at[sp], near_tiles.at[4, s], halo_send.at[0], halo_recv.at[0], sp, g
        ).start()
    near_tiles[4, s] = tiles[s]
    for i in range(HG):

        @pl.when(at_home[i])
        def _(i=i):
            await_bytes(ob.at[i, pl.ds(0, NBLK - TOK), :], o_send.at[i])

        @pl.when(jnp.logical_not(at_home[i]))
        def _(i=i):
            await_bytes(ob.at[i], o_send.at[i])

    await_bytes(tiles.at[pl.ds(0, 3)], halo_recv.at[0])
    for dy, dx in neighbours:
        remote(
            near_tiles.at[4],
            near_tiles.at[(1 - dy) * 3 + 1 - dx],
            halo_send.at[1],
            halo_recv.at[1],
            s,
            tile_seq(dy, dx),
        ).start()
    await_bytes(tiles.at[pl.ds(0, 3)], halo_send.at[0])
    await_bytes(near_tiles.at[pl.ds(0, 8)], halo_recv.at[1])

    def clear(at_edge, gone):
        @pl.when(at_edge)
        def _():
            for place in gone:
                near_tiles[place] = jnp.zeros((4, 8, 128), F32)

    clear(z == 0, (0, 1, 2))
    clear(z == NZ - 1, (6, 7, 8))
    clear(col == 0, (0, 3, 6))
    clear(col == 2 * NY - 1, (2, 5, 8))

    for yy in range(4):
        vert, dr = ((0, 1), (1, 0), (1, 1), (2, 0))[yy]
        lo = dr * BC * LATC
        hi = lo + BC * LATC
        sides = [near_tiles[vert * 3 + dx].reshape(32, 128) for dx in range(3)]
        strip = jnp.concatenate(
            [
                sides[0][:, hi - LATC : hi],
                sides[1][:, lo:hi],
                sides[2][:, lo : lo + LATC],
                jnp.zeros((32, 2 * LATC), F32),
            ],
            axis=1,
        )
        for x in range(BC):
            moved = strip if x == 0 else pltpu.roll(strip, 128 - x * LATC, axis=1)
            moved = moved.reshape(4, 8, 128)
            for dt in range(3):
                piece = moved[:, dt : dt + 4, :].reshape(16, 128)
                for dy in range(3):
                    row = yy - dy
                    if 0 <= row < BR:
                        windows[dt * 3 + dy, pl.ds(row * BC + x, 16, stride=8), :] = piece
    await_bytes(cw_ref.at[:, pl.ds(0, 48), :], cw_sem)
    left_side = jnp.concatenate([windows[tap].astype(BF16) for tap in range(9)], axis=1)
    conv = jnp.dot(
        left_side, cw_ref[...].reshape(9 * 128, cw_ref.shape[2]), preferred_element_type=F32
    )
    conv = (conv + cb_ref[...]) * gg_ref[...] + gb_ref[...]
    out_ref[...] = (conv / (1.0 + jnp.exp(-conv))).astype(BF16)

    await_bytes(near_tiles.at[pl.ds(0, 8)], halo_send.at[1])


def on_device(
    queries,
    keys,
    values,
    residual,
    shift_mod,
    scale_mod,
    gate_mod,
    final_weight,
    final_bias,
    conv_weight,
    conv_bias,
    group_gain,
    group_bias,
):
    any_spec = pl.BlockSpec(memory_space=pl.ANY)
    dma = pltpu.SemaphoreType.DMA
    vae_width = conv_weight.shape[1]
    slots = 2 * HG * MOST_HOPS
    features = pl.pallas_call(
        whole_kernel,
        out_shape=jax.ShapeDtypeStruct((4 * 4 * BR * BC, vae_width), BF16),
        in_specs=[any_spec] * 13,
        out_specs=pl.BlockSpec(memory_space=pltpu.VMEM),
        scratch_shapes=[
            pltpu.VMEM((TOK, H * HD), BF16),
            pltpu.VMEM((TOK, H * HD), BF16),
            pltpu.VMEM((TOK, H * HD), BF16),
            pltpu.VMEM((NZ, 2, TOK, GW), BF16),
            pltpu.VMEM((NZ, TOK, GW), BF16),
            pltpu.VMEM((NZ, 2, TOK, GW), BF16),
            pltpu.VMEM((NZ, TOK, GW), BF16),
            pltpu.VMEM((HG, NBLK, HD), BF16),
            pltpu.VMEM((HALVES, HG, 2, HALF, HD), BF16),
            pltpu.VMEM((HALVES, HG, 2, HALF, HD), BF16),
            pltpu.VMEM((slots, HALVES, 2, HALF, HD), BF16),
            pltpu.VMEM((slots, HALVES, 2, HALF, HD), BF16),
            pltpu.VMEM((HG, NBLK, HD), BF16),
            pltpu.VMEM((HG, NBLK, HD), BF16),
            pltpu.VMEM((H, TOK, HD), BF16),
            pltpu.VMEM((HG, NBLK, HD), F32),
            pltpu.VMEM((HG, NBLK, HD), F32),
            pltpu.VMEM((HG, NBLK, HD), F32),
            pltpu.VMEM((TOK, 4 * LATC), F32),
            pltpu.VMEM((4, 8, 128), F32),
            pltpu.VMEM((9, 4, 8, 128), F32),
            pltpu.VMEM((9, 4 * 4 * BR * BC, 128), F32),
            pltpu.VMEM((TOK, H * HD), BF16),
            pltpu.VMEM((1, H * HD), F32),
            pltpu.VMEM((1, H * HD), F32),
            pltpu.VMEM((1, H * HD), F32),
            pltpu.VMEM((4 * LATC, H * HD), BF16),
            pltpu.VMEM((1, 4 * LATC), F32),
            pltpu.VMEM((9, 128, vae_width), BF16),
            pltpu.VMEM((1, vae_width), F32),
            pltpu.VMEM((1, vae_width), F32),
            pltpu.VMEM((1, vae_width), F32),
            dma((3,)),
            dma((9,)),
            dma(()),
            dma((2,)),
            dma((HALVES + 1,)),
            dma(()),
            dma(()),
            dma((HALVES,)),
            dma((HALVES, slots)),
            dma((HALVES,)),
            dma((HALVES,)),
            dma((HALVES,)),
            dma((HALVES,)),
            dma((HG,)),
            dma(()),
            dma((2,)),
            dma((2,)),
        ],
        compiler_params=pltpu.CompilerParams(
            collective_id=0, has_side_effects=True, vmem_limit_bytes=60 * 1024 * 1024
        ),
        name="whole",
    )(
        queries[0],
        keys[0],
        values[0],
        residual[0],
        shift_mod,
        scale_mod,
        gate_mod,
        final_weight.T,
        final_bias[None],
        conv_weight,
        conv_bias[None],
        group_gain[None],
        group_bias[None],
    )
    return features.reshape(4, 4, 1, BR * BC, vae_width)


def solution(mesh):
    return jax.shard_map(
        on_device,
        mesh=mesh,
        in_specs=(
            P("sec", "seq", None),
            P("sec", "seq", None),
            P("sec", "seq", None),
            P("sec", "seq", None),
            P("sec", None),
            P("sec", None),
            P("sec", None),
            P(),
            P(),
            P(),
            P(),
            P(),
            P(),
        ),
        out_specs=P(None, "sec", "seq", None, None),
        check_vma=False,
    )
```

```python
import functools

import jax
import jax.numpy as jnp
from jax import lax
from jax.experimental import pallas as pl
from jax.experimental.pallas import tpu as pltpu
from jax.sharding import PartitionSpec as P

H = 24
HD = 128
LATC = 16
F = 16
BR = 2
BC = 4
NZ = 8
NY = 8
TOK = 32
HG = 3
GW = HG * HD
NBLK = NZ * TOK

scaling = 0.476986
norm_eps = 1e-06
EXP2_SCALE = HD ** (-0.5) * 1.4426950408889634
F32 = jnp.float32
BF16 = jnp.bfloat16


def remote(src, dst, send_sem, recv_sem, sec, seq):
    return pltpu.make_async_remote_copy(
        src_ref=src,
        dst_ref=dst,
        send_sem=send_sem,
        recv_sem=recv_sem,
        device_id={"sec": sec, "seq": seq},
        device_id_type=pl.DeviceIdType.MESH,
    )


def signal(sem, sec, seq):
    pl.semaphore_signal(
        sem, inc=1, device_id={"sec": sec, "seq": seq}, device_id_type=pl.DeviceIdType.MESH
    )


def position():
    s = lax.axis_index("sec")
    g = lax.axis_index("seq")
    return s, g, s % 2, s // 2, g // (2 * NY), (g // 2) % NY, g % 2

NEAREST = (0, 1, 7, 2, 6, 3, 5, 4)
AROUND = [(dy, dx) for dy in (-1, 0, 1) for dx in (-1, 0, 1)]

HALVES = 2
PER_HALF = NZ // HALVES
HALF = NBLK // HALVES


def whole_kernel(
    q_ref,
    k_ref,
    v_ref,
    res_hbm,
    shift_hbm,
    scale_hbm,
    gate_hbm,
    fw_hbm,
    fb_hbm,
    cw_hbm,
    cb_hbm,
    gg_hbm,
    gb_hbm,
    out_ref,
    qb,
    q_beside,
    kb,
    vb,
    ob,
    att,
    peak,
    total,
    acc,
    give,
    got,
    pat,
    tiles,
    near_tiles,
    windows,
    res_ref,
    shift_ref,
    scale_ref,
    gate_ref,
    fw_ref,
    fb_ref,
    cw_ref,
    cb_ref,
    gg_ref,
    gb_ref,
    load_sem,
    cw_sem,
    s1_send,
    s1_recv,
    ring_send,
    ring_recv,
    last_recv,
    q_send,
    q_recv,
    part_send,
    part_recv,
    o_send,
    o_recv,
    halo_send,
    halo_recv,
    ready,
):
    s, g, core, xl, z, y, xh = position()
    stays = core == xh
    moves = jnp.logical_not(stays)
    swap_sec = xl * 2 + xh
    sibling = xl * 2 + 1 - core
    col = y * 2 + xh

    def swap_seq(zp, yp):
        return (zp * NY + yp) * 2 + core

    def ring_seq(yp):
        return (z * NY + yp) * 2 + xh

    right = ring_seq((y + 1) % NY)
    left = ring_seq((y + NY - 1) % NY)

    neighbours = [(dy, dx) for dy, dx in AROUND if (dy, dx) != (0, 0)]

    def tile_seq(dy, dx):
        return (z + NZ + dy) % NZ * (2 * NY) + (col + 2 * NY + dx) % (2 * NY)

    barrier = pltpu.get_barrier_semaphore()
    for e in NEAREST[1:]:
        signal(barrier, swap_sec, swap_seq((z + e) % NZ, y))

    @pl.when(moves)
    def _():
        signal(barrier, swap_sec, swap_seq(z, y))

    signal(barrier, s, right)
    signal(barrier, s, left)
    for ds in range(1, 4):
        signal(barrier, (s + ds) % 4, g)
    for dy, dx in neighbours:
        signal(barrier, s, tile_seq(dy, dx))

    def group_cols(zp):
        return pl.ds(pl.multiple_of(zp * GW, HD), GW)

    def head_cols(h):
        return pl.ds(pl.multiple_of(h * HD, HD), HD)

    def block_rows(place):
        return pl.ds(place * TOK, TOK)

    def await_bytes(ref, sem):
        pltpu.make_async_copy(ref, ref, sem).wait()

    stage_one = ((k_ref, kb.at[0]), (v_ref, vb.at[0]), (q_ref, qb))

    def stage_sem(t, place):
        return s1_recv.at[t, 0 if t == 2 else place // PER_HALF]

    def stage_copy(t, place):
        src, buf = stage_one[t]
        zp = (z + NZ - NEAREST[place]) % NZ
        return remote(
            src.at[:, group_cols(zp)],
            buf.at[block_rows(place), :],
            s1_send.at[t],
            stage_sem(t, place),
            swap_sec,
            swap_seq(zp, y),
        )

    def start_stage(t):
        src, buf = stage_one[t]

        @pl.when(stays)
        def _():
            pltpu.make_async_copy(
                src.at[:, group_cols(z)], buf.at[block_rows(0), :], stage_sem(t, 0)
            ).start()

        @pl.when(moves)
        def _():
            stage_copy(t, 0).start()

        for place in range(1, NZ):
            stage_copy(t, place).start()

    pl.semaphore_wait(barrier, 2 * NZ + 5 - jnp.where(stays, 1, 0))
    for t in range(3):
        start_stage(t)
    for ds in range(1, 4):
        signal(ready, (s + ds) % 4, g)

    loads = [
        pltpu.make_async_copy(src, dst, load_sem.at[i])
        for i, (src, dst) in enumerate(
            (
                (res_hbm, res_ref),
                (shift_hbm, shift_ref),
                (scale_hbm, scale_ref),
                (gate_hbm, gate_ref),
                (fw_hbm, fw_ref),
                (fb_hbm, fb_ref),
                (cb_hbm, cb_ref),
                (gg_hbm, gg_ref),
                (gb_hbm, gb_ref),
            )
        )
    ]
    for load in loads:
        load.start()
    for tap in range(9):
        pltpu.make_async_copy(
            cw_hbm.at[pl.ds(tap * 48, 48), :], cw_ref.at[tap, pl.ds(0, 48), :], cw_sem
        ).start()

    bufs = (kb, vb)

    def slot_of(way, hops):
        if hops in (0, 4):
            return hops
        return hops if way == 0 else 4 + hops

    def half_of(t, slot, half):
        return bufs[t].at[slot, pl.ds(half * HALF, HALF), :]

    def head_of(t, slot, h):
        return bufs[t].at[slot, :, pl.ds(h * HD, HD)]

    def hop(way, t, half, hops):
        return remote(
            half_of(t, slot_of(way, hops - 1), half),
            half_of(t, slot_of(way, hops), half),
            ring_send.at[way],
            ring_recv.at[way, t, half, hops],
            s,
            (right, left)[way],
        )

    def last_hop(t, h):
        return remote(
            head_of(t, slot_of(t, 3), h),
            head_of(t, 4, h),
            ring_send.at[t],
            last_recv.at[t, h],
            s,
            (right, left)[t],
        )

    both = slice(0, 2 * NBLK)
    mine = slice(0, NBLK)
    others = slice(NBLK, 2 * NBLK)

    def attend(h, slots, rows, first):
        lanes = slice(h * HD, (h + 1) * HD)
        if rows == both:
            q = jnp.concatenate([qb[:, lanes], q_beside[:, lanes]], axis=0)
        else:
            q = (qb if rows == mine else q_beside)[:, lanes]
        scores = [
            lax.dot_general(
                q, kb[slot, :, lanes], (((1,), (1,)), ((), ())), preferred_element_type=F32
            )
            for slot in slots
        ]
        top = functools.reduce(jnp.maximum, scores)
        top = jnp.max(top, axis=1, keepdims=True)
        top = jnp.broadcast_to(top, (q.shape[0], HD))
        if not first:
            old = peak[h, rows]
            top = jnp.maximum(old, top)
        peak[h, rows] = top
        wide = jnp.concatenate([top, top], axis=1)
        part = None
        mixed = None
        for slot, score in zip(slots, scores):
            weights = jnp.exp2((score - wide) * EXP2_SCALE)
            halves = weights[:, :HD] + weights[:, HD:]
            part = halves if part is None else part + halves
            term = jnp.dot(weights.astype(BF16), vb[slot, :, lanes], preferred_element_type=F32)
            mixed = term if mixed is None else mixed + term
        if first:
            total[h, rows] = part
            acc[h, rows] = mixed
        else:
            fade = jnp.exp2((old - top) * EXP2_SCALE)
            total[h, rows] = total[h, rows] * fade + part
            acc[h, rows] = acc[h, rows] * fade + mixed

    pieces = [(t, half) for t in range(2) for half in range(HALVES)]
    for t, half in pieces:
        await_bytes(half_of(t, 0, half), s1_recv.at[t, half])
        hop(0, t, half, 1).start()
        hop(1, t, half, 1).start()
    cw_ref[:, 48:, :] = jnp.zeros((9, 80, cw_ref.shape[2]), BF16)
    for n in range(1, 4):
        for t, half in pieces:
            for way in range(2):
                hop(way, t, half, n).wait_recv()
                if n < 3:
                    hop(way, t, half, n + 1).start()
                elif way == t and half == HALVES - 1:
                    for h in range(HG):
                        last_hop(t, h).start()
        if n == 1:
            await_bytes(qb, s1_recv.at[2, 0])
            remote(qb, q_beside, q_send, q_recv, sibling, g).start()
        if n == 2:
            await_bytes(q_beside, q_recv)
            for h in range(HG):
                attend(h, (0, 1, 5), both, True)
        if n >= 2:
            for h in range(HG):
                attend(h, (n, 4 + n), both, False)

    def part_copy(h):
        return remote(give.at[h], got.at[h], part_send.at[h], part_recv.at[h], sibling, g)

    first_lanes = lax.broadcasted_iota(jnp.int32, (NBLK, HD), 1) < HD // 2
    for h in range(HG):
        for t in range(2):
            last_hop(t, h).wait_recv()
        attend(h, (4,), others, False)
        give[h, 0] = acc[h, others]
        sums = jnp.sum(total[h, others], axis=1, keepdims=True)
        give[h, 1] = jnp.where(first_lanes, peak[h, others], sums)
        part_copy(h).start()
    for h in range(HG):
        attend(h, (4,), mine, False)

    def back_copy(h, place):
        zp = (z + NEAREST[place]) % NZ
        return remote(
            ob.at[h, block_rows(place), :],
            att.at[:, head_cols(z * HG + h)],
            o_send.at[h],
            o_recv,
            swap_sec,
            swap_seq(zp, y),
        )

    for h in range(HG):
        part_copy(h).wait_recv()
        packed = got[h, 1]
        turned = pltpu.roll(packed, HD // 2, axis=1)
        other_peak = jnp.where(first_lanes, packed, turned)
        other_sums = jnp.where(first_lanes, turned, packed)
        own_peak = peak[h, mine]
        top = jnp.maximum(own_peak, other_peak)
        own_fade = jnp.exp2((own_peak - top) * EXP2_SCALE)
        other_fade = jnp.exp2((other_peak - top) * EXP2_SCALE)
        sums = jnp.sum(total[h, mine], axis=1, keepdims=True)
        mixed = acc[h, mine] * own_fade + got[h, 0] * other_fade
        ob[h] = (mixed / (sums * own_fade + other_sums * other_fade)).astype(BF16)
        for place in range(NZ - 1, 0, -1):
            back_copy(h, place).start()

        @pl.when(moves)
        def _(h=h):
            back_copy(h, 0).start()

        @pl.when(stays)
        def _(h=h):
            pltpu.make_async_copy(
                ob.at[h, block_rows(0), :], att.at[:, head_cols(z * HG + h)], o_recv
            ).start()

    def sent_blocks(ref, sem):
        @pl.when(moves)
        def _():
            await_bytes(ref, sem)

        @pl.when(stays)
        def _():
            await_bytes(ref.at[pl.ds(0, NBLK - TOK), :], sem)

    for t in range(3):
        sent_blocks(qb, s1_send.at[t])
    for way in range(2):
        await_bytes(kb.at[pl.ds(0, 7)], ring_send.at[way])
    await_bytes(qb, q_send)
    for h in range(HG):
        part_copy(h).wait_send()
    for load in loads:
        load.wait()
    await_bytes(att, o_recv)

    hidden = res_ref[...].astype(F32) + gate_ref[...] * att[...].astype(F32)
    center = hidden - jnp.mean(hidden, axis=1, keepdims=True)
    normed = center * lax.rsqrt(jnp.mean(center * center, axis=1, keepdims=True) + norm_eps)
    modulated = (normed * (1.0 + scale_ref[...]) + shift_ref[...]).astype(BF16)
    patches = (
        lax.dot_general(
            modulated, fw_ref[...], (((1,), (1,)), ((), ())), preferred_element_type=F32
        )
        + fb_ref[...]
    ) / scaling
    pat[...] = patches.astype(BF16).astype(F32)
    even = pat[pl.ds(0, F, stride=2), :]
    odd = pat[pl.ds(1, F, stride=2), :]
    side = 2 * LATC
    tile = jnp.concatenate([even[:, :side], odd[:, :side], even[:, side:], odd[:, side:]], axis=1)
    tiles[0, 0:1, :] = tile[:1]
    tiles[0, 1:2, :] = tile[:1]
    tiles[0, 2:8, :] = tile[:6]
    for part in (1, 2):
        tiles[part] = tile[4 * part - 2 : 4 * part + 6]
    tiles[3, 0:6, :] = tile[10:16]
    tiles[3, 6:8, :] = tile[14:16]

    pl.semaphore_wait(ready, 3)
    for dy, dx in AROUND:
        place = (1 - dy) * 3 + 1 - dx
        for ds in range(4):
            if (dy, dx, ds) != (0, 0, 0):
                sp = (s + ds) % 4
                remote(
                    tiles.at[sp],
                    near_tiles.at[place * 4 + s],
                    halo_send,
                    halo_recv,
                    sp,
                    tile_seq(dy, dx),
                ).start()
    near_tiles[4 * 4 + s] = tiles[s]
    for h in range(HG):
        sent_blocks(ob.at[h], o_send.at[h])
    await_bytes(near_tiles.at[pl.ds(0, 35)], halo_recv)

    def clear(at_edge, gone):
        @pl.when(at_edge)
        def _():
            for place in gone:
                near_tiles[place * 4 : place * 4 + 4] = jnp.zeros((4, 8, 128), F32)

    clear(z == 0, (0, 1, 2))
    clear(z == NZ - 1, (6, 7, 8))
    clear(col == 0, (0, 3, 6))
    clear(col == 2 * NY - 1, (2, 5, 8))

    for yy in range(4):
        vert, dr = ((0, 1), (1, 0), (1, 1), (2, 0))[yy]
        lo = dr * BC * LATC
        hi = lo + BC * LATC
        sides = [
            near_tiles[(vert * 3 + dx) * 4 : (vert * 3 + dx) * 4 + 4].reshape(32, 128)
            for dx in range(3)
        ]
        strip = jnp.concatenate(
            [
                sides[0][:, hi - LATC : hi],
                sides[1][:, lo:hi],
                sides[2][:, lo : lo + LATC],
                jnp.zeros((32, 2 * LATC), F32),
            ],
            axis=1,
        )
        for x in range(BC):
            moved = strip if x == 0 else pltpu.roll(strip, 128 - x * LATC, axis=1)
            moved = moved.reshape(4, 8, 128)
            for dt in range(3):
                piece = moved[:, dt : dt + 4, :].reshape(16, 128)
                for dy in range(3):
                    row = yy - dy
                    if 0 <= row < BR:
                        windows[dt * 3 + dy, pl.ds(row * BC + x, 16, stride=8), :] = piece
    await_bytes(cw_ref.at[:, pl.ds(0, 48), :], cw_sem)
    left_side = jnp.concatenate([windows[tap].astype(BF16) for tap in range(9)], axis=1)
    conv = jnp.dot(
        left_side, cw_ref[...].reshape(9 * 128, cw_ref.shape[2]), preferred_element_type=F32
    )
    conv = (conv + cb_ref[...]) * gg_ref[...] + gb_ref[...]
    out_ref[...] = (conv / (1.0 + jnp.exp(-conv))).astype(BF16)

    await_bytes(near_tiles.at[pl.ds(0, 35)], halo_send)


def on_device(
    queries,
    keys,
    values,
    residual,
    shift_mod,
    scale_mod,
    gate_mod,
    final_weight,
    final_bias,
    conv_weight,
    conv_bias,
    group_gain,
    group_bias,
):
    any_spec = pl.BlockSpec(memory_space=pl.ANY)
    dma = pltpu.SemaphoreType.DMA
    vae_width = conv_weight.shape[1]
    features = pl.pallas_call(
        whole_kernel,
        out_shape=jax.ShapeDtypeStruct((4 * 4 * BR * BC, vae_width), BF16),
        in_specs=[any_spec] * 13,
        out_specs=pl.BlockSpec(memory_space=pltpu.VMEM),
        scratch_shapes=[
            pltpu.VMEM((NBLK, GW), BF16),
            pltpu.VMEM((NBLK, GW), BF16),
            pltpu.VMEM((8, NBLK, GW), BF16),
            pltpu.VMEM((8, NBLK, GW), BF16),
            pltpu.VMEM((HG, NBLK, HD), BF16),
            pltpu.VMEM((TOK, H * HD), BF16),
            pltpu.VMEM((HG, 2 * NBLK, HD), F32),
            pltpu.VMEM((HG, 2 * NBLK, HD), F32),
            pltpu.VMEM((HG, 2 * NBLK, HD), F32),
            pltpu.VMEM((HG, 2, NBLK, HD), F32),
            pltpu.VMEM((HG, 2, NBLK, HD), F32),
            pltpu.VMEM((TOK, 4 * LATC), F32),
            pltpu.VMEM((4, 8, 128), F32),
            pltpu.VMEM((36, 8, 128), F32),
            pltpu.VMEM((9, 4 * 4 * BR * BC, 128), F32),
            pltpu.VMEM((TOK, H * HD), BF16),
            pltpu.VMEM((1, H * HD), F32),
            pltpu.VMEM((1, H * HD), F32),
            pltpu.VMEM((1, H * HD), F32),
            pltpu.VMEM((4 * LATC, H * HD), BF16),
            pltpu.VMEM((1, 4 * LATC), F32),
            pltpu.VMEM((9, 128, vae_width), BF16),
            pltpu.VMEM((1, vae_width), F32),
            pltpu.VMEM((1, vae_width), F32),
            pltpu.VMEM((1, vae_width), F32),
            dma((9,)),
            dma(()),
            dma((3,)),
            dma((3, HALVES)),
            dma((2,)),
            dma((2, 2, HALVES, 4)),
            dma((2, HG)),
            dma(()),
            dma(()),
            dma((HG,)),
            dma((HG,)),
            dma((HG,)),
            dma(()),
            dma(()),
            dma(()),
            pltpu.SemaphoreType.REGULAR,
        ],
        compiler_params=pltpu.CompilerParams(
            collective_id=0, has_side_effects=True, vmem_limit_bytes=60 * 1024 * 1024
        ),
        name="whole",
    )(
        queries[0],
        keys[0],
        values[0],
        residual[0],
        shift_mod,
        scale_mod,
        gate_mod,
        final_weight.T,
        final_bias[None],
        conv_weight,
        conv_bias[None],
        group_gain[None],
        group_bias[None],
    )
    return features.reshape(4, 4, 1, BR * BC, vae_width)


def solution(mesh):
    return jax.shard_map(
        on_device,
        mesh=mesh,
        in_specs=(
            P("sec", "seq", None),
            P("sec", "seq", None),
            P("sec", "seq", None),
            P("sec", "seq", None),
            P("sec", None),
            P("sec", None),
            P("sec", None),
            P(),
            P(),
            P(),
            P(),
            P(),
            P(),
        ),
        out_specs=P(None, "sec", "seq", None, None),
        check_vma=False,
    )
```

```python
import functools

import jax
import jax.numpy as jnp
from jax import lax
from jax.experimental import pallas as pl
from jax.experimental.pallas import tpu as pltpu
from jax.sharding import PartitionSpec as P

H = 24
HD = 128
LATC = 16
F = 16
BR = 2
BC = 4
NZ = 8
NY = 8
TOK = 32
HG = 3
NBLK = NZ * TOK

scaling = 0.476986
norm_eps = 1e-06
EXP2_SCALE = HD ** (-0.5) * 1.4426950408889634
F32 = jnp.float32
BF16 = jnp.bfloat16


def remote(src, dst, send_sem, recv_sem, sec, seq):
    return pltpu.make_async_remote_copy(
        src_ref=src,
        dst_ref=dst,
        send_sem=send_sem,
        recv_sem=recv_sem,
        device_id={"sec": sec, "seq": seq},
        device_id_type=pl.DeviceIdType.MESH,
    )


def signal(sem, sec, seq):
    pl.semaphore_signal(
        sem, inc=1, device_id={"sec": sec, "seq": seq}, device_id_type=pl.DeviceIdType.MESH
    )


def position():
    s = lax.axis_index("sec")
    g = lax.axis_index("seq")
    return s, g, s % 2, s // 2, g // (2 * NY), (g // 2) % NY, g % 2

NEAREST = (0, 1, 7, 2, 6, 3, 5, 4)
AROUND = [(dy, dx) for dy in (-1, 0, 1) for dx in (-1, 0, 1)]

RING_HEADS = ((0, 1), (2,))
FIRST_HEAD = (0, 2 * NZ)
PARTS = (2, 1)
WIDTH = (2 * HD, HD)


def whole_kernel(
    q_ref,
    k_ref,
    v_ref,
    res_hbm,
    shift_hbm,
    scale_hbm,
    gate_hbm,
    fw_hbm,
    fb_hbm,
    cw_hbm,
    cb_hbm,
    gg_hbm,
    gb_hbm,
    out_ref,
    q_rows,
    q_rows_beside,
    k_rows,
    v_rows,
    q_cols,
    q_cols_beside,
    k_cols,
    v_cols,
    ob,
    att,
    peak,
    total,
    acc,
    give,
    got,
    pat,
    tiles,
    near_tiles,
    windows,
    res_ref,
    shift_ref,
    scale_ref,
    gate_ref,
    fw_ref,
    fb_ref,
    cw_ref,
    cb_ref,
    gg_ref,
    gb_ref,
    load_sem,
    cw_sem,
    s1_send,
    s1_recv,
    ring_send,
    ring_recv,
    last_recv,
    q_send,
    q_recv,
    part_send,
    part_recv,
    o_send,
    o_recv,
    halo_send,
    halo_recv,
    ready,
):
    s, g, core, xl, z, y, xh = position()
    stays = core == xh
    moves = jnp.logical_not(stays)
    swap_sec = xl * 2 + xh
    sibling = xl * 2 + 1 - core
    col = y * 2 + xh

    def swap_seq(zp, yp):
        return (zp * NY + yp) * 2 + core

    def ring_seq(yp):
        return (z * NY + yp) * 2 + xh

    ways = (
        (ring_seq((y + 1) % NY), ring_seq((y + NY - 1) % NY)),
        (
            ((z + 1) % NZ * NY + y) * 2 + xh,
            ((z + NZ - 1) % NZ * NY + y) * 2 + xh,
        ),
    )
    along = (z, y)

    neighbours = [(dy, dx) for dy, dx in AROUND if (dy, dx) != (0, 0)]

    def tile_seq(dy, dx):
        return (z + NZ + dy) % NZ * (2 * NY) + (col + 2 * NY + dx) % (2 * NY)

    barrier = pltpu.get_barrier_semaphore()
    for e in NEAREST[1:]:
        signal(barrier, swap_sec, swap_seq((z + e) % NZ, y))

    @pl.when(moves)
    def _():
        signal(barrier, swap_sec, swap_seq(z, y))

    for e in NEAREST[1:]:
        signal(barrier, swap_sec, swap_seq(z, (y + e) % NY))
    for r in range(2):
        for way in range(2):
            signal(barrier, s, ways[r][way])
    for ds in range(1, 4):
        signal(barrier, (s + ds) % 4, g)
    for dy, dx in neighbours:
        signal(barrier, s, tile_seq(dy, dx))

    def group_cols(r, group):
        first = FIRST_HEAD[r] * HD + group * WIDTH[r]
        return pl.ds(pl.multiple_of(first, HD), WIDTH[r])

    def head_cols(h):
        return pl.ds(pl.multiple_of(h * HD, HD), HD)

    def swap_along(r, group):
        return swap_seq(group, y) if r == 0 else swap_seq(z, group)

    def block_rows(place):
        return pl.ds(place * TOK, TOK)

    def await_bytes(ref, sem):
        pltpu.make_async_copy(ref, ref, sem).wait()

    sources = (k_ref, v_ref, q_ref)
    queries = (q_rows, q_cols)
    beside = (q_rows_beside, q_cols_beside)
    bufs = ((k_rows, v_rows), (k_cols, v_cols))

    def landing(r, t):
        return queries[r] if t == 2 else bufs[r][t].at[0]

    def stage_sem(r, t, place):
        return s1_recv.at[r, t, 0 if t == 2 else place * PARTS[r] // NZ]

    def stage_copy(r, t, place):
        group = (along[r] + NZ - NEAREST[place]) % NZ
        return remote(
            sources[t].at[:, group_cols(r, group)],
            landing(r, t).at[block_rows(place), :],
            s1_send.at[r, t],
            stage_sem(r, t, place),
            swap_sec,
            swap_along(r, group),
        )

    def start_stage(r, t):
        @pl.when(stays)
        def _():
            pltpu.make_async_copy(
                sources[t].at[:, group_cols(r, along[r])],
                landing(r, t).at[block_rows(0), :],
                stage_sem(r, t, 0),
            ).start()

        @pl.when(moves)
        def _():
            stage_copy(r, t, 0).start()

        for place in range(1, NZ):
            stage_copy(r, t, place).start()

    pl.semaphore_wait(barrier, 3 * NZ + 6 - jnp.where(stays, 1, 0))
    for t in range(3):
        for r in range(2):
            start_stage(r, t)
    for ds in range(1, 4):
        signal(ready, (s + ds) % 4, g)

    loads = [
        pltpu.make_async_copy(src, dst, load_sem.at[i])
        for i, (src, dst) in enumerate(
            (
                (res_hbm, res_ref),
                (shift_hbm, shift_ref),
                (scale_hbm, scale_ref),
                (gate_hbm, gate_ref),
                (fw_hbm, fw_ref),
                (fb_hbm, fb_ref),
                (cb_hbm, cb_ref),
                (gg_hbm, gg_ref),
                (gb_hbm, gb_ref),
            )
        )
    ]
    for load in loads:
        load.start()
    for tap in range(9):
        pltpu.make_async_copy(
            cw_hbm.at[pl.ds(tap * 48, 48), :], cw_ref.at[tap, pl.ds(0, 48), :], cw_sem
        ).start()

    def slot_of(way, hops):
        if hops in (0, 4):
            return hops
        return hops if way == 0 else 4 + hops

    def part_of(r, t, slot, part):
        rows = NBLK // PARTS[r]
        return bufs[r][t].at[slot, pl.ds(part * rows, rows), :]

    def head_of(h, t, slot):
        if h == 2:
            return k_cols.at[slot] if t == 0 else v_cols.at[slot]
        return bufs[0][t].at[slot, :, pl.ds(h * HD, HD)]

    def hop(r, way, t, part, hops):
        return remote(
            part_of(r, t, slot_of(way, hops - 1), part),
            part_of(r, t, slot_of(way, hops), part),
            ring_send.at[r, way],
            ring_recv.at[r, way, t, part, hops],
            s,
            ways[r][way],
        )

    def last_hop(t, h):
        r = 0 if h < 2 else 1
        return remote(
            head_of(h, t, slot_of(t, 3)),
            head_of(h, t, 4),
            ring_send.at[r, t],
            last_recv.at[t, h],
            s,
            ways[r][t],
        )

    both = slice(0, 2 * NBLK)
    mine = slice(0, NBLK)
    others = slice(NBLK, 2 * NBLK)

    def attend(h, slots, rows, first):
        r, lanes = (1, slice(0, HD)) if h == 2 else (0, slice(h * HD, (h + 1) * HD))
        if rows == both:
            q = jnp.concatenate([queries[r][:, lanes], beside[r][:, lanes]], axis=0)
        else:
            q = (queries if rows == mine else beside)[r][:, lanes]
        scores = [
            lax.dot_general(
                q, head_of(h, 0, slot)[...], (((1,), (1,)), ((), ())), preferred_element_type=F32
            )
            for slot in slots
        ]
        top = functools.reduce(jnp.maximum, scores)
        top = jnp.max(top, axis=1, keepdims=True)
        top = jnp.broadcast_to(top, (q.shape[0], HD))
        if not first:
            old = peak[h, rows]
            top = jnp.maximum(old, top)
        peak[h, rows] = top
        wide = jnp.concatenate([top, top], axis=1)
        part = None
        mixed = None
        for slot, score in zip(slots, scores):
            weights = jnp.exp2((score - wide) * EXP2_SCALE)
            halves = weights[:, :HD] + weights[:, HD:]
            part = halves if part is None else part + halves
            term = jnp.dot(
                weights.astype(BF16), head_of(h, 1, slot)[...], preferred_element_type=F32
            )
            mixed = term if mixed is None else mixed + term
        if first:
            total[h, rows] = part
            acc[h, rows] = mixed
        else:
            fade = jnp.exp2((old - top) * EXP2_SCALE)
            total[h, rows] = total[h, rows] * fade + part
            acc[h, rows] = acc[h, rows] * fade + mixed

    pieces = [(0, 0, 0), (1, 0, 0), (0, 0, 1), (0, 1, 0), (1, 1, 0), (0, 1, 1)]
    for r, t, part in pieces:
        await_bytes(part_of(r, t, 0, part), s1_recv.at[r, t, part])
        for way in range(2):
            hop(r, way, t, part, 1).start()
    cw_ref[:, 48:, :] = jnp.zeros((9, 80, cw_ref.shape[2]), BF16)
    for n in range(1, 4):
        for r, t, part in pieces:
            for way in range(2):
                hop(r, way, t, part, n).wait_recv()
                if n < 3:
                    hop(r, way, t, part, n + 1).start()
                elif way == t and part == PARTS[r] - 1:
                    for h in RING_HEADS[r]:
                        last_hop(t, h).start()
        if n == 1:
            for r in range(2):
                await_bytes(queries[r], s1_recv.at[r, 2, 0])
                remote(queries[r], beside[r], q_send.at[r], q_recv.at[r], sibling, g).start()
        if n == 2:
            for r in range(2):
                await_bytes(beside[r], q_recv.at[r])
            for h in range(HG):
                attend(h, (0, 1, 5), both, True)
        if n >= 2:
            for h in range(HG):
                attend(h, (n, 4 + n), both, False)

    def part_copy(h):
        return remote(give.at[h], got.at[h], part_send.at[h], part_recv.at[h], sibling, g)

    first_lanes = lax.broadcasted_iota(jnp.int32, (NBLK, HD), 1) < HD // 2
    for h in range(HG):
        for t in range(2):
            last_hop(t, h).wait_recv()
        attend(h, (4,), others, False)
        give[h, 0] = acc[h, others]
        sums = jnp.sum(total[h, others], axis=1, keepdims=True)
        give[h, 1] = jnp.where(first_lanes, peak[h, others], sums)
        part_copy(h).start()
    for h in range(HG):
        attend(h, (4,), mine, False)

    def home_cols(h):
        return head_cols(z * 2 + h if h < 2 else FIRST_HEAD[1] + y)

    def back_copy(h, place):
        r = 0 if h < 2 else 1
        return remote(
            ob.at[h, block_rows(place), :],
            att.at[:, home_cols(h)],
            o_send.at[h],
            o_recv,
            swap_sec,
            swap_along(r, (along[r] + NEAREST[place]) % NZ),
        )

    for h in range(HG):
        part_copy(h).wait_recv()
        packed = got[h, 1]
        turned = pltpu.roll(packed, HD // 2, axis=1)
        other_peak = jnp.where(first_lanes, packed, turned)
        other_sums = jnp.where(first_lanes, turned, packed)
        own_peak = peak[h, mine]
        top = jnp.maximum(own_peak, other_peak)
        own_fade = jnp.exp2((own_peak - top) * EXP2_SCALE)
        other_fade = jnp.exp2((other_peak - top) * EXP2_SCALE)
        sums = jnp.sum(total[h, mine], axis=1, keepdims=True)
        mixed = acc[h, mine] * own_fade + got[h, 0] * other_fade
        ob[h] = (mixed / (sums * own_fade + other_sums * other_fade)).astype(BF16)
        for place in range(NZ - 1, 0, -1):
            back_copy(h, place).start()

        @pl.when(moves)
        def _(h=h):
            back_copy(h, 0).start()

        @pl.when(stays)
        def _(h=h):
            pltpu.make_async_copy(
                ob.at[h, block_rows(0), :], att.at[:, home_cols(h)], o_recv
            ).start()

    def sent_blocks(ref, sem):
        @pl.when(moves)
        def _():
            await_bytes(ref, sem)

        @pl.when(stays)
        def _():
            await_bytes(ref.at[pl.ds(0, NBLK - TOK), :], sem)

    for r in range(2):
        for t in range(3):
            sent_blocks(queries[r], s1_send.at[r, t])
        for way in range(2):
            await_bytes(bufs[r][0].at[pl.ds(0, 7)], ring_send.at[r, way])
        await_bytes(queries[r], q_send.at[r])
    for h in range(HG):
        part_copy(h).wait_send()
    for load in loads:
        load.wait()
    await_bytes(att, o_recv)

    hidden = res_ref[...].astype(F32) + gate_ref[...] * att[...].astype(F32)
    center = hidden - jnp.mean(hidden, axis=1, keepdims=True)
    normed = center * lax.rsqrt(jnp.mean(center * center, axis=1, keepdims=True) + norm_eps)
    modulated = (normed * (1.0 + scale_ref[...]) + shift_ref[...]).astype(BF16)
    patches = (
        lax.dot_general(
            modulated, fw_ref[...], (((1,), (1,)), ((), ())), preferred_element_type=F32
        )
        + fb_ref[...]
    ) / scaling
    pat[...] = patches.astype(BF16).astype(F32)
    even = pat[pl.ds(0, F, stride=2), :]
    odd = pat[pl.ds(1, F, stride=2), :]
    side = 2 * LATC
    tile = jnp.concatenate([even[:, :side], odd[:, :side], even[:, side:], odd[:, side:]], axis=1)
    tiles[0, 0:1, :] = tile[:1]
    tiles[0, 1:2, :] = tile[:1]
    tiles[0, 2:8, :] = tile[:6]
    for part in (1, 2):
        tiles[part] = tile[4 * part - 2 : 4 * part + 6]
    tiles[3, 0:6, :] = tile[10:16]
    tiles[3, 6:8, :] = tile[14:16]

    pl.semaphore_wait(ready, 3)
    for dy, dx in AROUND:
        place = (1 - dy) * 3 + 1 - dx
        for ds in range(4):
            if (dy, dx, ds) != (0, 0, 0):
                sp = (s + ds) % 4
                remote(
                    tiles.at[sp],
                    near_tiles.at[place * 4 + s],
                    halo_send,
                    halo_recv,
                    sp,
                    tile_seq(dy, dx),
                ).start()
    near_tiles[4 * 4 + s] = tiles[s]
    for h in range(HG):
        sent_blocks(ob.at[h], o_send.at[h])
    await_bytes(near_tiles.at[pl.ds(0, 35)], halo_recv)

    def clear(at_edge, gone):
        @pl.when(at_edge)
        def _():
            for place in gone:
                near_tiles[place * 4 : place * 4 + 4] = jnp.zeros((4, 8, 128), F32)

    clear(z == 0, (0, 1, 2))
    clear(z == NZ - 1, (6, 7, 8))
    clear(col == 0, (0, 3, 6))
    clear(col == 2 * NY - 1, (2, 5, 8))

    for yy in range(4):
        vert, dr = ((0, 1), (1, 0), (1, 1), (2, 0))[yy]
        lo = dr * BC * LATC
        hi = lo + BC * LATC
        sides = [
            near_tiles[(vert * 3 + dx) * 4 : (vert * 3 + dx) * 4 + 4].reshape(32, 128)
            for dx in range(3)
        ]
        strip = jnp.concatenate(
            [
                sides[0][:, hi - LATC : hi],
                sides[1][:, lo:hi],
                sides[2][:, lo : lo + LATC],
                jnp.zeros((32, 2 * LATC), F32),
            ],
            axis=1,
        )
        for x in range(BC):
            moved = strip if x == 0 else pltpu.roll(strip, 128 - x * LATC, axis=1)
            moved = moved.reshape(4, 8, 128)
            for dt in range(3):
                piece = moved[:, dt : dt + 4, :].reshape(16, 128)
                for dy in range(3):
                    row = yy - dy
                    if 0 <= row < BR:
                        windows[dt * 3 + dy, pl.ds(row * BC + x, 16, stride=8), :] = piece
    await_bytes(cw_ref.at[:, pl.ds(0, 48), :], cw_sem)
    left_side = jnp.concatenate([windows[tap].astype(BF16) for tap in range(9)], axis=1)
    conv = jnp.dot(
        left_side, cw_ref[...].reshape(9 * 128, cw_ref.shape[2]), preferred_element_type=F32
    )
    conv = (conv + cb_ref[...]) * gg_ref[...] + gb_ref[...]
    out_ref[...] = (conv / (1.0 + jnp.exp(-conv))).astype(BF16)

    await_bytes(near_tiles.at[pl.ds(0, 35)], halo_send)


def on_device(
    queries,
    keys,
    values,
    residual,
    shift_mod,
    scale_mod,
    gate_mod,
    final_weight,
    final_bias,
    conv_weight,
    conv_bias,
    group_gain,
    group_bias,
):
    any_spec = pl.BlockSpec(memory_space=pl.ANY)
    dma = pltpu.SemaphoreType.DMA
    vae_width = conv_weight.shape[1]
    features = pl.pallas_call(
        whole_kernel,
        out_shape=jax.ShapeDtypeStruct((4 * 4 * BR * BC, vae_width), BF16),
        in_specs=[any_spec] * 13,
        out_specs=pl.BlockSpec(memory_space=pltpu.VMEM),
        scratch_shapes=[
            pltpu.VMEM((NBLK, 2 * HD), BF16),
            pltpu.VMEM((NBLK, 2 * HD), BF16),
            pltpu.VMEM((8, NBLK, 2 * HD), BF16),
            pltpu.VMEM((8, NBLK, 2 * HD), BF16),
            pltpu.VMEM((NBLK, HD), BF16),
            pltpu.VMEM((NBLK, HD), BF16),
            pltpu.VMEM((8, NBLK, HD), BF16),
            pltpu.VMEM((8, NBLK, HD), BF16),
            pltpu.VMEM((HG, NBLK, HD), BF16),
            pltpu.VMEM((TOK, H * HD), BF16),
            pltpu.VMEM((HG, 2 * NBLK, HD), F32),
            pltpu.VMEM((HG, 2 * NBLK, HD), F32),
            pltpu.VMEM((HG, 2 * NBLK, HD), F32),
            pltpu.VMEM((HG, 2, NBLK, HD), F32),
            pltpu.VMEM((HG, 2, NBLK, HD), F32),
            pltpu.VMEM((TOK, 4 * LATC), F32),
            pltpu.VMEM((4, 8, 128), F32),
            pltpu.VMEM((36, 8, 128), F32),
            pltpu.VMEM((9, 4 * 4 * BR * BC, 128), F32),
            pltpu.VMEM((TOK, H * HD), BF16),
            pltpu.VMEM((1, H * HD), F32),
            pltpu.VMEM((1, H * HD), F32),
            pltpu.VMEM((1, H * HD), F32),
            pltpu.VMEM((4 * LATC, H * HD), BF16),
            pltpu.VMEM((1, 4 * LATC), F32),
            pltpu.VMEM((9, 128, vae_width), BF16),
            pltpu.VMEM((1, vae_width), F32),
            pltpu.VMEM((1, vae_width), F32),
            pltpu.VMEM((1, vae_width), F32),
            dma((9,)),
            dma(()),
            dma((2, 3)),
            dma((2, 3, 2)),
            dma((2, 2)),
            dma((2, 2, 2, 2, 4)),
            dma((2, HG)),
            dma((2,)),
            dma((2,)),
            dma((HG,)),
            dma((HG,)),
            dma((HG,)),
            dma(()),
            dma(()),
            dma(()),
            pltpu.SemaphoreType.REGULAR,
        ],
        compiler_params=pltpu.CompilerParams(
            collective_id=0, has_side_effects=True, vmem_limit_bytes=60 * 1024 * 1024
        ),
        name="whole",
    )(
        queries[0],
        keys[0],
        values[0],
        residual[0],
        shift_mod,
        scale_mod,
        gate_mod,
        final_weight.T,
        final_bias[None],
        conv_weight,
        conv_bias[None],
        group_gain[None],
        group_bias[None],
    )
    return features.reshape(4, 4, 1, BR * BC, vae_width)


def solution(mesh):
    return jax.shard_map(
        on_device,
        mesh=mesh,
        in_specs=(
            P("sec", "seq", None),
            P("sec", "seq", None),
            P("sec", "seq", None),
            P("sec", "seq", None),
            P("sec", None),
            P("sec", None),
            P("sec", None),
            P(),
            P(),
            P(),
            P(),
            P(),
            P(),
        ),
        out_specs=P(None, "sec", "seq", None, None),
        check_vma=False,
    )
```

```python
import functools

import jax
import jax.numpy as jnp
from jax import lax
from jax.experimental import pallas as pl
from jax.experimental.pallas import tpu as pltpu
from jax.sharding import PartitionSpec as P

H = 24
HD = 128
LATC = 16
F = 16
BR = 2
BC = 4
NZ = 8
NY = 8
TOK = 32
HG = 3
NBLK = NZ * TOK

scaling = 0.476986
norm_eps = 1e-06
EXP2_SCALE = HD ** (-0.5) * 1.4426950408889634
F32 = jnp.float32
BF16 = jnp.bfloat16


def remote(src, dst, send_sem, recv_sem, sec, seq):
    return pltpu.make_async_remote_copy(
        src_ref=src,
        dst_ref=dst,
        send_sem=send_sem,
        recv_sem=recv_sem,
        device_id={"sec": sec, "seq": seq},
        device_id_type=pl.DeviceIdType.MESH,
    )


def signal(sem, sec, seq):
    pl.semaphore_signal(
        sem, inc=1, device_id={"sec": sec, "seq": seq}, device_id_type=pl.DeviceIdType.MESH
    )


def position():
    s = lax.axis_index("sec")
    g = lax.axis_index("seq")
    return s, g, s % 2, s // 2, g // (2 * NY), (g // 2) % NY, g % 2

NEAREST = (0, 1, 7, 2, 6, 3, 5, 4)
AROUND = [(dy, dx) for dy in (-1, 0, 1) for dx in (-1, 0, 1)]

RING_HEADS = ((0, 1), (2,))
FIRST_HEAD = (0, 2 * NZ)
PARTS = (2, 1)
WIDTH = (2 * HD, HD)


def whole_kernel(
    q_ref,
    k_ref,
    v_ref,
    res_hbm,
    shift_hbm,
    scale_hbm,
    gate_hbm,
    fw_hbm,
    fb_hbm,
    out_ref,
    q_rows,
    q_rows_beside,
    k_rows,
    v_rows,
    q_cols,
    q_cols_beside,
    k_cols,
    v_cols,
    ob,
    att,
    peak,
    total,
    acc,
    give,
    got,
    pat,
    tiles,
    near_tiles,
    windows,
    res_ref,
    shift_ref,
    scale_ref,
    gate_ref,
    fw_ref,
    fb_ref,
    load_sem,
    s1_send,
    s1_recv,
    ring_send,
    ring_recv,
    last_recv,
    q_send,
    q_recv,
    part_send,
    part_recv,
    o_send,
    o_recv,
    halo_send,
    halo_recv,
    ready,
):
    s, g, core, xl, z, y, xh = position()
    stays = core == xh
    moves = jnp.logical_not(stays)
    swap_sec = xl * 2 + xh
    sibling = xl * 2 + 1 - core
    col = y * 2 + xh

    def swap_seq(zp, yp):
        return (zp * NY + yp) * 2 + core

    def ring_seq(yp):
        return (z * NY + yp) * 2 + xh

    ways = (
        (ring_seq((y + 1) % NY), ring_seq((y + NY - 1) % NY)),
        (
            ((z + 1) % NZ * NY + y) * 2 + xh,
            ((z + NZ - 1) % NZ * NY + y) * 2 + xh,
        ),
    )
    along = (z, y)

    neighbours = [(dy, dx) for dy, dx in AROUND if (dy, dx) != (0, 0)]

    def tile_seq(dy, dx):
        return (z + NZ + dy) % NZ * (2 * NY) + (col + 2 * NY + dx) % (2 * NY)

    barrier = pltpu.get_barrier_semaphore()
    for e in NEAREST[1:]:
        signal(barrier, swap_sec, swap_seq((z + e) % NZ, y))

    @pl.when(moves)
    def _():
        signal(barrier, swap_sec, swap_seq(z, y))

    for e in NEAREST[1:]:
        signal(barrier, swap_sec, swap_seq(z, (y + e) % NY))
    for r in range(2):
        for way in range(2):
            signal(barrier, s, ways[r][way])
    for ds in range(1, 4):
        signal(barrier, (s + ds) % 4, g)
    for dy, dx in neighbours:
        signal(barrier, s, tile_seq(dy, dx))

    def group_cols(r, group):
        first = FIRST_HEAD[r] * HD + group * WIDTH[r]
        return pl.ds(pl.multiple_of(first, HD), WIDTH[r])

    def head_cols(h):
        return pl.ds(pl.multiple_of(h * HD, HD), HD)

    def swap_along(r, group):
        return swap_seq(group, y) if r == 0 else swap_seq(z, group)

    def block_rows(place):
        return pl.ds(place * TOK, TOK)

    def await_bytes(ref, sem):
        pltpu.make_async_copy(ref, ref, sem).wait()

    sources = (k_ref, v_ref, q_ref)
    queries = (q_rows, q_cols)
    beside = (q_rows_beside, q_cols_beside)
    bufs = ((k_rows, v_rows), (k_cols, v_cols))

    def landing(r, t):
        return queries[r] if t == 2 else bufs[r][t].at[0]

    def stage_sem(r, t, place):
        return s1_recv.at[r, t, 0 if t == 2 else place * PARTS[r] // NZ]

    def stage_copy(r, t, place):
        group = (along[r] + NZ - NEAREST[place]) % NZ
        return remote(
            sources[t].at[:, group_cols(r, group)],
            landing(r, t).at[block_rows(place), :],
            s1_send.at[r, t],
            stage_sem(r, t, place),
            swap_sec,
            swap_along(r, group),
        )

    def start_stage(r, t):
        @pl.when(stays)
        def _():
            pltpu.make_async_copy(
                sources[t].at[:, group_cols(r, along[r])],
                landing(r, t).at[block_rows(0), :],
                stage_sem(r, t, 0),
            ).start()

        @pl.when(moves)
        def _():
            stage_copy(r, t, 0).start()

        for place in range(1, NZ):
            stage_copy(r, t, place).start()

    pl.semaphore_wait(barrier, 3 * NZ + 6 - jnp.where(stays, 1, 0))
    for t in range(3):
        for r in range(2):
            start_stage(r, t)
    for ds in range(1, 4):
        signal(ready, (s + ds) % 4, g)

    loads = [
        pltpu.make_async_copy(src, dst, load_sem.at[i])
        for i, (src, dst) in enumerate(
            (
                (res_hbm, res_ref),
                (shift_hbm, shift_ref),
                (scale_hbm, scale_ref),
                (gate_hbm, gate_ref),
                (fw_hbm, fw_ref),
                (fb_hbm, fb_ref),
            )
        )
    ]
    for load in loads:
        load.start()
    def slot_of(way, hops):
        if hops in (0, 4):
            return hops
        return hops if way == 0 else 4 + hops

    def part_of(r, t, slot, part):
        rows = NBLK // PARTS[r]
        return bufs[r][t].at[slot, pl.ds(part * rows, rows), :]

    def head_of(h, t, slot):
        if h == 2:
            return k_cols.at[slot] if t == 0 else v_cols.at[slot]
        return bufs[0][t].at[slot, :, pl.ds(h * HD, HD)]

    def hop(r, way, t, part, hops):
        return remote(
            part_of(r, t, slot_of(way, hops - 1), part),
            part_of(r, t, slot_of(way, hops), part),
            ring_send.at[r, way],
            ring_recv.at[r, way, t, part, hops],
            s,
            ways[r][way],
        )

    def last_hop(t, h):
        r = 0 if h < 2 else 1
        return remote(
            head_of(h, t, slot_of(t, 3)),
            head_of(h, t, 4),
            ring_send.at[r, t],
            last_recv.at[t, h],
            s,
            ways[r][t],
        )

    both = slice(0, 2 * NBLK)
    mine = slice(0, NBLK)
    others = slice(NBLK, 2 * NBLK)

    def attend(h, slots, rows, first):
        r, lanes = (1, slice(0, HD)) if h == 2 else (0, slice(h * HD, (h + 1) * HD))
        if rows == both:
            q = jnp.concatenate([queries[r][:, lanes], beside[r][:, lanes]], axis=0)
        else:
            q = (queries if rows == mine else beside)[r][:, lanes]
        scores = [
            lax.dot_general(
                q, head_of(h, 0, slot)[...], (((1,), (1,)), ((), ())), preferred_element_type=F32
            )
            for slot in slots
        ]
        top = functools.reduce(jnp.maximum, scores)
        top = jnp.max(top, axis=1, keepdims=True)
        top = jnp.broadcast_to(top, (q.shape[0], HD))
        if not first:
            old = peak[h, rows]
            top = jnp.maximum(old, top)
        peak[h, rows] = top
        wide = jnp.concatenate([top, top], axis=1)
        part = None
        mixed = None
        for slot, score in zip(slots, scores):
            weights = jnp.exp2((score - wide) * EXP2_SCALE)
            halves = weights[:, :HD] + weights[:, HD:]
            part = halves if part is None else part + halves
            term = jnp.dot(
                weights.astype(BF16), head_of(h, 1, slot)[...], preferred_element_type=F32
            )
            mixed = term if mixed is None else mixed + term
        if first:
            total[h, rows] = part
            acc[h, rows] = mixed
        else:
            fade = jnp.exp2((old - top) * EXP2_SCALE)
            total[h, rows] = total[h, rows] * fade + part
            acc[h, rows] = acc[h, rows] * fade + mixed

    pieces = [(0, 0, 0), (1, 0, 0), (0, 0, 1), (0, 1, 0), (1, 1, 0), (0, 1, 1)]
    for r, t, part in pieces:
        await_bytes(part_of(r, t, 0, part), s1_recv.at[r, t, part])
        for way in range(2):
            hop(r, way, t, part, 1).start()
    for n in range(1, 4):
        for r, t, part in pieces:
            for way in range(2):
                hop(r, way, t, part, n).wait_recv()
                if n < 3:
                    hop(r, way, t, part, n + 1).start()
                elif way == t and part == PARTS[r] - 1:
                    for h in RING_HEADS[r]:
                        last_hop(t, h).start()
        if n == 1:
            for r in range(2):
                await_bytes(queries[r], s1_recv.at[r, 2, 0])
                remote(queries[r], beside[r], q_send.at[r], q_recv.at[r], sibling, g).start()
        if n == 2:
            for r in range(2):
                await_bytes(beside[r], q_recv.at[r])
            for h in range(HG):
                attend(h, (0, 1, 5), both, True)
        if n >= 2:
            for h in range(HG):
                attend(h, (n, 4 + n), both, False)

    def part_copy(h):
        return remote(give.at[h], got.at[h], part_send.at[h], part_recv.at[h], sibling, g)

    first_lanes = lax.broadcasted_iota(jnp.int32, (NBLK, HD), 1) < HD // 2
    for h in range(HG):
        for t in range(2):
            last_hop(t, h).wait_recv()
        attend(h, (4,), others, False)
        give[h, 0] = acc[h, others]
        sums = jnp.sum(total[h, others], axis=1, keepdims=True)
        give[h, 1] = jnp.where(first_lanes, peak[h, others], sums)
        part_copy(h).start()
    for h in range(HG):
        attend(h, (4,), mine, False)

    def home_cols(h):
        return head_cols(z * 2 + h if h < 2 else FIRST_HEAD[1] + y)

    def back_copy(h, place):
        r = 0 if h < 2 else 1
        return remote(
            ob.at[h, block_rows(place), :],
            att.at[:, home_cols(h)],
            o_send.at[h],
            o_recv,
            swap_sec,
            swap_along(r, (along[r] + NEAREST[place]) % NZ),
        )

    for h in range(HG):
        part_copy(h).wait_recv()
        packed = got[h, 1]
        turned = pltpu.roll(packed, HD // 2, axis=1)
        other_peak = jnp.where(first_lanes, packed, turned)
        other_sums = jnp.where(first_lanes, turned, packed)
        own_peak = peak[h, mine]
        top = jnp.maximum(own_peak, other_peak)
        own_fade = jnp.exp2((own_peak - top) * EXP2_SCALE)
        other_fade = jnp.exp2((other_peak - top) * EXP2_SCALE)
        sums = jnp.sum(total[h, mine], axis=1, keepdims=True)
        mixed = acc[h, mine] * own_fade + got[h, 0] * other_fade
        ob[h] = (mixed / (sums * own_fade + other_sums * other_fade)).astype(BF16)
        for place in range(NZ - 1, 0, -1):
            back_copy(h, place).start()

        @pl.when(moves)
        def _(h=h):
            back_copy(h, 0).start()

        @pl.when(stays)
        def _(h=h):
            pltpu.make_async_copy(
                ob.at[h, block_rows(0), :], att.at[:, home_cols(h)], o_recv
            ).start()

    def sent_blocks(ref, sem):
        @pl.when(moves)
        def _():
            await_bytes(ref, sem)

        @pl.when(stays)
        def _():
            await_bytes(ref.at[pl.ds(0, NBLK - TOK), :], sem)

    for r in range(2):
        for t in range(3):
            sent_blocks(queries[r], s1_send.at[r, t])
        for way in range(2):
            await_bytes(bufs[r][0].at[pl.ds(0, 7)], ring_send.at[r, way])
        await_bytes(queries[r], q_send.at[r])
    for h in range(HG):
        part_copy(h).wait_send()
    for load in loads:
        load.wait()
    await_bytes(att, o_recv)

    hidden = res_ref[...].astype(F32) + gate_ref[...] * att[...].astype(F32)
    center = hidden - jnp.mean(hidden, axis=1, keepdims=True)
    normed = center * lax.rsqrt(jnp.mean(center * center, axis=1, keepdims=True) + norm_eps)
    modulated = (normed * (1.0 + scale_ref[...]) + shift_ref[...]).astype(BF16)
    patches = (
        lax.dot_general(
            modulated, fw_ref[...], (((1,), (1,)), ((), ())), preferred_element_type=F32
        )
        + fb_ref[...]
    ) / scaling
    pat[...] = patches.astype(BF16).astype(F32)
    even = pat[pl.ds(0, F, stride=2), :]
    odd = pat[pl.ds(1, F, stride=2), :]
    side = 2 * LATC
    tile = jnp.concatenate([even[:, :side], odd[:, :side], even[:, side:], odd[:, side:]], axis=1)
    tiles[0, 0:1, :] = tile[:1]
    tiles[0, 1:2, :] = tile[:1]
    tiles[0, 2:8, :] = tile[:6]
    for part in (1, 2):
        tiles[part] = tile[4 * part - 2 : 4 * part + 6]
    tiles[3, 0:6, :] = tile[10:16]
    tiles[3, 6:8, :] = tile[14:16]

    pl.semaphore_wait(ready, 3)
    for dy, dx in AROUND:
        place = (1 - dy) * 3 + 1 - dx
        for ds in range(4):
            if (dy, dx, ds) != (0, 0, 0):
                sp = (s + ds) % 4
                remote(
                    tiles.at[sp],
                    near_tiles.at[place * 4 + s],
                    halo_send,
                    halo_recv,
                    sp,
                    tile_seq(dy, dx),
                ).start()
    near_tiles[4 * 4 + s] = tiles[s]
    for h in range(HG):
        sent_blocks(ob.at[h], o_send.at[h])
    await_bytes(near_tiles.at[pl.ds(0, 35)], halo_recv)

    def clear(at_edge, gone):
        @pl.when(at_edge)
        def _():
            for place in gone:
                near_tiles[place * 4 : place * 4 + 4] = jnp.zeros((4, 8, 128), F32)

    clear(z == 0, (0, 1, 2))
    clear(z == NZ - 1, (6, 7, 8))
    clear(col == 0, (0, 3, 6))
    clear(col == 2 * NY - 1, (2, 5, 8))

    for yy in range(4):
        vert, dr = ((0, 1), (1, 0), (1, 1), (2, 0))[yy]
        lo = dr * BC * LATC
        hi = lo + BC * LATC
        sides = [
            near_tiles[(vert * 3 + dx) * 4 : (vert * 3 + dx) * 4 + 4].reshape(32, 128)
            for dx in range(3)
        ]
        strip = jnp.concatenate(
            [
                sides[0][:, hi - LATC : hi],
                sides[1][:, lo:hi],
                sides[2][:, lo : lo + LATC],
                jnp.zeros((32, 2 * LATC), F32),
            ],
            axis=1,
        )
        for x in range(BC):
            moved = strip if x == 0 else pltpu.roll(strip, 128 - x * LATC, axis=1)
            moved = moved.reshape(4, 8, 128)
            for dt in range(3):
                piece = moved[:, dt : dt + 4, :].reshape(16, 128)
                for dy in range(3):
                    row = yy - dy
                    if 0 <= row < BR:
                        windows[dt * 3 + dy, pl.ds(row * BC + x, 16, stride=8), :] = piece
    taps = [windows[tap][:, : 3 * LATC] for tap in range(9)]
    out_ref[...] = jnp.concatenate(taps, axis=1).astype(BF16)

    await_bytes(near_tiles.at[pl.ds(0, 35)], halo_send)


def on_device(
    queries,
    keys,
    values,
    residual,
    shift_mod,
    scale_mod,
    gate_mod,
    final_weight,
    final_bias,
    conv_weight,
    conv_bias,
    group_gain,
    group_bias,
):
    any_spec = pl.BlockSpec(memory_space=pl.ANY)
    dma = pltpu.SemaphoreType.DMA
    vae_width = conv_weight.shape[1]
    kin = conv_weight.shape[0]
    columns = pl.pallas_call(
        whole_kernel,
        out_shape=jax.ShapeDtypeStruct((4 * 4 * BR * BC, kin), BF16),
        in_specs=[any_spec] * 9,
        out_specs=pl.BlockSpec(memory_space=pltpu.VMEM),
        scratch_shapes=[
            pltpu.VMEM((NBLK, 2 * HD), BF16),
            pltpu.VMEM((NBLK, 2 * HD), BF16),
            pltpu.VMEM((8, NBLK, 2 * HD), BF16),
            pltpu.VMEM((8, NBLK, 2 * HD), BF16),
            pltpu.VMEM((NBLK, HD), BF16),
            pltpu.VMEM((NBLK, HD), BF16),
            pltpu.VMEM((8, NBLK, HD), BF16),
            pltpu.VMEM((8, NBLK, HD), BF16),
            pltpu.VMEM((HG, NBLK, HD), BF16),
            pltpu.VMEM((TOK, H * HD), BF16),
            pltpu.VMEM((HG, 2 * NBLK, HD), F32),
            pltpu.VMEM((HG, 2 * NBLK, HD), F32),
            pltpu.VMEM((HG, 2 * NBLK, HD), F32),
            pltpu.VMEM((HG, 2, NBLK, HD), F32),
            pltpu.VMEM((HG, 2, NBLK, HD), F32),
            pltpu.VMEM((TOK, 4 * LATC), F32),
            pltpu.VMEM((4, 8, 128), F32),
            pltpu.VMEM((36, 8, 128), F32),
            pltpu.VMEM((9, 4 * 4 * BR * BC, 128), F32),
            pltpu.VMEM((TOK, H * HD), BF16),
            pltpu.VMEM((1, H * HD), F32),
            pltpu.VMEM((1, H * HD), F32),
            pltpu.VMEM((1, H * HD), F32),
            pltpu.VMEM((4 * LATC, H * HD), BF16),
            pltpu.VMEM((1, 4 * LATC), F32),
            dma((6,)),
            dma((2, 3)),
            dma((2, 3, 2)),
            dma((2, 2)),
            dma((2, 2, 2, 2, 4)),
            dma((2, HG)),
            dma((2,)),
            dma((2,)),
            dma((HG,)),
            dma((HG,)),
            dma((HG,)),
            dma(()),
            dma(()),
            dma(()),
            pltpu.SemaphoreType.REGULAR,
        ],
        compiler_params=pltpu.CompilerParams(
            collective_id=0, has_side_effects=True, vmem_limit_bytes=60 * 1024 * 1024
        ),
        name="whole",
    )(
        queries[0],
        keys[0],
        values[0],
        residual[0],
        shift_mod,
        scale_mod,
        gate_mod,
        final_weight.T,
        final_bias[None],
    )
    conv_out = jnp.dot(columns, conv_weight, preferred_element_type=F32) + conv_bias
    features = jax.nn.silu(conv_out * group_gain + group_bias).astype(BF16)
    return features.reshape(4, 4, 1, BR * BC, vae_width)


def solution(mesh):
    return jax.shard_map(
        on_device,
        mesh=mesh,
        in_specs=(
            P("sec", "seq", None),
            P("sec", "seq", None),
            P("sec", "seq", None),
            P("sec", "seq", None),
            P("sec", None),
            P("sec", None),
            P("sec", None),
            P(),
            P(),
            P(),
            P(),
            P(),
            P(),
        ),
        out_specs=P(None, "sec", "seq", None, None),
        check_vma=False,
    )
```

```python
import functools

import jax
import jax.numpy as jnp
from jax import lax
from jax.experimental import pallas as pl
from jax.experimental.pallas import tpu as pltpu
from jax.sharding import PartitionSpec as P

H = 24
HD = 128
LATC = 16
F = 16
BR = 2
BC = 4
NZ = 8
NY = 8
TOK = 32
HG = 3
NBLK = NZ * TOK

scaling = 0.476986
norm_eps = 1e-06
EXP2_SCALE = HD ** (-0.5) * 1.4426950408889634
F32 = jnp.float32
BF16 = jnp.bfloat16


def remote(src, dst, send_sem, recv_sem, sec, seq):
    return pltpu.make_async_remote_copy(
        src_ref=src,
        dst_ref=dst,
        send_sem=send_sem,
        recv_sem=recv_sem,
        device_id={"sec": sec, "seq": seq},
        device_id_type=pl.DeviceIdType.MESH,
    )


def signal(sem, sec, seq):
    pl.semaphore_signal(
        sem, inc=1, device_id={"sec": sec, "seq": seq}, device_id_type=pl.DeviceIdType.MESH
    )


def position():
    s = lax.axis_index("sec")
    g = lax.axis_index("seq")
    return s, g, s % 2, s // 2, g // (2 * NY), (g // 2) % NY, g % 2

NEAREST = (0, 1, 7, 2, 6, 3, 5, 4)
AROUND = [(dy, dx) for dy in (-1, 0, 1) for dx in (-1, 0, 1)]

RING_HEADS = ((0, 1), (2,))
FIRST_HEAD = (0, 2 * NZ)
PARTS = (2, 1)
WIDTH = (2 * HD, HD)


def whole_kernel(
    q_ref,
    k_ref,
    v_ref,
    res_hbm,
    shift_hbm,
    scale_hbm,
    gate_hbm,
    fw_hbm,
    fb_hbm,
    cw_hbm,
    cb_hbm,
    gg_hbm,
    gb_hbm,
    out_ref,
    q_rows,
    q_rows_beside,
    k_rows,
    v_rows,
    q_cols,
    q_cols_beside,
    k_cols,
    v_cols,
    ob,
    att,
    peak,
    total,
    acc,
    give,
    got,
    pat,
    tiles,
    near_tiles,
    windows,
    res_ref,
    shift_ref,
    scale_ref,
    gate_ref,
    fw_ref,
    fb_ref,
    cw_ref,
    cb_ref,
    gg_ref,
    gb_ref,
    load_sem,
    cw_sem,
    s1_send,
    s1_recv,
    ring_send,
    ring_recv,
    last_recv,
    q_send,
    q_recv,
    part_send,
    part_recv,
    o_send,
    o_recv,
    halo_send,
    halo_recv,
    ready,
):
    s, g, core, xl, z, y, xh = position()
    stays = core == xh
    moves = jnp.logical_not(stays)
    swap_sec = xl * 2 + xh
    sibling = xl * 2 + 1 - core
    col = y * 2 + xh

    def swap_seq(zp, yp):
        return (zp * NY + yp) * 2 + core

    def ring_seq(yp):
        return (z * NY + yp) * 2 + xh

    ways = (
        (ring_seq((y + 1) % NY), ring_seq((y + NY - 1) % NY)),
        (
            ((z + 1) % NZ * NY + y) * 2 + xh,
            ((z + NZ - 1) % NZ * NY + y) * 2 + xh,
        ),
    )
    along = (z, y)

    neighbours = [(dy, dx) for dy, dx in AROUND if (dy, dx) != (0, 0)]

    def tile_seq(dy, dx):
        return (z + NZ + dy) % NZ * (2 * NY) + (col + 2 * NY + dx) % (2 * NY)

    barrier = pltpu.get_barrier_semaphore()
    for e in NEAREST[1:]:
        signal(barrier, swap_sec, swap_seq((z + e) % NZ, y))

    @pl.when(moves)
    def _():
        signal(barrier, swap_sec, swap_seq(z, y))

    for e in NEAREST[1:]:
        signal(barrier, swap_sec, swap_seq(z, (y + e) % NY))
    for r in range(2):
        for way in range(2):
            signal(barrier, s, ways[r][way])
    for ds in range(1, 4):
        signal(barrier, (s + ds) % 4, g)
    for dy, dx in neighbours:
        signal(barrier, s, tile_seq(dy, dx))

    def group_cols(r, group):
        first = FIRST_HEAD[r] * HD + group * WIDTH[r]
        return pl.ds(pl.multiple_of(first, HD), WIDTH[r])

    def head_cols(h):
        return pl.ds(pl.multiple_of(h * HD, HD), HD)

    def swap_along(r, group):
        return swap_seq(group, y) if r == 0 else swap_seq(z, group)

    def block_rows(place):
        return pl.ds(place * TOK, TOK)

    def await_bytes(ref, sem):
        pltpu.make_async_copy(ref, ref, sem).wait()

    sources = (k_ref, v_ref, q_ref)
    queries = (q_rows, q_cols)
    beside = (q_rows_beside, q_cols_beside)
    bufs = ((k_rows, v_rows), (k_cols, v_cols))

    def landing(r, t):
        return queries[r] if t == 2 else bufs[r][t].at[0]

    def stage_sem(r, t, place):
        return s1_recv.at[r, t, 0 if t == 2 else place * PARTS[r] // NZ]

    def stage_copy(r, t, place):
        group = (along[r] + NZ - NEAREST[place]) % NZ
        return remote(
            sources[t].at[:, group_cols(r, group)],
            landing(r, t).at[block_rows(place), :],
            s1_send.at[r, t],
            stage_sem(r, t, place),
            swap_sec,
            swap_along(r, group),
        )

    def start_stage(r, t):
        @pl.when(stays)
        def _():
            pltpu.make_async_copy(
                sources[t].at[:, group_cols(r, along[r])],
                landing(r, t).at[block_rows(0), :],
                stage_sem(r, t, 0),
            ).start()

        @pl.when(moves)
        def _():
            stage_copy(r, t, 0).start()

        for place in range(1, NZ):
            stage_copy(r, t, place).start()

    pl.semaphore_wait(barrier, 3 * NZ + 6 - jnp.where(stays, 1, 0))
    for t in range(2):
        for r in range(2):
            start_stage(r, t)
    for ds in range(1, 4):
        signal(ready, (s + ds) % 4, g)

    loads = [
        pltpu.make_async_copy(src, dst, load_sem.at[i])
        for i, (src, dst) in enumerate(
            (
                (res_hbm, res_ref),
                (shift_hbm, shift_ref),
                (scale_hbm, scale_ref),
                (gate_hbm, gate_ref),
                (fw_hbm, fw_ref),
                (fb_hbm, fb_ref),
                (cb_hbm, cb_ref),
                (gg_hbm, gg_ref),
                (gb_hbm, gb_ref),
            )
        )
    ]
    for load in loads:
        load.start()
    for tap in range(9):
        pltpu.make_async_copy(
            cw_hbm.at[pl.ds(tap * 48, 48), :], cw_ref.at[tap, pl.ds(0, 48), :], cw_sem
        ).start()

    def slot_of(way, hops):
        if hops in (0, 4):
            return hops
        return hops if way == 0 else 4 + hops

    def part_of(r, t, slot, part):
        rows = NBLK // PARTS[r]
        return bufs[r][t].at[slot, pl.ds(part * rows, rows), :]

    def head_of(h, t, slot):
        if h == 2:
            return k_cols.at[slot] if t == 0 else v_cols.at[slot]
        return bufs[0][t].at[slot, :, pl.ds(h * HD, HD)]

    def hop(r, way, t, part, hops):
        return remote(
            part_of(r, t, slot_of(way, hops - 1), part),
            part_of(r, t, slot_of(way, hops), part),
            ring_send.at[r, way],
            ring_recv.at[r, way, t, part, hops],
            s,
            ways[r][way],
        )

    def last_hop(t, h):
        r = 0 if h < 2 else 1
        return remote(
            head_of(h, t, slot_of(t, 3)),
            head_of(h, t, 4),
            ring_send.at[r, t],
            last_recv.at[t, h],
            s,
            ways[r][t],
        )

    both = slice(0, 2 * NBLK)
    mine = slice(0, NBLK)
    others = slice(NBLK, 2 * NBLK)

    def attend(h, slots, rows, first):
        r, lanes = (1, slice(0, HD)) if h == 2 else (0, slice(h * HD, (h + 1) * HD))
        if rows == both:
            q = jnp.concatenate([queries[r][:, lanes], beside[r][:, lanes]], axis=0)
        else:
            q = (queries if rows == mine else beside)[r][:, lanes]
        scores = [
            lax.dot_general(
                q, head_of(h, 0, slot)[...], (((1,), (1,)), ((), ())), preferred_element_type=F32
            )
            for slot in slots
        ]
        top = functools.reduce(jnp.maximum, scores)
        top = jnp.max(top, axis=1, keepdims=True)
        top = jnp.broadcast_to(top, (q.shape[0], HD))
        if not first:
            old = peak[h, rows]
            top = jnp.maximum(old, top)
        peak[h, rows] = top
        wide = jnp.concatenate([top, top], axis=1)
        part = None
        mixed = None
        for slot, score in zip(slots, scores):
            weights = jnp.exp2((score - wide) * EXP2_SCALE)
            halves = weights[:, :HD] + weights[:, HD:]
            part = halves if part is None else part + halves
            term = jnp.dot(
                weights.astype(BF16), head_of(h, 1, slot)[...], preferred_element_type=F32
            )
            mixed = term if mixed is None else mixed + term
        if first:
            total[h, rows] = part
            acc[h, rows] = mixed
        else:
            fade = jnp.exp2((old - top) * EXP2_SCALE)
            total[h, rows] = total[h, rows] * fade + part
            acc[h, rows] = acc[h, rows] * fade + mixed

    for r, t, part in [(0, 0, 0), (1, 0, 0), (0, 0, 1), (1, 1, 0), (0, 1, 0), (0, 1, 1)]:
        await_bytes(part_of(r, t, 0, part), s1_recv.at[r, t, part])
        for way in range(2):
            hop(r, way, t, part, 1).start()
        if (r, t) == (1, 1):
            for q_ring in range(2):
                start_stage(q_ring, 2)
    pieces = [(0, 0, 0), (0, 0, 1), (0, 1, 0), (0, 1, 1), (1, 0, 0), (1, 1, 0)]
    cw_ref[:, 48:, :] = jnp.zeros((9, 80, cw_ref.shape[2]), BF16)
    for n in range(1, 4):
        for r, t, part in pieces:
            for way in range(2):
                hop(r, way, t, part, n).wait_recv()
                if n < 3:
                    hop(r, way, t, part, n + 1).start()
                elif way == t and part == PARTS[r] - 1:
                    for h in RING_HEADS[r]:
                        last_hop(t, h).start()
        if n == 1:
            for r in range(2):
                await_bytes(queries[r], s1_recv.at[r, 2, 0])
                remote(queries[r], beside[r], q_send.at[r], q_recv.at[r], sibling, g).start()
        if n == 2:
            for r in range(2):
                await_bytes(beside[r], q_recv.at[r])
            for h in range(HG):
                attend(h, (0, 1, 5), both, True)
        if n >= 2:
            for h in range(HG):
                attend(h, (n, 4 + n), both, False)

    def part_copy(h):
        return remote(give.at[h], got.at[h], part_send.at[h], part_recv.at[h], sibling, g)

    first_lanes = lax.broadcasted_iota(jnp.int32, (NBLK, HD), 1) < HD // 2
    for h in range(HG):
        for t in range(2):
            last_hop(t, h).wait_recv()
        attend(h, (4,), others, False)
        give[h, 0] = acc[h, others]
        sums = jnp.sum(total[h, others], axis=1, keepdims=True)
        give[h, 1] = jnp.where(first_lanes, peak[h, others], sums)
        part_copy(h).start()
    for h in range(HG):
        attend(h, (4,), mine, False)

    def home_cols(h):
        return head_cols(z * 2 + h if h < 2 else FIRST_HEAD[1] + y)

    def back_copy(h, place):
        r = 0 if h < 2 else 1
        return remote(
            ob.at[h, block_rows(place), :],
            att.at[:, home_cols(h)],
            o_send.at[h],
            o_recv,
            swap_sec,
            swap_along(r, (along[r] + NEAREST[place]) % NZ),
        )

    for h in range(HG):
        part_copy(h).wait_recv()
        packed = got[h, 1]
        turned = pltpu.roll(packed, HD // 2, axis=1)
        other_peak = jnp.where(first_lanes, packed, turned)
        other_sums = jnp.where(first_lanes, turned, packed)
        own_peak = peak[h, mine]
        top = jnp.maximum(own_peak, other_peak)
        own_fade = jnp.exp2((own_peak - top) * EXP2_SCALE)
        other_fade = jnp.exp2((other_peak - top) * EXP2_SCALE)
        sums = jnp.sum(total[h, mine], axis=1, keepdims=True)
        mixed = acc[h, mine] * own_fade + got[h, 0] * other_fade
        ob[h] = (mixed / (sums * own_fade + other_sums * other_fade)).astype(BF16)
        for place in range(NZ - 1, 0, -1):
            back_copy(h, place).start()

        @pl.when(moves)
        def _(h=h):
            back_copy(h, 0).start()

        @pl.when(stays)
        def _(h=h):
            pltpu.make_async_copy(
                ob.at[h, block_rows(0), :], att.at[:, home_cols(h)], o_recv
            ).start()

    def sent_blocks(ref, sem):
        @pl.when(moves)
        def _():
            await_bytes(ref, sem)

        @pl.when(stays)
        def _():
            await_bytes(ref.at[pl.ds(0, NBLK - TOK), :], sem)

    for r in range(2):
        for t in range(3):
            sent_blocks(queries[r], s1_send.at[r, t])
        for way in range(2):
            await_bytes(bufs[r][0].at[pl.ds(0, 7)], ring_send.at[r, way])
        await_bytes(queries[r], q_send.at[r])
    for h in range(HG):
        part_copy(h).wait_send()
    for load in loads:
        load.wait()
    await_bytes(att, o_recv)

    hidden = res_ref[...].astype(F32) + gate_ref[...] * att[...].astype(F32)
    center = hidden - jnp.mean(hidden, axis=1, keepdims=True)
    normed = center * lax.rsqrt(jnp.mean(center * center, axis=1, keepdims=True) + norm_eps)
    modulated = (normed * (1.0 + scale_ref[...]) + shift_ref[...]).astype(BF16)
    patches = (
        lax.dot_general(
            modulated, fw_ref[...], (((1,), (1,)), ((), ())), preferred_element_type=F32
        )
        + fb_ref[...]
    ) / scaling
    pat[...] = patches.astype(BF16).astype(F32)
    even = pat[pl.ds(0, F, stride=2), :]
    odd = pat[pl.ds(1, F, stride=2), :]
    side = 2 * LATC
    tile = jnp.concatenate([even[:, :side], odd[:, :side], even[:, side:], odd[:, side:]], axis=1)
    tiles[0, 0:1, :] = tile[:1]
    tiles[0, 1:2, :] = tile[:1]
    tiles[0, 2:8, :] = tile[:6]
    for part in (1, 2):
        tiles[part] = tile[4 * part - 2 : 4 * part + 6]
    tiles[3, 0:6, :] = tile[10:16]
    tiles[3, 6:8, :] = tile[14:16]

    pl.semaphore_wait(ready, 3)
    for dy, dx in AROUND:
        place = (1 - dy) * 3 + 1 - dx
        for ds in range(4):
            if (dy, dx, ds) != (0, 0, 0):
                sp = (s + ds) % 4
                remote(
                    tiles.at[sp],
                    near_tiles.at[place * 4 + s],
                    halo_send,
                    halo_recv,
                    sp,
                    tile_seq(dy, dx),
                ).start()
    near_tiles[4 * 4 + s] = tiles[s]
    for h in range(HG):
        sent_blocks(ob.at[h], o_send.at[h])
    await_bytes(near_tiles.at[pl.ds(0, 35)], halo_recv)

    def clear(at_edge, gone):
        @pl.when(at_edge)
        def _():
            for place in gone:
                near_tiles[place * 4 : place * 4 + 4] = jnp.zeros((4, 8, 128), F32)

    clear(z == 0, (0, 1, 2))
    clear(z == NZ - 1, (6, 7, 8))
    clear(col == 0, (0, 3, 6))
    clear(col == 2 * NY - 1, (2, 5, 8))

    for yy in range(4):
        vert, dr = ((0, 1), (1, 0), (1, 1), (2, 0))[yy]
        lo = dr * BC * LATC
        hi = lo + BC * LATC
        sides = [
            near_tiles[(vert * 3 + dx) * 4 : (vert * 3 + dx) * 4 + 4].reshape(32, 128)
            for dx in range(3)
        ]
        strip = jnp.concatenate(
            [
                sides[0][:, hi - LATC : hi],
                sides[1][:, lo:hi],
                sides[2][:, lo : lo + LATC],
                jnp.zeros((32, 2 * LATC), F32),
            ],
            axis=1,
        )
        for x in range(BC):
            moved = strip if x == 0 else pltpu.roll(strip, 128 - x * LATC, axis=1)
            moved = moved.reshape(4, 8, 128)
            for dt in range(3):
                piece = moved[:, dt : dt + 4, :].reshape(16, 128)
                for dy in range(3):
                    row = yy - dy
                    if 0 <= row < BR:
                        windows[dt * 3 + dy, pl.ds(row * BC + x, 16, stride=8), :] = piece
    await_bytes(cw_ref.at[:, pl.ds(0, 48), :], cw_sem)
    left_side = jnp.concatenate([windows[tap].astype(BF16) for tap in range(9)], axis=1)
    conv = jnp.dot(
        left_side, cw_ref[...].reshape(9 * 128, cw_ref.shape[2]), preferred_element_type=F32
    )
    conv = (conv + cb_ref[...]) * gg_ref[...] + gb_ref[...]
    out_ref[...] = (conv / (1.0 + jnp.exp(-conv))).astype(BF16)

    await_bytes(near_tiles.at[pl.ds(0, 35)], halo_send)


def on_device(
    queries,
    keys,
    values,
    residual,
    shift_mod,
    scale_mod,
    gate_mod,
    final_weight,
    final_bias,
    conv_weight,
    conv_bias,
    group_gain,
    group_bias,
):
    any_spec = pl.BlockSpec(memory_space=pl.ANY)
    dma = pltpu.SemaphoreType.DMA
    vae_width = conv_weight.shape[1]
    features = pl.pallas_call(
        whole_kernel,
        out_shape=jax.ShapeDtypeStruct((4 * 4 * BR * BC, vae_width), BF16),
        in_specs=[any_spec] * 13,
        out_specs=pl.BlockSpec(memory_space=pltpu.VMEM),
        scratch_shapes=[
            pltpu.VMEM((NBLK, 2 * HD), BF16),
            pltpu.VMEM((NBLK, 2 * HD), BF16),
            pltpu.VMEM((8, NBLK, 2 * HD), BF16),
            pltpu.VMEM((8, NBLK, 2 * HD), BF16),
            pltpu.VMEM((NBLK, HD), BF16),
            pltpu.VMEM((NBLK, HD), BF16),
            pltpu.VMEM((8, NBLK, HD), BF16),
            pltpu.VMEM((8, NBLK, HD), BF16),
            pltpu.VMEM((HG, NBLK, HD), BF16),
            pltpu.VMEM((TOK, H * HD), BF16),
            pltpu.VMEM((HG, 2 * NBLK, HD), F32),
            pltpu.VMEM((HG, 2 * NBLK, HD), F32),
            pltpu.VMEM((HG, 2 * NBLK, HD), F32),
            pltpu.VMEM((HG, 2, NBLK, HD), F32),
            pltpu.VMEM((HG, 2, NBLK, HD), F32),
            pltpu.VMEM((TOK, 4 * LATC), F32),
            pltpu.VMEM((4, 8, 128), F32),
            pltpu.VMEM((36, 8, 128), F32),
            pltpu.VMEM((9, 4 * 4 * BR * BC, 128), F32),
            pltpu.VMEM((TOK, H * HD), BF16),
            pltpu.VMEM((1, H * HD), F32),
            pltpu.VMEM((1, H * HD), F32),
            pltpu.VMEM((1, H * HD), F32),
            pltpu.VMEM((4 * LATC, H * HD), BF16),
            pltpu.VMEM((1, 4 * LATC), F32),
            pltpu.VMEM((9, 128, vae_width), BF16),
            pltpu.VMEM((1, vae_width), F32),
            pltpu.VMEM((1, vae_width), F32),
            pltpu.VMEM((1, vae_width), F32),
            dma((9,)),
            dma(()),
            dma((2, 3)),
            dma((2, 3, 2)),
            dma((2, 2)),
            dma((2, 2, 2, 2, 4)),
            dma((2, HG)),
            dma((2,)),
            dma((2,)),
            dma((HG,)),
            dma((HG,)),
            dma((HG,)),
            dma(()),
            dma(()),
            dma(()),
            pltpu.SemaphoreType.REGULAR,
        ],
        compiler_params=pltpu.CompilerParams(
            collective_id=0, has_side_effects=True, vmem_limit_bytes=60 * 1024 * 1024
        ),
        name="whole",
    )(
        queries[0],
        keys[0],
        values[0],
        residual[0],
        shift_mod,
        scale_mod,
        gate_mod,
        final_weight.T,
        final_bias[None],
        conv_weight,
        conv_bias[None],
        group_gain[None],
        group_bias[None],
    )
    return features.reshape(4, 4, 1, BR * BC, vae_width)


def solution(mesh):
    return jax.shard_map(
        on_device,
        mesh=mesh,
        in_specs=(
            P("sec", "seq", None),
            P("sec", "seq", None),
            P("sec", "seq", None),
            P("sec", "seq", None),
            P("sec", None),
            P("sec", None),
            P("sec", None),
            P(),
            P(),
            P(),
            P(),
            P(),
            P(),
        ),
        out_specs=P(None, "sec", "seq", None, None),
        check_vma=False,
    )
```

```python
import functools

import jax
import jax.numpy as jnp
from jax import lax
from jax.experimental import pallas as pl
from jax.experimental.pallas import tpu as pltpu
from jax.sharding import PartitionSpec as P

H = 24
HD = 128
LATC = 16
F = 16
BR = 2
BC = 4
NZ = 8
NY = 8
TOK = 32
HG = 3
NBLK = NZ * TOK

scaling = 0.476986
norm_eps = 1e-06
EXP2_SCALE = HD ** (-0.5) * 1.4426950408889634
F32 = jnp.float32
BF16 = jnp.bfloat16


def remote(src, dst, send_sem, recv_sem, sec, seq):
    return pltpu.make_async_remote_copy(
        src_ref=src,
        dst_ref=dst,
        send_sem=send_sem,
        recv_sem=recv_sem,
        device_id={"sec": sec, "seq": seq},
        device_id_type=pl.DeviceIdType.MESH,
    )


def signal(sem, sec, seq):
    pl.semaphore_signal(
        sem, inc=1, device_id={"sec": sec, "seq": seq}, device_id_type=pl.DeviceIdType.MESH
    )


def position():
    s = lax.axis_index("sec")
    g = lax.axis_index("seq")
    return s, g, s % 2, s // 2, g // (2 * NY), (g // 2) % NY, g % 2

NEAREST = (0, 1, 7, 2, 6, 3, 5, 4)
AROUND = [(dy, dx) for dy in (-1, 0, 1) for dx in (-1, 0, 1)]

RING_HEADS = ((0, 1), (2,))
FIRST_HEAD = (0, 2 * NZ)
PARTS = (2, 1)
WIDTH = (2 * HD, HD)


def whole_kernel(
    q_ref,
    k_ref,
    v_ref,
    res_hbm,
    shift_hbm,
    scale_hbm,
    gate_hbm,
    fw_hbm,
    fb_hbm,
    cw_hbm,
    cb_hbm,
    gg_hbm,
    gb_hbm,
    out_ref,
    q_rows,
    q_rows_beside,
    k_rows,
    v_rows,
    q_cols,
    q_cols_beside,
    k_cols,
    v_cols,
    ob,
    att,
    peak,
    total,
    acc,
    give,
    got,
    give_stats,
    got_stats,
    pat,
    tiles,
    near_tiles,
    windows,
    res_ref,
    shift_ref,
    scale_ref,
    gate_ref,
    fw_ref,
    fb_ref,
    cw_ref,
    cb_ref,
    gg_ref,
    gb_ref,
    load_sem,
    cw_sem,
    s1_send,
    s1_recv,
    ring_send,
    ring_recv,
    last_recv,
    q_send,
    q_recv,
    part_send,
    part_recv,
    o_send,
    o_recv,
    halo_send,
    halo_recv,
    ready,
):
    s, g, core, xl, z, y, xh = position()
    stays = core == xh
    moves = jnp.logical_not(stays)
    swap_sec = xl * 2 + xh
    sibling = xl * 2 + 1 - core
    col = y * 2 + xh

    def swap_seq(zp, yp):
        return (zp * NY + yp) * 2 + core

    def ring_seq(yp):
        return (z * NY + yp) * 2 + xh

    ways = (
        (ring_seq((y + 1) % NY), ring_seq((y + NY - 1) % NY)),
        (
            ((z + 1) % NZ * NY + y) * 2 + xh,
            ((z + NZ - 1) % NZ * NY + y) * 2 + xh,
        ),
    )
    along = (z, y)

    neighbours = [(dy, dx) for dy, dx in AROUND if (dy, dx) != (0, 0)]

    def tile_seq(dy, dx):
        return (z + NZ + dy) % NZ * (2 * NY) + (col + 2 * NY + dx) % (2 * NY)

    barrier = pltpu.get_barrier_semaphore()
    for e in NEAREST[1:]:
        signal(barrier, swap_sec, swap_seq((z + e) % NZ, y))

    @pl.when(moves)
    def _():
        signal(barrier, swap_sec, swap_seq(z, y))

    for e in NEAREST[1:]:
        signal(barrier, swap_sec, swap_seq(z, (y + e) % NY))
    for r in range(2):
        for way in range(2):
            signal(barrier, s, ways[r][way])
    for ds in range(1, 4):
        signal(barrier, (s + ds) % 4, g)
    for dy, dx in neighbours:
        signal(barrier, s, tile_seq(dy, dx))

    def group_cols(r, group):
        first = FIRST_HEAD[r] * HD + group * WIDTH[r]
        return pl.ds(pl.multiple_of(first, HD), WIDTH[r])

    def head_cols(h):
        return pl.ds(pl.multiple_of(h * HD, HD), HD)

    def swap_along(r, group):
        return swap_seq(group, y) if r == 0 else swap_seq(z, group)

    def block_rows(place):
        return pl.ds(place * TOK, TOK)

    def await_bytes(ref, sem):
        pltpu.make_async_copy(ref, ref, sem).wait()

    sources = (k_ref, v_ref, q_ref)
    queries = (q_rows, q_cols)
    beside = (q_rows_beside, q_cols_beside)
    bufs = ((k_rows, v_rows), (k_cols, v_cols))

    def landing(r, t):
        return queries[r] if t == 2 else bufs[r][t].at[0]

    def stage_sem(r, t, place):
        return s1_recv.at[r, t, 0 if t == 2 else place * PARTS[r] // NZ]

    def stage_copy(r, t, place):
        group = (along[r] + NZ - NEAREST[place]) % NZ
        return remote(
            sources[t].at[:, group_cols(r, group)],
            landing(r, t).at[block_rows(place), :],
            s1_send.at[r, t],
            stage_sem(r, t, place),
            swap_sec,
            swap_along(r, group),
        )

    def start_stage(r, t):
        @pl.when(stays)
        def _():
            pltpu.make_async_copy(
                sources[t].at[:, group_cols(r, along[r])],
                landing(r, t).at[block_rows(0), :],
                stage_sem(r, t, 0),
            ).start()

        @pl.when(moves)
        def _():
            stage_copy(r, t, 0).start()

        for place in range(1, NZ):
            stage_copy(r, t, place).start()

    pl.semaphore_wait(barrier, 3 * NZ + 6 - jnp.where(stays, 1, 0))
    for t in range(3):
        for r in range(2):
            start_stage(r, t)
    for ds in range(1, 4):
        signal(ready, (s + ds) % 4, g)

    loads = [
        pltpu.make_async_copy(src, dst, load_sem.at[i])
        for i, (src, dst) in enumerate(
            (
                (res_hbm, res_ref),
                (shift_hbm, shift_ref),
                (scale_hbm, scale_ref),
                (gate_hbm, gate_ref),
                (fw_hbm, fw_ref),
                (fb_hbm, fb_ref),
                (cb_hbm, cb_ref),
                (gg_hbm, gg_ref),
                (gb_hbm, gb_ref),
            )
        )
    ]
    for load in loads:
        load.start()
    for tap in range(9):
        pltpu.make_async_copy(
            cw_hbm.at[pl.ds(tap * 48, 48), :], cw_ref.at[tap, pl.ds(0, 48), :], cw_sem
        ).start()

    def slot_of(way, hops):
        if hops in (0, 4):
            return hops
        return hops if way == 0 else 4 + hops

    def part_of(r, t, slot, part):
        rows = NBLK // PARTS[r]
        return bufs[r][t].at[slot, pl.ds(part * rows, rows), :]

    def head_of(h, t, slot):
        if h == 2:
            return k_cols.at[slot] if t == 0 else v_cols.at[slot]
        return bufs[0][t].at[slot, :, pl.ds(h * HD, HD)]

    def hop(r, way, t, part, hops):
        return remote(
            part_of(r, t, slot_of(way, hops - 1), part),
            part_of(r, t, slot_of(way, hops), part),
            ring_send.at[r, way],
            ring_recv.at[r, way, t, part, hops],
            s,
            ways[r][way],
        )

    def last_hop(t, h):
        r = 0 if h < 2 else 1
        return remote(
            head_of(h, t, slot_of(t, 3)),
            head_of(h, t, 4),
            ring_send.at[r, t],
            last_recv.at[t, h],
            s,
            ways[r][t],
        )

    both = slice(0, 2 * NBLK)
    mine = slice(0, NBLK)
    others = slice(NBLK, 2 * NBLK)

    def attend(h, slots, rows, first):
        r, lanes = (1, slice(0, HD)) if h == 2 else (0, slice(h * HD, (h + 1) * HD))
        if rows == both:
            q = jnp.concatenate([queries[r][:, lanes], beside[r][:, lanes]], axis=0)
        else:
            q = (queries if rows == mine else beside)[r][:, lanes]
        scores = [
            lax.dot_general(
                q, head_of(h, 0, slot)[...], (((1,), (1,)), ((), ())), preferred_element_type=F32
            )
            for slot in slots
        ]
        top = functools.reduce(jnp.maximum, scores)
        top = jnp.max(top, axis=1, keepdims=True)
        top = jnp.broadcast_to(top, (q.shape[0], HD))
        if not first:
            old = peak[h, rows]
            top = jnp.maximum(old, top)
        peak[h, rows] = top
        wide = jnp.concatenate([top, top], axis=1)
        part = None
        mixed = None
        for slot, score in zip(slots, scores):
            weights = jnp.exp2((score - wide) * EXP2_SCALE)
            halves = weights[:, :HD] + weights[:, HD:]
            part = halves if part is None else part + halves
            term = jnp.dot(
                weights.astype(BF16), head_of(h, 1, slot)[...], preferred_element_type=F32
            )
            mixed = term if mixed is None else mixed + term
        if first:
            total[h, rows] = part
            acc[h, rows] = mixed
        else:
            fade = jnp.exp2((old - top) * EXP2_SCALE)
            total[h, rows] = total[h, rows] * fade + part
            acc[h, rows] = acc[h, rows] * fade + mixed

    pieces = [(0, 0, 0), (1, 0, 0), (0, 0, 1), (0, 1, 0), (1, 1, 0), (0, 1, 1)]
    for r, t, part in pieces:
        await_bytes(part_of(r, t, 0, part), s1_recv.at[r, t, part])
        for way in range(2):
            hop(r, way, t, part, 1).start()
    cw_ref[:, 48:, :] = jnp.zeros((9, 80, cw_ref.shape[2]), BF16)
    for n in range(1, 4):
        for r, t, part in pieces:
            for way in range(2):
                hop(r, way, t, part, n).wait_recv()
                if n < 3:
                    hop(r, way, t, part, n + 1).start()
                elif way == t and part == PARTS[r] - 1:
                    for h in RING_HEADS[r]:
                        last_hop(t, h).start()
        if n == 2:
            for r in range(2):
                await_bytes(queries[r], s1_recv.at[r, 2, 0])
                remote(queries[r], beside[r], q_send.at[r], q_recv.at[r], sibling, g).start()
    for r in range(2):
        await_bytes(beside[r], q_recv.at[r])
    for h in range(HG):
        attend(h, (0, 1, 5), both, True)
    for n in (2, 3):
        for h in range(HG):
            attend(h, (n, 4 + n), both, False)

    lane = lax.broadcasted_iota(jnp.int32, (NBLK, HD), 1)
    stats = jnp.zeros((NBLK, HD), F32)
    for h in range(HG):
        for t in range(2):
            last_hop(t, h).wait_recv()
        attend(h, (4,), others, False)
        give[h] = acc[h, others].astype(BF16)
        sums = jnp.sum(total[h, others], axis=1, keepdims=True)
        stats = jnp.where(lane == 2 * h, peak[h, others], stats)
        stats = jnp.where(lane == 2 * h + 1, sums, stats)
    give_stats[...] = stats
    hand_over = (
        remote(give_stats, got_stats, part_send.at[0], part_recv.at[0], sibling, g),
        remote(give, got, part_send.at[1], part_recv.at[1], sibling, g),
    )
    for copy in hand_over:
        copy.start()
    for h in range(HG):
        attend(h, (4,), mine, False)
    for copy in hand_over:
        copy.wait_recv()

    def home_cols(h):
        return head_cols(z * 2 + h if h < 2 else FIRST_HEAD[1] + y)

    def back_copy(h, place):
        r = 0 if h < 2 else 1
        return remote(
            ob.at[h, block_rows(place), :],
            att.at[:, home_cols(h)],
            o_send.at[h],
            o_recv,
            swap_sec,
            swap_along(r, (along[r] + NEAREST[place]) % NZ),
        )

    for h in range(HG):
        other_peak = jnp.broadcast_to(got_stats[:, 2 * h : 2 * h + 1], (NBLK, HD))
        other_sums = jnp.broadcast_to(got_stats[:, 2 * h + 1 : 2 * h + 2], (NBLK, HD))
        own_peak = peak[h, mine]
        top = jnp.maximum(own_peak, other_peak)
        own_fade = jnp.exp2((own_peak - top) * EXP2_SCALE)
        other_fade = jnp.exp2((other_peak - top) * EXP2_SCALE)
        sums = jnp.sum(total[h, mine], axis=1, keepdims=True)
        mixed = acc[h, mine] * own_fade + got[h].astype(F32) * other_fade
        ob[h] = (mixed / (sums * own_fade + other_sums * other_fade)).astype(BF16)
        for place in range(NZ - 1, 0, -1):
            back_copy(h, place).start()

        @pl.when(moves)
        def _(h=h):
            back_copy(h, 0).start()

        @pl.when(stays)
        def _(h=h):
            pltpu.make_async_copy(
                ob.at[h, block_rows(0), :], att.at[:, home_cols(h)], o_recv
            ).start()

    def sent_blocks(ref, sem):
        @pl.when(moves)
        def _():
            await_bytes(ref, sem)

        @pl.when(stays)
        def _():
            await_bytes(ref.at[pl.ds(0, NBLK - TOK), :], sem)

    for r in range(2):
        for t in range(3):
            sent_blocks(queries[r], s1_send.at[r, t])
        for way in range(2):
            await_bytes(bufs[r][0].at[pl.ds(0, 7)], ring_send.at[r, way])
        await_bytes(queries[r], q_send.at[r])
    for copy in hand_over:
        copy.wait_send()
    for load in loads:
        load.wait()
    await_bytes(att, o_recv)

    hidden = res_ref[...].astype(F32) + gate_ref[...] * att[...].astype(F32)
    center = hidden - jnp.mean(hidden, axis=1, keepdims=True)
    normed = center * lax.rsqrt(jnp.mean(center * center, axis=1, keepdims=True) + norm_eps)
    modulated = (normed * (1.0 + scale_ref[...]) + shift_ref[...]).astype(BF16)
    patches = (
        lax.dot_general(
            modulated, fw_ref[...], (((1,), (1,)), ((), ())), preferred_element_type=F32
        )
        + fb_ref[...]
    ) / scaling
    pat[...] = patches.astype(BF16).astype(F32)
    even = pat[pl.ds(0, F, stride=2), :]
    odd = pat[pl.ds(1, F, stride=2), :]
    side = 2 * LATC
    tile = jnp.concatenate([even[:, :side], odd[:, :side], even[:, side:], odd[:, side:]], axis=1)
    tiles[0, 0:1, :] = tile[:1]
    tiles[0, 1:2, :] = tile[:1]
    tiles[0, 2:8, :] = tile[:6]
    for part in (1, 2):
        tiles[part] = tile[4 * part - 2 : 4 * part + 6]
    tiles[3, 0:6, :] = tile[10:16]
    tiles[3, 6:8, :] = tile[14:16]

    pl.semaphore_wait(ready, 3)
    for dy, dx in AROUND:
        place = (1 - dy) * 3 + 1 - dx
        for ds in range(4):
            if (dy, dx, ds) != (0, 0, 0):
                sp = (s + ds) % 4
                remote(
                    tiles.at[sp],
                    near_tiles.at[place * 4 + s],
                    halo_send,
                    halo_recv,
                    sp,
                    tile_seq(dy, dx),
                ).start()
    near_tiles[4 * 4 + s] = tiles[s]
    for h in range(HG):
        sent_blocks(ob.at[h], o_send.at[h])
    await_bytes(near_tiles.at[pl.ds(0, 35)], halo_recv)

    def clear(at_edge, gone):
        @pl.when(at_edge)
        def _():
            for place in gone:
                near_tiles[place * 4 : place * 4 + 4] = jnp.zeros((4, 8, 128), F32)

    clear(z == 0, (0, 1, 2))
    clear(z == NZ - 1, (6, 7, 8))
    clear(col == 0, (0, 3, 6))
    clear(col == 2 * NY - 1, (2, 5, 8))

    for yy in range(4):
        vert, dr = ((0, 1), (1, 0), (1, 1), (2, 0))[yy]
        lo = dr * BC * LATC
        hi = lo + BC * LATC
        sides = [
            near_tiles[(vert * 3 + dx) * 4 : (vert * 3 + dx) * 4 + 4].reshape(32, 128)
            for dx in range(3)
        ]
        strip = jnp.concatenate(
            [
                sides[0][:, hi - LATC : hi],
                sides[1][:, lo:hi],
                sides[2][:, lo : lo + LATC],
                jnp.zeros((32, 2 * LATC), F32),
            ],
            axis=1,
        )
        for x in range(BC):
            moved = strip if x == 0 else pltpu.roll(strip, 128 - x * LATC, axis=1)
            moved = moved.reshape(4, 8, 128)
            for dt in range(3):
                piece = moved[:, dt : dt + 4, :].reshape(16, 128)
                for dy in range(3):
                    row = yy - dy
                    if 0 <= row < BR:
                        windows[dt * 3 + dy, pl.ds(row * BC + x, 16, stride=8), :] = piece
    await_bytes(cw_ref.at[:, pl.ds(0, 48), :], cw_sem)
    left_side = jnp.concatenate([windows[tap].astype(BF16) for tap in range(9)], axis=1)
    conv = jnp.dot(
        left_side, cw_ref[...].reshape(9 * 128, cw_ref.shape[2]), preferred_element_type=F32
    )
    conv = (conv + cb_ref[...]) * gg_ref[...] + gb_ref[...]
    out_ref[...] = (conv / (1.0 + jnp.exp(-conv))).astype(BF16)

    await_bytes(near_tiles.at[pl.ds(0, 35)], halo_send)


def on_device(
    queries,
    keys,
    values,
    residual,
    shift_mod,
    scale_mod,
    gate_mod,
    final_weight,
    final_bias,
    conv_weight,
    conv_bias,
    group_gain,
    group_bias,
):
    any_spec = pl.BlockSpec(memory_space=pl.ANY)
    dma = pltpu.SemaphoreType.DMA
    vae_width = conv_weight.shape[1]
    features = pl.pallas_call(
        whole_kernel,
        out_shape=jax.ShapeDtypeStruct((4 * 4 * BR * BC, vae_width), BF16),
        in_specs=[any_spec] * 13,
        out_specs=pl.BlockSpec(memory_space=pltpu.VMEM),
        scratch_shapes=[
            pltpu.VMEM((NBLK, 2 * HD), BF16),
            pltpu.VMEM((NBLK, 2 * HD), BF16),
            pltpu.VMEM((8, NBLK, 2 * HD), BF16),
            pltpu.VMEM((8, NBLK, 2 * HD), BF16),
            pltpu.VMEM((NBLK, HD), BF16),
            pltpu.VMEM((NBLK, HD), BF16),
            pltpu.VMEM((8, NBLK, HD), BF16),
            pltpu.VMEM((8, NBLK, HD), BF16),
            pltpu.VMEM((HG, NBLK, HD), BF16),
            pltpu.VMEM((TOK, H * HD), BF16),
            pltpu.VMEM((HG, 2 * NBLK, HD), F32),
            pltpu.VMEM((HG, 2 * NBLK, HD), F32),
            pltpu.VMEM((HG, 2 * NBLK, HD), F32),
            pltpu.VMEM((HG, NBLK, HD), BF16),
            pltpu.VMEM((HG, NBLK, HD), BF16),
            pltpu.VMEM((NBLK, HD), F32),
            pltpu.VMEM((NBLK, HD), F32),
            pltpu.VMEM((TOK, 4 * LATC), F32),
            pltpu.VMEM((4, 8, 128), F32),
            pltpu.VMEM((36, 8, 128), F32),
            pltpu.VMEM((9, 4 * 4 * BR * BC, 128), F32),
            pltpu.VMEM((TOK, H * HD), BF16),
            pltpu.VMEM((1, H * HD), F32),
            pltpu.VMEM((1, H * HD), F32),
            pltpu.VMEM((1, H * HD), F32),
            pltpu.VMEM((4 * LATC, H * HD), BF16),
            pltpu.VMEM((1, 4 * LATC), F32),
            pltpu.VMEM((9, 128, vae_width), BF16),
            pltpu.VMEM((1, vae_width), F32),
            pltpu.VMEM((1, vae_width), F32),
            pltpu.VMEM((1, vae_width), F32),
            dma((9,)),
            dma(()),
            dma((2, 3)),
            dma((2, 3, 2)),
            dma((2, 2)),
            dma((2, 2, 2, 2, 4)),
            dma((2, HG)),
            dma((2,)),
            dma((2,)),
            dma((HG,)),
            dma((HG,)),
            dma((HG,)),
            dma(()),
            dma(()),
            dma(()),
            pltpu.SemaphoreType.REGULAR,
        ],
        compiler_params=pltpu.CompilerParams(
            collective_id=0, has_side_effects=True, vmem_limit_bytes=60 * 1024 * 1024
        ),
        name="whole",
    )(
        queries[0],
        keys[0],
        values[0],
        residual[0],
        shift_mod,
        scale_mod,
        gate_mod,
        final_weight.T,
        final_bias[None],
        conv_weight,
        conv_bias[None],
        group_gain[None],
        group_bias[None],
    )
    return features.reshape(4, 4, 1, BR * BC, vae_width)


def solution(mesh):
    return jax.shard_map(
        on_device,
        mesh=mesh,
        in_specs=(
            P("sec", "seq", None),
            P("sec", "seq", None),
            P("sec", "seq", None),
            P("sec", "seq", None),
            P("sec", None),
            P("sec", None),
            P("sec", None),
            P(),
            P(),
            P(),
            P(),
            P(),
            P(),
        ),
        out_specs=P(None, "sec", "seq", None, None),
        check_vma=False,
    )
```

```python
import functools

import jax
import jax.numpy as jnp
from jax import lax
from jax.experimental import pallas as pl
from jax.experimental.pallas import tpu as pltpu
from jax.sharding import PartitionSpec as P

H = 24
HD = 128
LATC = 16
F = 16
BR = 2
BC = 4
NZ = 8
NY = 8
TOK = 32
HG = 3
NBLK = NZ * TOK

scaling = 0.476986
norm_eps = 1e-06
EXP2_SCALE = HD ** (-0.5) * 1.4426950408889634
F32 = jnp.float32
BF16 = jnp.bfloat16


def remote(src, dst, send_sem, recv_sem, sec, seq):
    return pltpu.make_async_remote_copy(
        src_ref=src,
        dst_ref=dst,
        send_sem=send_sem,
        recv_sem=recv_sem,
        device_id={"sec": sec, "seq": seq},
        device_id_type=pl.DeviceIdType.MESH,
    )


def signal(sem, sec, seq):
    pl.semaphore_signal(
        sem, inc=1, device_id={"sec": sec, "seq": seq}, device_id_type=pl.DeviceIdType.MESH
    )


def position():
    s = lax.axis_index("sec")
    g = lax.axis_index("seq")
    return s, g, s % 2, s // 2, g // (2 * NY), (g // 2) % NY, g % 2

NEAREST = (0, 1, 7, 2, 6, 3, 5, 4)
AROUND = [(dy, dx) for dy in (-1, 0, 1) for dx in (-1, 0, 1)]

RING_HEADS = ((0, 1), (2,))
FIRST_HEAD = (0, 2 * NZ)
PARTS = (2, 1)
WIDTH = (2 * HD, HD)


def whole_kernel(
    q_ref,
    k_ref,
    v_ref,
    res_hbm,
    shift_hbm,
    scale_hbm,
    gate_hbm,
    fw_hbm,
    fb_hbm,
    cw_hbm,
    cb_hbm,
    gg_hbm,
    gb_hbm,
    out_ref,
    q_rows,
    q_rows_beside,
    k_rows,
    v_rows,
    q_cols,
    q_cols_beside,
    k_cols,
    v_cols,
    ob,
    att,
    peak,
    total,
    acc,
    give,
    got,
    pat,
    tiles,
    near_tiles,
    windows,
    res_ref,
    shift_ref,
    scale_ref,
    gate_ref,
    fw_ref,
    fb_ref,
    cw_ref,
    cb_ref,
    gg_ref,
    gb_ref,
    load_sem,
    cw_sem,
    s1_send,
    s1_recv,
    ring_send,
    ring_recv,
    last_recv,
    q_send,
    q_recv,
    part_send,
    part_recv,
    o_send,
    o_recv,
    halo_send,
    halo_recv,
    ready,
):
    s, g, core, xl, z, y, xh = position()
    stays = core == xh
    moves = jnp.logical_not(stays)
    swap_sec = xl * 2 + xh
    sibling = xl * 2 + 1 - core
    col = y * 2 + xh

    def swap_seq(zp, yp):
        return (zp * NY + yp) * 2 + core

    def ring_seq(yp):
        return (z * NY + yp) * 2 + xh

    ways = (
        (ring_seq((y + 1) % NY), ring_seq((y + NY - 1) % NY)),
        (
            ((z + 1) % NZ * NY + y) * 2 + xh,
            ((z + NZ - 1) % NZ * NY + y) * 2 + xh,
        ),
    )
    along = (z, y)

    neighbours = [(dy, dx) for dy, dx in AROUND if (dy, dx) != (0, 0)]

    def tile_seq(dy, dx):
        return (z + NZ + dy) % NZ * (2 * NY) + (col + 2 * NY + dx) % (2 * NY)

    barrier = pltpu.get_barrier_semaphore()
    for e in NEAREST[1:]:
        signal(barrier, swap_sec, swap_seq((z + e) % NZ, y))

    @pl.when(moves)
    def _():
        signal(barrier, swap_sec, swap_seq(z, y))

    for e in NEAREST[1:]:
        signal(barrier, swap_sec, swap_seq(z, (y + e) % NY))
    for r in range(2):
        for way in range(2):
            signal(barrier, s, ways[r][way])
    for ds in range(1, 4):
        signal(barrier, (s + ds) % 4, g)
    for dy, dx in neighbours:
        signal(barrier, s, tile_seq(dy, dx))

    def group_cols(r, group):
        first = FIRST_HEAD[r] * HD + group * WIDTH[r]
        return pl.ds(pl.multiple_of(first, HD), WIDTH[r])

    def head_cols(h):
        return pl.ds(pl.multiple_of(h * HD, HD), HD)

    def swap_along(r, group):
        return swap_seq(group, y) if r == 0 else swap_seq(z, group)

    def block_rows(place):
        return pl.ds(place * TOK, TOK)

    def await_bytes(ref, sem):
        pltpu.make_async_copy(ref, ref, sem).wait()

    sources = (k_ref, v_ref, q_ref)
    queries = (q_rows, q_cols)
    beside = (q_rows_beside, q_cols_beside)
    bufs = ((k_rows, v_rows), (k_cols, v_cols))

    def landing(r, t):
        return queries[r] if t == 2 else bufs[r][t].at[0]

    def stage_sem(r, t, place):
        return s1_recv.at[r, t, 0 if t == 2 else place * PARTS[r] // NZ]

    def stage_copy(r, t, place):
        group = (along[r] + NZ - NEAREST[place]) % NZ
        return remote(
            sources[t].at[:, group_cols(r, group)],
            landing(r, t).at[block_rows(place), :],
            s1_send.at[r, t],
            stage_sem(r, t, place),
            swap_sec,
            swap_along(r, group),
        )

    def start_stage(r, t):
        @pl.when(stays)
        def _():
            pltpu.make_async_copy(
                sources[t].at[:, group_cols(r, along[r])],
                landing(r, t).at[block_rows(0), :],
                stage_sem(r, t, 0),
            ).start()

        @pl.when(moves)
        def _():
            stage_copy(r, t, 0).start()

        for place in range(1, NZ):
            stage_copy(r, t, place).start()

    pl.semaphore_wait(barrier, 3 * NZ + 6 - jnp.where(stays, 1, 0))
    for t in range(3):
        for r in range(2):
            start_stage(r, t)
    for ds in range(1, 4):
        signal(ready, (s + ds) % 4, g)

    loads = [
        pltpu.make_async_copy(src, dst, load_sem.at[i])
        for i, (src, dst) in enumerate(
            (
                (res_hbm, res_ref),
                (shift_hbm, shift_ref),
                (scale_hbm, scale_ref),
                (gate_hbm, gate_ref),
                (fw_hbm, fw_ref),
                (fb_hbm, fb_ref),
                (cb_hbm, cb_ref),
                (gg_hbm, gg_ref),
                (gb_hbm, gb_ref),
            )
        )
    ]
    for load in loads:
        load.start()
    for tap in range(9):
        pltpu.make_async_copy(
            cw_hbm.at[pl.ds(tap * 48, 48), :], cw_ref.at[tap, pl.ds(0, 48), :], cw_sem
        ).start()

    def slot_of(way, hops):
        if hops in (0, 4):
            return hops
        return hops if way == 0 else 4 + hops

    def part_of(r, t, slot, part):
        rows = NBLK // PARTS[r]
        return bufs[r][t].at[slot, pl.ds(part * rows, rows), :]

    def head_of(h, t, slot):
        if h == 2:
            return k_cols.at[slot] if t == 0 else v_cols.at[slot]
        return bufs[0][t].at[slot, :, pl.ds(h * HD, HD)]

    def hop(r, way, t, part, hops):
        return remote(
            part_of(r, t, slot_of(way, hops - 1), part),
            part_of(r, t, slot_of(way, hops), part),
            ring_send.at[r, way],
            ring_recv.at[r, way, t, part, hops],
            s,
            ways[r][way],
        )

    def last_hop(t, h):
        r = 0 if h < 2 else 1
        return remote(
            head_of(h, t, slot_of(t, 3)),
            head_of(h, t, 4),
            ring_send.at[r, t],
            last_recv.at[t, h],
            s,
            ways[r][t],
        )

    both = slice(0, 2 * NBLK)
    mine = slice(0, NBLK)
    others = slice(NBLK, 2 * NBLK)

    def attend(h, slots, rows, first):
        r, lanes = (1, slice(0, HD)) if h == 2 else (0, slice(h * HD, (h + 1) * HD))
        if rows == both:
            q = jnp.concatenate([queries[r][:, lanes], beside[r][:, lanes]], axis=0)
        else:
            q = (queries if rows == mine else beside)[r][:, lanes]
        scores = [
            lax.dot_general(
                q, head_of(h, 0, slot)[...], (((1,), (1,)), ((), ())), preferred_element_type=F32
            )
            for slot in slots
        ]
        top = functools.reduce(jnp.maximum, scores)
        top = jnp.max(top, axis=1, keepdims=True)
        top = jnp.broadcast_to(top, (q.shape[0], HD))
        if not first:
            old = peak[h, rows]
            top = jnp.maximum(old, top)
        peak[h, rows] = top
        wide = jnp.concatenate([top, top], axis=1)
        part = None
        mixed = None
        for slot, score in zip(slots, scores):
            weights = jnp.exp2((score - wide) * EXP2_SCALE)
            halves = weights[:, :HD] + weights[:, HD:]
            part = halves if part is None else part + halves
            term = jnp.dot(
                weights.astype(BF16), head_of(h, 1, slot)[...], preferred_element_type=F32
            )
            mixed = term if mixed is None else mixed + term
        if first:
            total[h, rows] = part
            acc[h, rows] = mixed
        else:
            fade = jnp.exp2((old - top) * EXP2_SCALE)
            total[h, rows] = total[h, rows] * fade + part
            acc[h, rows] = acc[h, rows] * fade + mixed

    pieces = [(0, 0, 0), (1, 0, 0), (0, 0, 1), (0, 1, 0), (1, 1, 0), (0, 1, 1)]
    for r, t, part in pieces:
        await_bytes(part_of(r, t, 0, part), s1_recv.at[r, t, part])
        for way in range(2):
            hop(r, way, t, part, 1).start()
    cw_ref[:, 48:, :] = jnp.zeros((9, 80, cw_ref.shape[2]), BF16)
    for n in range(1, 4):
        for r, t, part in pieces:
            for way in range(2):
                hop(r, way, t, part, n).wait_recv()
                if n < 3:
                    hop(r, way, t, part, n + 1).start()
                elif way == t and part == PARTS[r] - 1:
                    for h in RING_HEADS[r]:
                        last_hop(t, h).start()
        if n == 1:
            for r in range(2):
                await_bytes(queries[r], s1_recv.at[r, 2, 0])
                remote(queries[r], beside[r], q_send.at[r], q_recv.at[r], sibling, g).start()
        if n == 2:
            for r in range(2):
                await_bytes(beside[r], q_recv.at[r])
            for h in range(HG):
                attend(h, (0, 1, 5), both, True)
        if n >= 2:
            for h in range(HG):
                attend(h, (n, 4 + n), both, False)

    def part_copy(h):
        return remote(give.at[h], got.at[h], part_send.at[h], part_recv.at[h], sibling, g)

    first_lanes = lax.broadcasted_iota(jnp.int32, (NBLK, HD), 1) < HD // 2
    for h in range(HG):
        for t in range(2):
            last_hop(t, h).wait_recv()
        attend(h, (4,), others, False)
        give[h, 0] = acc[h, others]
        sums = jnp.sum(total[h, others], axis=1, keepdims=True)
        give[h, 1] = jnp.where(first_lanes, peak[h, others], sums)
        part_copy(h).start()
    for h in range(HG):
        attend(h, (4,), mine, False)

    def home_cols(h):
        return head_cols(z * 2 + h if h < 2 else FIRST_HEAD[1] + y)

    def back_copy(h, place):
        r = 0 if h < 2 else 1
        return remote(
            ob.at[h, block_rows(place), :],
            att.at[:, home_cols(h)],
            o_send.at[h],
            o_recv,
            swap_sec,
            swap_along(r, (along[r] + NEAREST[place]) % NZ),
        )

    for h in range(HG):
        part_copy(h).wait_recv()
        packed = got[h, 1]
        turned = pltpu.roll(packed, HD // 2, axis=1)
        other_peak = jnp.where(first_lanes, packed, turned)
        other_sums = jnp.where(first_lanes, turned, packed)
        own_peak = peak[h, mine]
        top = jnp.maximum(own_peak, other_peak)
        own_fade = jnp.exp2((own_peak - top) * EXP2_SCALE)
        other_fade = jnp.exp2((other_peak - top) * EXP2_SCALE)
        sums = jnp.sum(total[h, mine], axis=1, keepdims=True)
        mixed = acc[h, mine] * own_fade + got[h, 0] * other_fade
        ob[h] = (mixed / (sums * own_fade + other_sums * other_fade)).astype(BF16)
        for place in range(NZ - 1, 0, -1):
            back_copy(h, place).start()

        @pl.when(moves)
        def _(h=h):
            back_copy(h, 0).start()

        @pl.when(stays)
        def _(h=h):
            pltpu.make_async_copy(
                ob.at[h, block_rows(0), :], att.at[:, home_cols(h)], o_recv
            ).start()

    def sent_blocks(ref, sem):
        @pl.when(moves)
        def _():
            await_bytes(ref, sem)

        @pl.when(stays)
        def _():
            await_bytes(ref.at[pl.ds(0, NBLK - TOK), :], sem)

    for r in range(2):
        for t in range(3):
            sent_blocks(queries[r], s1_send.at[r, t])
        for way in range(2):
            await_bytes(bufs[r][0].at[pl.ds(0, 7)], ring_send.at[r, way])
        await_bytes(queries[r], q_send.at[r])
    for h in range(HG):
        part_copy(h).wait_send()
    for load in loads:
        load.wait()
    await_bytes(att, o_recv)

    hidden = res_ref[...].astype(F32) + gate_ref[...] * att[...].astype(F32)
    center = hidden - jnp.mean(hidden, axis=1, keepdims=True)
    normed = center * lax.rsqrt(jnp.mean(center * center, axis=1, keepdims=True) + norm_eps)
    modulated = (normed * (1.0 + scale_ref[...]) + shift_ref[...]).astype(BF16)
    patches = (
        lax.dot_general(
            modulated, fw_ref[...], (((1,), (1,)), ((), ())), preferred_element_type=F32
        )
        + fb_ref[...]
    ) / scaling
    pat[...] = patches.astype(BF16).astype(F32)
    even = pat[pl.ds(0, F, stride=2), :]
    odd = pat[pl.ds(1, F, stride=2), :]
    side = 2 * LATC
    tile = jnp.concatenate([even[:, :side], odd[:, :side], even[:, side:], odd[:, side:]], axis=1)
    tiles[0, 0:1, :] = tile[:1]
    tiles[0, 1:2, :] = tile[:1]
    tiles[0, 2:8, :] = tile[:6]
    for part in (1, 2):
        tiles[part] = tile[4 * part - 2 : 4 * part + 6]
    tiles[3, 0:6, :] = tile[10:16]
    tiles[3, 6:8, :] = tile[14:16]

    pl.semaphore_wait(ready, 3)
    for dy, dx in AROUND:
        place = (1 - dy) * 3 + 1 - dx
        for ds in range(4):
            if (dy, dx, ds) != (0, 0, 0):
                sp = (s + ds) % 4
                remote(
                    tiles.at[sp],
                    near_tiles.at[place * 4 + s],
                    halo_send,
                    halo_recv,
                    sp,
                    tile_seq(dy, dx),
                ).start()
    near_tiles[4 * 4 + s] = tiles[s]
    for h in range(HG):
        sent_blocks(ob.at[h], o_send.at[h])
    await_bytes(near_tiles.at[pl.ds(0, 35)], halo_recv)

    def clear(at_edge, gone):
        @pl.when(at_edge)
        def _():
            for place in gone:
                near_tiles[place * 4 : place * 4 + 4] = jnp.zeros((4, 8, 128), F32)

    clear(z == 0, (0, 1, 2))
    clear(z == NZ - 1, (6, 7, 8))
    clear(col == 0, (0, 3, 6))
    clear(col == 2 * NY - 1, (2, 5, 8))

    for yy in range(4):
        vert, dr = ((0, 1), (1, 0), (1, 1), (2, 0))[yy]
        lo = dr * BC * LATC
        hi = lo + BC * LATC
        sides = [
            near_tiles[(vert * 3 + dx) * 4 : (vert * 3 + dx) * 4 + 4].reshape(32, 128)
            for dx in range(3)
        ]
        strip = jnp.concatenate(
            [
                sides[0][:, hi - LATC : hi],
                sides[1][:, lo:hi],
                sides[2][:, lo : lo + LATC],
                jnp.zeros((32, 2 * LATC), F32),
            ],
            axis=1,
        )
        for x in range(BC):
            moved = strip if x == 0 else pltpu.roll(strip, 128 - x * LATC, axis=1)
            moved = moved.reshape(4, 8, 128)
            for dt in range(3):
                piece = moved[:, dt : dt + 4, :].reshape(16, 128)
                for dy in range(3):
                    row = yy - dy
                    if 0 <= row < BR:
                        windows[dt * 3 + dy, pl.ds(row * BC + x, 16, stride=8), :] = piece
    await_bytes(cw_ref.at[:, pl.ds(0, 48), :], cw_sem)
    left_side = jnp.concatenate([windows[tap].astype(BF16) for tap in range(9)], axis=1)
    conv = jnp.dot(
        left_side, cw_ref[...].reshape(9 * 128, cw_ref.shape[2]), preferred_element_type=F32
    )
    conv = (conv + cb_ref[...]) * gg_ref[...] + gb_ref[...]
    out_ref[...] = (conv / (1.0 + jnp.exp(-conv))).astype(BF16)

    await_bytes(near_tiles.at[pl.ds(0, 35)], halo_send)


def on_device(
    queries,
    keys,
    values,
    residual,
    shift_mod,
    scale_mod,
    gate_mod,
    final_weight,
    final_bias,
    conv_weight,
    conv_bias,
    group_gain,
    group_bias,
):
    any_spec = pl.BlockSpec(memory_space=pl.ANY)
    dma = pltpu.SemaphoreType.DMA
    vae_width = conv_weight.shape[1]
    features = pl.pallas_call(
        whole_kernel,
        out_shape=jax.ShapeDtypeStruct((4 * 4 * BR * BC, vae_width), BF16),
        in_specs=[any_spec] * 13,
        out_specs=pl.BlockSpec(memory_space=pltpu.VMEM),
        scratch_shapes=[
            pltpu.VMEM((NBLK, 2 * HD), BF16),
            pltpu.VMEM((NBLK, 2 * HD), BF16),
            pltpu.VMEM((8, NBLK, 2 * HD), BF16),
            pltpu.VMEM((8, NBLK, 2 * HD), BF16),
            pltpu.VMEM((NBLK, HD), BF16),
            pltpu.VMEM((NBLK, HD), BF16),
            pltpu.VMEM((8, NBLK, HD), BF16),
            pltpu.VMEM((8, NBLK, HD), BF16),
            pltpu.VMEM((HG, NBLK, HD), BF16),
            pltpu.VMEM((TOK, H * HD), BF16),
            pltpu.VMEM((HG, 2 * NBLK, HD), F32),
            pltpu.VMEM((HG, 2 * NBLK, HD), F32),
            pltpu.VMEM((HG, 2 * NBLK, HD), F32),
            pltpu.VMEM((HG, 2, NBLK, HD), F32),
            pltpu.VMEM((HG, 2, NBLK, HD), F32),
            pltpu.VMEM((TOK, 4 * LATC), F32),
            pltpu.VMEM((4, 8, 128), F32),
            pltpu.VMEM((36, 8, 128), F32),
            pltpu.VMEM((9, 4 * 4 * BR * BC, 128), F32),
            pltpu.VMEM((TOK, H * HD), BF16),
            pltpu.VMEM((1, H * HD), F32),
            pltpu.VMEM((1, H * HD), F32),
            pltpu.VMEM((1, H * HD), F32),
            pltpu.VMEM((4 * LATC, H * HD), BF16),
            pltpu.VMEM((1, 4 * LATC), F32),
            pltpu.VMEM((9, 128, vae_width), BF16),
            pltpu.VMEM((1, vae_width), F32),
            pltpu.VMEM((1, vae_width), F32),
            pltpu.VMEM((1, vae_width), F32),
            dma((9,)),
            dma(()),
            dma((2, 3)),
            dma((2, 3, 2)),
            dma((2, 2)),
            dma((2, 2, 2, 2, 4)),
            dma((2, HG)),
            dma((2,)),
            dma((2,)),
            dma((HG,)),
            dma((HG,)),
            dma((HG,)),
            dma(()),
            dma(()),
            dma(()),
            pltpu.SemaphoreType.REGULAR,
        ],
        compiler_params=pltpu.CompilerParams(
            collective_id=0, has_side_effects=True, vmem_limit_bytes=54976 * 1024
        ),
        name="whole",
    )(
        queries[0],
        keys[0],
        values[0],
        residual[0],
        shift_mod,
        scale_mod,
        gate_mod,
        final_weight.T,
        final_bias[None],
        conv_weight,
        conv_bias[None],
        group_gain[None],
        group_bias[None],
    )
    return features.reshape(4, 4, 1, BR * BC, vae_width)


def solution(mesh):
    return jax.shard_map(
        on_device,
        mesh=mesh,
        in_specs=(
            P("sec", "seq", None),
            P("sec", "seq", None),
            P("sec", "seq", None),
            P("sec", "seq", None),
            P("sec", None),
            P("sec", None),
            P("sec", None),
            P(),
            P(),
            P(),
            P(),
            P(),
            P(),
        ),
        out_specs=P(None, "sec", "seq", None, None),
        check_vma=False,
    )
```
